32 devices in a mesh: frame: 4 (over x, core), tile: 8 (over z, y).
Axes of the slice: x: 2, y: 2, z: 4, core: 2. Of those that a mesh axis runs over, the one named last changes fastest.
Arguments:
- state_tokens: bfloat16 [16, 8192, 256], P('frame', 'tile'), may hold values from -12 to 12
- gain_time: float32 [256], replicated, may hold values from 0.25 to 1.75
- query_time: bfloat16 [256, 256], replicated, may hold values from -2 to 2
- key_time: bfloat16 [256, 256], replicated, may hold values from -2 to 2
- value_time: bfloat16 [256, 256], replicated, may hold values from -0.375 to 0.375
- output_time: bfloat16 [256, 256], replicated, may hold values from -0.375 to 0.375
- gain_space: float32 [256], replicated, may hold values from 0.25 to 1.75
- query_space: bfloat16 [256, 256], replicated, may hold values from -2 to 2
- key_space: bfloat16 [256, 256], replicated, may hold values from -2 to 2
- value_space: bfloat16 [256, 256], replicated, may hold values from -0.375 to 0.375
- output_space: bfloat16 [256, 256], replicated, may hold values from -0.375 to 0.375
- neighbours: int32 [64, 9], P('tile'), may hold values from -1 to 63, as said below
Outputs:
- updated: bfloat16 [16, 8192, 256], P('frame', 'tile')
The draws below stay inside these ranges and needn't reach their ends.
Inputs may be any that keep to these rules, and one draw needn't show every extreme that they name: `neighbours`: entry 0 of row b is b itself; the other entries are distinct block ids at most 8 blocks away from b in the cyclic order of the 64 blocks, or -1; only the last entry is ever -1.
All inputs are finite; a program needn't handle non-finite values.
Results may differ from the reference program's by a relative error of at most 0.013.
Values may be sent and summed in bfloat16 or wider, within the bound.
No kernel may reach another device: no remote copies, remote signals or barrier semaphores. Data moves between devices by JAX's collectives and lax.ppermute only.
A program may use at most 128 MiB of HBM per device.

```python
import math
import jax
import jax.numpy as jnp
from jax import lax

WIDTH = 256
HEADS = 8
FRAMES = 16
BLOCK = 128
NEIGHBOUR_COUNT = 9
TOK_DEV = 1024
TOKENS = 8192
BLOCKS_DEV = 8
BLOCKS = 64


def draw_state_tokens(key, part):
    second = jax.random.fold_in(key, 102)
    values = jax.random.normal(second, (FRAMES, TOKENS, WIDTH), jnp.float32)
    return jnp.clip(values, -12.0, 12.0).astype(jnp.bfloat16)


def query_key_pair(key, tag):
    query_matrix = jax.random.normal(jax.random.fold_in(key, 200 + tag), (WIDTH, WIDTH), jnp.float32) / math.sqrt(WIDTH)
    key_matrix = jax.random.normal(jax.random.fold_in(key, 210 + tag), (WIDTH, WIDTH), jnp.float32) / math.sqrt(WIDTH)
    return (jnp.clip(query_matrix, -2.0, 2.0), jnp.clip(key_matrix, -2.0, 2.0))


def draw_query_time(key, part):
    return query_key_pair(key, 0)[0].astype(jnp.bfloat16)


def draw_key_time(key, part):
    return query_key_pair(key, 0)[1].astype(jnp.bfloat16)


def draw_query_space(key, part):
    return query_key_pair(key, 1)[0].astype(jnp.bfloat16)


def draw_key_space(key, part):
    return query_key_pair(key, 1)[1].astype(jnp.bfloat16)


def draw_neighbours(key, part):
    count = 2 * BLOCKS_DEV
    offsets = jnp.concatenate([jnp.arange(-BLOCKS_DEV, 0, dtype=jnp.int32), jnp.arange(1, BLOCKS_DEV + 1, dtype=jnp.int32)])
    scores = jax.random.randint(jax.random.fold_in(key, 301), (BLOCKS, count), 0, 1 << 20) * count + jnp.arange(count, dtype=jnp.int32)[None, :]
    chosen_values, picked = lax.top_k(scores, NEIGHBOUR_COUNT - 1)
    chosen = offsets[picked]
    block_ids = jnp.arange(BLOCKS, dtype=jnp.int32)[:, None] + jnp.concatenate([jnp.zeros((BLOCKS, 1), jnp.int32), chosen], axis=1)
    block_ids = block_ids % BLOCKS
    corner = jax.random.randint(jax.random.fold_in(key, 302), (BLOCKS,), 0, 6) == 0
    block_ids = block_ids.at[:, NEIGHBOUR_COUNT - 1].set(jnp.where(corner, -1, block_ids[:, NEIGHBOUR_COUNT - 1]))
    return block_ids.astype(jnp.int32)


def bell_draw(rng, dims, scale, bound, held_as=jnp.bfloat16):
    entries = scale * jax.random.normal(rng, dims, jnp.float32)
    return jnp.clip(entries, min=-bound, max=bound).astype(held_as)


def setup_inputs(seed: int = 0) -> dict:
    key_list = jax.random.split(jax.random.key(seed), 13)
    return {
        "state_tokens": draw_state_tokens(jax.random.fold_in(key_list[12], 71), 0),
        "gain_time": jnp.clip(1.0 + 0.15 * jax.random.normal(key_list[1], (WIDTH,), jnp.float32), 0.25, 1.75),
        "query_time": draw_query_time(jax.random.fold_in(key_list[12], 71), 0),
        "key_time": draw_key_time(jax.random.fold_in(key_list[12], 71), 0),
        "value_time": bell_draw(key_list[4], (WIDTH, WIDTH), WIDTH ** -0.5, 0.375),
        "output_time": bell_draw(key_list[5], (WIDTH, WIDTH), WIDTH ** -0.5, 0.375),
        "gain_space": jnp.clip(1.0 + 0.15 * jax.random.normal(key_list[6], (WIDTH,), jnp.float32), 0.25, 1.75),
        "query_space": draw_query_space(jax.random.fold_in(key_list[12], 71), 0),
        "key_space": draw_key_space(jax.random.fold_in(key_list[12], 71), 0),
        "value_space": bell_draw(key_list[9], (WIDTH, WIDTH), WIDTH ** -0.5, 0.375),
        "output_space": bell_draw(key_list[10], (WIDTH, WIDTH), WIDTH ** -0.5, 0.375),
        "neighbours": draw_neighbours(jax.random.fold_in(key_list[12], 71), 0),
    }


EPS = 1e-05
ROT_PERIOD = 1024

def rms_scale(rows, gain):
    values = rows.astype(jnp.float32)
    square_mean = lax.optimization_barrier(jnp.mean(values * values, axis=-1, keepdims=True))
    return (values * lax.rsqrt(square_mean + EPS) * gain).astype(jnp.bfloat16)

def project_rows(rows, weight):
    flat = rows.reshape(-1, rows.shape[-1])
    result = jnp.dot(flat, weight, preferred_element_type=jnp.float32)
    return result.reshape(rows.shape[:-1] + (weight.shape[1],))

def rotate_pairs(values, positions, heads):
    features = values.shape[-1]
    head_dim = features // heads
    half = head_dim // 2
    freqs = jnp.power(10000.0, -jnp.arange(half, dtype=jnp.float32) / half)
    angle = (positions % ROT_PERIOD).astype(jnp.float32)[:, None] * freqs[None, :]
    cosine = jnp.cos(angle)[:, None, :]
    sine = jnp.sin(angle)[:, None, :]
    shaped = values.reshape(values.shape[:-1] + (heads, head_dim))
    first = shaped[..., :half]
    second = shaped[..., half:]
    turned = jnp.concatenate([first * cosine - second * sine, first * sine + second * cosine], axis=-1)
    return turned.reshape(values.shape)

def temporal_attend(normed, query_time, key_time, value_time):
    frames, count, features = normed.shape
    head_dim = features // HEADS
    t_query = project_rows(normed, query_time).astype(jnp.bfloat16).reshape(frames, count, HEADS, head_dim)
    t_key = project_rows(normed, key_time).astype(jnp.bfloat16).reshape(frames, count, HEADS, head_dim)
    t_value = project_rows(normed, value_time).astype(jnp.bfloat16).reshape(frames, count, HEADS, head_dim)
    scores = jnp.einsum('fghd,eghd->ghfe', t_query.astype(jnp.float32), t_key.astype(jnp.float32)) / jnp.sqrt(jnp.float32(head_dim))
    weights = jax.nn.softmax(scores, axis=-1).astype(jnp.bfloat16)
    result = jnp.einsum('ghfe,eghd->fghd', weights.astype(jnp.float32), t_value.astype(jnp.float32))
    return result.astype(jnp.bfloat16).reshape(frames, count, features)

def reference(state_tokens, gain_time, query_time, key_time, value_time, output_time, gain_space, query_space, key_space, value_space, output_space, neighbours):
    head_dim = WIDTH // HEADS
    groups = TOKENS // TOK_DEV

    def temporal_group(group_index):
        shard_rows = lax.dynamic_slice_in_dim(state_tokens, group_index * TOK_DEV, TOK_DEV, 1)
        normed = rms_scale(shard_rows, gain_time)
        attended = temporal_attend(normed, query_time, key_time, value_time)
        return (shard_rows.astype(jnp.float32) + project_rows(attended, output_time)).astype(jnp.bfloat16)
    middle = lax.map(temporal_group, jnp.arange(groups, dtype=jnp.int32))
    middle = jnp.moveaxis(middle, 0, 1).reshape(FRAMES, TOKENS, WIDTH)
    normed_space = rms_scale(middle, gain_space)
    positions = jnp.arange(TOKENS, dtype=jnp.int32)
    space_query = rotate_pairs(project_rows(normed_space, query_space), positions, HEADS).astype(jnp.bfloat16)
    space_key = rotate_pairs(project_rows(normed_space, key_space), positions, HEADS).astype(jnp.bfloat16)
    space_value = project_rows(normed_space, value_space).astype(jnp.bfloat16)
    query_blocks = space_query.reshape(FRAMES, BLOCKS, BLOCK, WIDTH)
    key_blocks = space_key.reshape(FRAMES, BLOCKS, BLOCK, WIDTH)
    value_blocks = space_value.reshape(FRAMES, BLOCKS, BLOCK, WIDTH)

    def spatial_block(block_index):
        block_ids = neighbours[block_index]
        valid_slot = block_ids >= 0
        safe_ids = jnp.where(valid_slot, block_ids, 0)
        gathered_keys = key_blocks[:, safe_ids].reshape(FRAMES, NEIGHBOUR_COUNT * BLOCK, HEADS, head_dim)
        gathered_values = value_blocks[:, safe_ids].reshape(FRAMES, NEIGHBOUR_COUNT * BLOCK, HEADS, head_dim)
        key_mask = jnp.repeat(valid_slot, BLOCK)
        query = query_blocks[:, block_index].reshape(FRAMES, BLOCK, HEADS, head_dim)
        scores = jnp.einsum('frhd,fkhd->fhrk', query.astype(jnp.float32), gathered_keys.astype(jnp.float32)) / jnp.sqrt(jnp.float32(head_dim))
        scores = jnp.where(key_mask[None, None, None, :], scores, -1e+30)
        weights = jax.nn.softmax(scores, axis=-1).astype(jnp.bfloat16)
        result = jnp.einsum('fhrk,fkhd->frhd', weights.astype(jnp.float32), gathered_values.astype(jnp.float32))
        return result.astype(jnp.bfloat16).reshape(FRAMES, BLOCK, WIDTH)
    attended = lax.map(spatial_block, jnp.arange(BLOCKS, dtype=jnp.int32))
    attended = jnp.moveaxis(attended, 0, 1).reshape(FRAMES, TOKENS, WIDTH)
    return (middle.astype(jnp.float32) + project_rows(attended, output_space)).astype(jnp.bfloat16)
```

```python
import functools

import jax
import jax.numpy as jnp
import numpy as np
from jax import lax
from jax.experimental import pallas as pl
from jax.experimental.pallas import tpu as pltpu
from jax.sharding import PartitionSpec as P

HEADS = 8
BLOCK = 128
NEIGHBOUR_COUNT = 9
EPS = 1e-05
ROT_PERIOD = 1024
LOG2E = 1.4426950408889634
SAFE_SCORE = 64.0
FRAME_CHUNKS = 4
BF16 = jnp.bfloat16
F32 = jnp.float32


def rms_rows(x, gain):
    square_mean = jnp.mean(x * x, axis=-1, keepdims=True)
    return (x * lax.rsqrt(square_mean + EPS) * gain).astype(BF16)


def mm(a, b):
    return jnp.dot(a, b, preferred_element_type=F32)


def mm_t(a, b):
    return lax.dot_general(a, b, (((1,), (1,)), ((), ())), preferred_element_type=F32)


def iota(shape, dim):
    return lax.broadcasted_iota(jnp.int32, shape, dim)


def time_kernel(scale, pieces, chunks, gain_ref, wq_ref, wk_ref, wv_ref, wo_ref, *refs):
    x_refs = refs[:pieces]
    o_refs = refs[pieces : pieces + pieces * chunks]
    q_s, k_s, v_s, a_s = refs[pieces + pieces * chunks :]
    tokens, width = x_refs[0].shape[1:]
    head_dim = width // HEADS
    frames = q_s.shape[0]
    x = jnp.concatenate([r[...].astype(F32) for r in x_refs], axis=0)
    normed = rms_rows(x, gain_ref[...]).reshape(frames * tokens, width)
    q_s[...] = (mm(normed, wq_ref[...]) * scale).reshape(frames, tokens, width)
    k_s[...] = mm(normed, wk_ref[...]).reshape(frames, tokens, width)
    v_s[...] = mm(normed, wv_ref[...]).reshape(frames, tokens, width)
    rows = frames * 8
    head_of = iota((1, width), 1) // head_dim
    same = (iota((rows, rows), 0) % 8) == (iota((rows, rows), 1) % 8)
    for g in range(tokens // 8):
        part = slice(g * 8, g * 8 + 8)
        q = q_s[:, part, :].reshape(rows, width)
        k = k_s[:, part, :].reshape(rows, width).astype(BF16)
        v = v_s[:, part, :].reshape(rows, width).astype(BF16)
        acc = None
        for h in range(HEADS):
            qm = jnp.where(head_of == h, q, 0.0).astype(BF16)
            s = jnp.where(same, mm_t(qm, k), -1e30)
            p = jnp.exp2(s - jnp.max(s, axis=1, keepdims=True))
            d = jnp.sum(p, axis=1, keepdims=True)
            o = mm(p.astype(BF16), v) / d
            acc = o if acc is None else jnp.where(head_of == h, o, acc)
        a_s[:, part, :] = acc.reshape(frames, 8, width)
    attended = a_s[...].reshape(frames * tokens, width).astype(BF16)
    middle = x + mm(attended, wo_ref[...]).reshape(frames, tokens, width)
    frames_here = x_refs[0].shape[0]
    step = frames_here // chunks
    for i in range(pieces):
        for j in range(chunks):
            low = i * frames_here + j * step
            o_refs[i * chunks + j][...] = middle[low : low + step].astype(BF16)


def time_stage(pieces, chunks, gain, wq, wk, wv, wo):
    frames_here, tokens, width = pieces[0].shape
    frames = frames_here * len(pieces)
    tile = min(tokens, 32)
    scale = LOG2E / float(np.sqrt(width // HEADS))
    full = pl.BlockSpec((width, width), lambda t: (0, 0))
    step = frames_here // chunks
    count = len(pieces) * chunks
    return pl.pallas_call(
        functools.partial(time_kernel, scale, len(pieces), chunks),
        grid=(tokens // tile,),
        in_specs=[pl.BlockSpec((1, width), lambda t: (0, 0))]
        + [full] * 4
        + [pl.BlockSpec((frames_here, tile, width), lambda t: (0, t, 0))] * len(pieces),
        out_specs=[pl.BlockSpec((step, tile, width), lambda t: (0, t, 0))] * count,
        out_shape=[jax.ShapeDtypeStruct((step, tokens, width), BF16)] * count,
        scratch_shapes=[pltpu.VMEM((frames, tile, width), F32)] * 4,
        compiler_params=pltpu.CompilerParams(vmem_limit_bytes=48 << 20),
        name="time_attention",
    )(gain, wq, wk, wv, wo, *pieces)


def space_kernel(scale, pieces, has_prev, ids, pos, gain_ref, wq_ref, wk_ref, wv_ref, wo_ref, cos_ref, sin_ref, *refs):
    x_refs = refs[: 3 * pieces]
    refs = refs[3 * pieces + (1 if has_prev else 0) :]
    o_ref, wq_s, wk_s, q_s, k_s, v_s, x_s, kg, vg, flag = refs
    frame, block = pl.program_id(0), pl.program_id(1)
    piece_rows, width = x_refs[0].shape[1:]
    half = width // 2
    head_dim = width // HEADS
    quarter = head_dim // 2

    @pl.when((frame == 0) & (block == 0))
    def _():
        src = iota((width, width), 0)
        dst = iota((width, width), 1)
        low = dst % half
        wanted = (low // quarter) * head_dim + low % quarter + jnp.where(dst >= half, quarter, 0)
        order = jnp.where(src == wanted, 1.0, 0.0).astype(BF16)
        wq_s[...] = mm(wq_ref[...], order).astype(BF16)
        wk_s[...] = mm(wk_ref[...], order).astype(BF16)

    @pl.when(block == 0)
    def _():
        same_head = jnp.where(
            iota((half, half), 0) // quarter == iota((half, half), 1) // quarter, 1.0, 0.0
        ).astype(BF16)

        def turn(rows, c, s):
            u, w = rows[:, :half], rows[:, half:]
            return u * c - w * s, u * s + w * c

        def head_squares(u, w):
            squares = mm((u * u + w * w).astype(BF16), same_head)
            return jnp.max(squares, axis=0, keepdims=True)

        k_top, q_top = None, None
        for side in range(3):
            for i in range(pieces):
                x_raw = x_refs[side * pieces + i][0]
                normed = rms_rows(x_raw.astype(F32), gain_ref[...])
                at = pl.ds(pl.multiple_of(pos[i], piece_rows), piece_rows)
                c, s = cos_ref[at, :], sin_ref[at, :]
                low = (side * pieces + i) * piece_rows
                rows = slice(low, low + piece_rows)
                u, w = turn(mm(normed, wk_s[...]), c, s)
                k_s[rows, :half] = u.astype(BF16)
                k_s[rows, half:] = w.astype(BF16)
                top = head_squares(u, w)
                k_top = top if k_top is None else jnp.maximum(k_top, top)
                v_s[rows, :] = mm(normed, wv_ref[...]).astype(BF16)
                if side == 0:
                    u, w = turn(mm(normed, wq_s[...]) * scale, c, s)
                    q_s[rows, :half] = u.astype(BF16)
                    q_s[rows, half:] = w.astype(BF16)
                    top = head_squares(u, w)
                    q_top = top if q_top is None else jnp.maximum(q_top, top)
                    x_s[rows, :] = x_raw
        flag[0] = jnp.max(k_top * q_top)

    for m in range(NEIGHBOUR_COUNT):
        at = pl.ds(pl.multiple_of(ids[block * (NEIGHBOUR_COUNT + 2) + m] * BLOCK, BLOCK), BLOCK)
        kg[m * BLOCK : (m + 1) * BLOCK, :] = k_s[at, :]
        vg[m * BLOCK : (m + 1) * BLOCK, :] = v_s[at, :]
    last = (NEIGHBOUR_COUNT - 1) * BLOCK
    present = ids[block * (NEIGHBOUR_COUNT + 2) + NEIGHBOUR_COUNT] > 0
    own = pl.ds(pl.multiple_of(ids[block * (NEIGHBOUR_COUNT + 2) + NEIGHBOUR_COUNT + 1] * BLOCK, BLOCK), BLOCK)
    lane = iota((1, width), 1)
    rot_head = (lane % half) // quarter
    head_of = lane // head_dim
    bias = jnp.where(present | (iota((1, NEIGHBOUR_COUNT * BLOCK), 1) < last), 0.0, -1e30)

    def attend(group, shift):
        q = q_s[own, :]
        acc = None
        for g in range(HEADS // group):
            heads = range(g * group, g * group + group)
            qm = jnp.concatenate([jnp.where(rot_head == h, q, 0).astype(BF16) for h in heads], axis=0)
            s = mm_t(qm, kg[...]) + bias
            if shift:
                s = s - jnp.max(s, axis=1, keepdims=True)
            p = jnp.exp2(s)
            d = jnp.sum(p, axis=1, keepdims=True)
            o = mm(p.astype(BF16), vg[...]) / d
            for j, h in enumerate(heads):
                part = o[j * BLOCK : (j + 1) * BLOCK]
                acc = part if acc is None else jnp.where(head_of == h, part, acc)
        y = mm(acc.astype(BF16), wo_ref[...])
        o_ref[0] = (x_s[own, :].astype(F32) + y).astype(BF16)

    safe = flag[0] <= SAFE_SCORE * SAFE_SCORE

    @pl.when(safe)
    def _():
        attend(4, False)

    @pl.when(jnp.logical_not(safe))
    def _():
        attend(2, True)


def space_stage(sides, ids, pos, gain, wq, wk, wv, wo, cos, sin, prev, chunk, chunks):
    pieces = len(sides[0])
    step, piece_rows, width = sides[0][0].shape
    tokens = pieces * piece_rows
    blocks = tokens // BLOCK
    scale = LOG2E / float(np.sqrt(width // HEADS))
    full = pl.BlockSpec((width, width), lambda f, b, *_: (0, 0))
    table = pl.BlockSpec(cos.shape, lambda f, b, *_: (0, 0))
    piece = pl.BlockSpec((1, piece_rows, width), lambda f, b, *_: (f, 0, 0))
    in_specs = [pl.BlockSpec((1, width), lambda f, b, *_: (0, 0))] + [full] * 4 + [table] * 2
    in_specs += [piece] * (3 * pieces)
    args = [gain, wq, wk, wv, wo, cos, sin] + [p for side in sides for p in side]
    aliases = {}
    if prev is not None:
        in_specs.append(pl.BlockSpec(memory_space=pl.ANY))
        aliases = {2 + len(args): 0}
        args.append(prev)
    wide = NEIGHBOUR_COUNT * BLOCK
    spec = pltpu.PrefetchScalarGridSpec(
        num_scalar_prefetch=2,
        grid=(step, blocks),
        in_specs=in_specs,
        out_specs=pl.BlockSpec((1, BLOCK, width), lambda f, b, *_: (f + chunk * step, b, 0)),
        scratch_shapes=[
            pltpu.VMEM((width, width), BF16),
            pltpu.VMEM((width, width), BF16),
            pltpu.VMEM((tokens, width), BF16),
            pltpu.VMEM((3 * tokens, width), BF16),
            pltpu.VMEM((3 * tokens, width), BF16),
            pltpu.VMEM((tokens, width), BF16),
            pltpu.VMEM((wide, width), BF16),
            pltpu.VMEM((wide, width), BF16),
            pltpu.SMEM((1,), F32),
        ],
    )
    return pl.pallas_call(
        functools.partial(space_kernel, scale, pieces, prev is not None),
        grid_spec=spec,
        out_shape=jax.ShapeDtypeStruct((step * chunks, tokens, width), BF16),
        input_output_aliases=aliases,
        compiler_params=pltpu.CompilerParams(vmem_limit_bytes=56 << 20),
        name="space_attention",
    )(ids, pos, *args)


def rotary_tables(tokens, width):
    half = width // HEADS // 2
    freqs = np.power(10000.0, -np.arange(half, dtype=np.float64) / half)
    angle = (np.arange(tokens) % ROT_PERIOD)[:, None] * freqs[None, :]
    cos = np.tile(np.cos(angle).astype(np.float32), (1, HEADS))
    sin = np.tile(np.sin(angle).astype(np.float32), (1, HEADS))
    return jnp.asarray(cos), jnp.asarray(sin)


def body(
    state_tokens,
    gain_time,
    query_time,
    key_time,
    value_time,
    output_time,
    gain_space,
    query_space,
    key_space,
    value_space,
    output_space,
    neighbours,
):
    frames_here, tokens_here, width = state_tokens.shape
    frame_count = lax.axis_size("frame")
    tile_count = lax.axis_size("tile")
    me = lax.axis_index("frame")
    tile = lax.axis_index("tile")
    chunks = FRAME_CHUNKS if frames_here % FRAME_CHUNKS == 0 else 1
    rows = tokens_here // frame_count

    def swap(value, k):
        return lax.ppermute(value, "frame", [(i, i ^ k) for i in range(frame_count)])

    pieces = []
    for k in range(frame_count):
        part = lax.dynamic_slice_in_dim(state_tokens, (me ^ k) * rows, rows, axis=1)
        pieces.append(part if k == 0 else swap(part, k))
    outs = time_stage(
        pieces, chunks, gain_time.reshape(1, width), query_time, key_time, value_time, output_time
    )

    pairs = [(i, i ^ 1) for i in range(tile_count)]
    onward = [(i, (i + 2) % tile_count if i % 2 == 0 else (i - 2) % tile_count) for i in range(tile_count)]
    split = rows % BLOCK == 0
    places = me ^ jnp.arange(frame_count, dtype=jnp.int32)
    sides = []
    for j in range(chunks):
        own = [outs[k * chunks + j] for k in range(frame_count)]
        own = [p if k == 0 else swap(p, k) for k, p in enumerate(own)]
        if not split:
            stacked = jnp.stack(own, axis=1)[:, places]
            own = [stacked.reshape(-1, tokens_here, width)]
        near = [lax.ppermute(p, "tile", pairs) for p in own]
        far = [lax.ppermute(p, "tile", onward) for p in near]
        sides.append((own, near, far))

    blocks = tokens_here // BLOCK
    total = blocks * tile_count
    even = tile % 2 == 0
    offset = (neighbours - (tile - 1) * blocks) % total
    side_of = offset // blocks
    side_at = jnp.where(side_of == 1, 0, jnp.where((side_of == 2) == even, 1, 2))
    inner = offset % blocks
    own_inner = jnp.arange(blocks, dtype=jnp.int32)
    if split:
        per = rows // BLOCK
        inner = ((inner // per) ^ me) * per + inner % per
        own_inner = ((own_inner // per) ^ me) * per + own_inner % per
        pos = (places * rows).astype(jnp.int32)
    else:
        pos = jnp.zeros((1,), jnp.int32)
    present = neighbours >= 0
    ids = jnp.where(present, side_at * blocks + inner, own_inner[:, None])
    ids = jnp.concatenate(
        [ids, present[:, -1:].astype(jnp.int32), own_inner[:, None]], axis=1
    ).reshape(-1)
    cos, sin = rotary_tables(tokens_here, width)
    result = None
    for j in range(chunks):
        result = space_stage(
            sides[j], ids, pos, gain_space.reshape(1, width), query_space, key_space, value_space,
            output_space, cos, sin, result, j, chunks,
        )
    return result


def solution(mesh):
    rows = P("frame", "tile", None)
    return jax.shard_map(
        body,
        mesh=mesh,
        in_specs=(rows,) + (P(),) * 10 + (P("tile", None),),
        out_specs=rows,
        check_vma=False,
    )
```

```python
import functools

import jax
import jax.numpy as jnp
import numpy as np
from jax import lax
from jax.experimental import pallas as pl
from jax.experimental.pallas import tpu as pltpu
from jax.sharding import PartitionSpec as P

HEADS = 8
BLOCK = 128
NEIGHBOUR_COUNT = 9
EPS = 1e-05
ROT_PERIOD = 1024
LOG2E = 1.4426950408889634
SAFE_SCORE = 64.0
FRAME_CHUNKS = 4
BF16 = jnp.bfloat16
F32 = jnp.float32


def rms_rows(x, gain):
    square_mean = jnp.mean(x * x, axis=-1, keepdims=True)
    return (x * lax.rsqrt(square_mean + EPS) * gain).astype(BF16)


def mm(a, b):
    return jnp.dot(a, b, preferred_element_type=F32)


def mm_t(a, b):
    return lax.dot_general(a, b, (((1,), (1,)), ((), ())), preferred_element_type=F32)


def iota(shape, dim):
    return lax.broadcasted_iota(jnp.int32, shape, dim)


def cost(us):
    return pl.CostEstimate(flops=int(us * 900e6), transcendentals=0, bytes_accessed=int(us * 1e6))


def time_kernel(scale, pieces, chunks, gain_ref, wq_ref, wk_ref, wv_ref, wo_ref, *refs):
    x_refs = refs[:pieces]
    o_refs = refs[pieces : pieces + pieces * chunks]
    q_s, k_s, v_s, a_s = refs[pieces + pieces * chunks :]
    tokens, width = x_refs[0].shape[1:]
    head_dim = width // HEADS
    frames = q_s.shape[0]
    x = jnp.concatenate([r[...].astype(F32) for r in x_refs], axis=0)
    normed = rms_rows(x, gain_ref[...]).reshape(frames * tokens, width)
    q_s[...] = (mm(normed, wq_ref[...]) * scale).reshape(frames, tokens, width)
    k_s[...] = mm(normed, wk_ref[...]).reshape(frames, tokens, width)
    v_s[...] = mm(normed, wv_ref[...]).reshape(frames, tokens, width)
    rows = frames * 8
    head_of = iota((1, width), 1) // head_dim
    same = (iota((rows, rows), 0) % 8) == (iota((rows, rows), 1) % 8)
    for g in range(tokens // 8):
        part = slice(g * 8, g * 8 + 8)
        q = q_s[:, part, :].reshape(rows, width)
        k = k_s[:, part, :].reshape(rows, width).astype(BF16)
        v = v_s[:, part, :].reshape(rows, width).astype(BF16)
        acc = None
        for h in range(HEADS):
            qm = jnp.where(head_of == h, q, 0.0).astype(BF16)
            s = jnp.where(same, mm_t(qm, k), -1e30)
            p = jnp.exp2(s - jnp.max(s, axis=1, keepdims=True))
            d = jnp.sum(p, axis=1, keepdims=True)
            o = mm(p.astype(BF16), v) / d
            acc = o if acc is None else jnp.where(head_of == h, o, acc)
        a_s[:, part, :] = acc.reshape(frames, 8, width)
    attended = a_s[...].reshape(frames * tokens, width).astype(BF16)
    middle = x + mm(attended, wo_ref[...]).reshape(frames, tokens, width)
    frames_here = x_refs[0].shape[0]
    step = frames_here // chunks
    for i in range(pieces):
        for j in range(chunks):
            low = i * frames_here + j * step
            o_refs[i * chunks + j][...] = middle[low : low + step].astype(BF16)


def time_stage(pieces, chunks, gain, wq, wk, wv, wo):
    frames_here, tokens, width = pieces[0].shape
    frames = frames_here * len(pieces)
    tile = min(tokens, 32)
    scale = LOG2E / float(np.sqrt(width // HEADS))
    full = pl.BlockSpec((width, width), lambda t: (0, 0))
    step = frames_here // chunks
    count = len(pieces) * chunks
    return pl.pallas_call(
        functools.partial(time_kernel, scale, len(pieces), chunks),
        grid=(tokens // tile,),
        in_specs=[pl.BlockSpec((1, width), lambda t: (0, 0))]
        + [full] * 4
        + [pl.BlockSpec((frames_here, tile, width), lambda t: (0, t, 0))] * len(pieces),
        out_specs=[pl.BlockSpec((step, tile, width), lambda t: (0, t, 0))] * count,
        out_shape=[jax.ShapeDtypeStruct((step, tokens, width), BF16)] * count,
        scratch_shapes=[pltpu.VMEM((frames, tile, width), F32)] * 4,
        compiler_params=pltpu.CompilerParams(vmem_limit_bytes=48 << 20),
        cost_estimate=cost(18),
        name="time_attention",
    )(gain, wq, wk, wv, wo, *pieces)


def space_kernel(scale, pieces, has_prev, ids, pos, wq_ref, wk_ref, wv_ref, wo_ref, cos_ref, sin_ref, *refs):
    x_refs, n_refs = refs[:pieces], refs[pieces : pieces + 3]
    refs = refs[pieces + 3 + (1 if has_prev else 0) :]
    o_ref, wq_s, wk_s, q_s, k_s, v_s, x_s, kg, vg, flag = refs
    frame, block = pl.program_id(0), pl.program_id(1)
    piece_rows, width = x_refs[0].shape[1:]
    half = width // 2
    head_dim = width // HEADS
    quarter = head_dim // 2

    @pl.when((frame == 0) & (block == 0))
    def _():
        src = iota((width, width), 0)
        dst = iota((width, width), 1)
        low = dst % half
        wanted = (low // quarter) * head_dim + low % quarter + jnp.where(dst >= half, quarter, 0)
        order = jnp.where(src == wanted, 1.0, 0.0).astype(BF16)
        wq_s[...] = mm(wq_ref[...], order).astype(BF16)
        wk_s[...] = mm(wk_ref[...], order).astype(BF16)

    @pl.when(block == 0)
    def _():
        same_head = jnp.where(
            iota((half, half), 0) // quarter == iota((half, half), 1) // quarter, 1.0, 0.0
        ).astype(BF16)

        def turn(rows, c, s):
            u, w = rows[:, :half], rows[:, half:]
            return u * c - w * s, u * s + w * c

        def head_squares(u, w):
            squares = mm((u * u + w * w).astype(BF16), same_head)
            return jnp.max(squares, axis=0, keepdims=True)

        k_top, q_top = None, None
        for side in range(3):
            for i in range(pieces):
                low = i * piece_rows
                rows = slice(low, low + piece_rows)
                normed = n_refs[side][0, rows, :]
                at = pl.ds(pl.multiple_of(pos[i], piece_rows), piece_rows)
                c, s = cos_ref[at, :], sin_ref[at, :]
                if side == 0:
                    u, w = turn(mm(normed, wq_s[...]) * scale, c, s)
                    q_s[rows, :half] = u.astype(BF16)
                    q_s[rows, half:] = w.astype(BF16)
                    top = head_squares(u, w)
                    q_top = top if q_top is None else jnp.maximum(q_top, top)
                    x_s[rows, :] = x_refs[i][0]
                low += side * pieces * piece_rows
                rows = slice(low, low + piece_rows)
                u, w = turn(mm(normed, wk_s[...]), c, s)
                k_s[rows, :half] = u.astype(BF16)
                k_s[rows, half:] = w.astype(BF16)
                top = head_squares(u, w)
                k_top = top if k_top is None else jnp.maximum(k_top, top)
                v_s[rows, :] = mm(normed, wv_ref[...]).astype(BF16)
        flag[0] = jnp.max(k_top * q_top)

    for m in range(NEIGHBOUR_COUNT):
        at = pl.ds(pl.multiple_of(ids[block * (NEIGHBOUR_COUNT + 2) + m] * BLOCK, BLOCK), BLOCK)
        kg[m * BLOCK : (m + 1) * BLOCK, :] = k_s[at, :]
        vg[m * BLOCK : (m + 1) * BLOCK, :] = v_s[at, :]
    last = (NEIGHBOUR_COUNT - 1) * BLOCK
    present = ids[block * (NEIGHBOUR_COUNT + 2) + NEIGHBOUR_COUNT] > 0
    own = pl.ds(pl.multiple_of(ids[block * (NEIGHBOUR_COUNT + 2) + NEIGHBOUR_COUNT + 1] * BLOCK, BLOCK), BLOCK)
    lane = iota((1, width), 1)
    rot_head = (lane % half) // quarter
    head_of = lane // head_dim
    bias = jnp.where(present | (iota((1, NEIGHBOUR_COUNT * BLOCK), 1) < last), 0.0, -1e30)

    def attend(group, shift):
        q = q_s[own, :]
        acc = None
        for g in range(HEADS // group):
            heads = range(g * group, g * group + group)
            qm = jnp.concatenate([jnp.where(rot_head == h, q, 0).astype(BF16) for h in heads], axis=0)
            s = mm_t(qm, kg[...]) + bias
            if shift:
                s = s - jnp.max(s, axis=1, keepdims=True)
            p = jnp.exp2(s)
            d = jnp.sum(p, axis=1, keepdims=True)
            o = mm(p.astype(BF16), vg[...]) / d
            for j, h in enumerate(heads):
                part = o[j * BLOCK : (j + 1) * BLOCK]
                acc = part if acc is None else jnp.where(head_of == h, part, acc)
        y = mm(acc.astype(BF16), wo_ref[...])
        o_ref[0] = (x_s[own, :].astype(F32) + y).astype(BF16)

    safe = flag[0] <= SAFE_SCORE * SAFE_SCORE

    @pl.when(safe)
    def _():
        attend(4, False)

    @pl.when(jnp.logical_not(safe))
    def _():
        attend(2, True)


def norm_kernel(pieces, gain_ref, *refs):
    rows = refs[0].shape[1]
    for i in range(pieces):
        refs[pieces][:, i * rows : (i + 1) * rows, :] = rms_rows(refs[i][...].astype(F32), gain_ref[...])


def norm_stage(own, gain):
    step, rows, width = own[0].shape
    shape = (step, rows * len(own), width)
    return pl.pallas_call(
        functools.partial(norm_kernel, len(own)),
        out_shape=jax.ShapeDtypeStruct(shape, BF16),
        compiler_params=pltpu.CompilerParams(vmem_limit_bytes=48 << 20),
        cost_estimate=cost(2),
        name="norm_join",
    )(gain, *own)


def space_stage(own, normed, ids, pos, wq, wk, wv, wo, cos, sin, prev, chunk, chunks):
    pieces = len(own)
    step, piece_rows, width = own[0].shape
    tokens = pieces * piece_rows
    blocks = tokens // BLOCK
    scale = LOG2E / float(np.sqrt(width // HEADS))
    full = pl.BlockSpec((width, width), lambda f, b, *_: (0, 0))
    table = pl.BlockSpec(cos.shape, lambda f, b, *_: (0, 0))
    piece = pl.BlockSpec((1, piece_rows, width), lambda f, b, *_: (f, 0, 0))
    whole = pl.BlockSpec((1, tokens, width), lambda f, b, *_: (f, 0, 0))
    in_specs = [full] * 4 + [table] * 2 + [piece] * pieces + [whole] * 3
    args = [wq, wk, wv, wo, cos, sin, *own, *normed]
    aliases = {}
    if prev is not None:
        in_specs.append(pl.BlockSpec(memory_space=pl.ANY))
        aliases = {2 + len(args): 0}
        args.append(prev)
    wide = NEIGHBOUR_COUNT * BLOCK
    spec = pltpu.PrefetchScalarGridSpec(
        num_scalar_prefetch=2,
        grid=(step, blocks),
        in_specs=in_specs,
        out_specs=pl.BlockSpec((1, BLOCK, width), lambda f, b, *_: (f + chunk * step, b, 0)),
        scratch_shapes=[
            pltpu.VMEM((width, width), BF16),
            pltpu.VMEM((width, width), BF16),
            pltpu.VMEM((tokens, width), BF16),
            pltpu.VMEM((3 * tokens, width), BF16),
            pltpu.VMEM((3 * tokens, width), BF16),
            pltpu.VMEM((tokens, width), BF16),
            pltpu.VMEM((wide, width), BF16),
            pltpu.VMEM((wide, width), BF16),
            pltpu.SMEM((1,), F32),
        ],
    )
    return pl.pallas_call(
        functools.partial(space_kernel, scale, pieces, prev is not None),
        grid_spec=spec,
        out_shape=jax.ShapeDtypeStruct((step * chunks, tokens, width), BF16),
        input_output_aliases=aliases,
        compiler_params=pltpu.CompilerParams(vmem_limit_bytes=56 << 20),
        cost_estimate=cost(20 * step),
        name="space_attention",
    )(ids, pos, *args)


def rotary_tables(tokens, width):
    half = width // HEADS // 2
    freqs = np.power(10000.0, -np.arange(half, dtype=np.float64) / half)
    angle = (np.arange(tokens) % ROT_PERIOD)[:, None] * freqs[None, :]
    cos = np.tile(np.cos(angle).astype(np.float32), (1, HEADS))
    sin = np.tile(np.sin(angle).astype(np.float32), (1, HEADS))
    return jnp.asarray(cos), jnp.asarray(sin)


def body(
    state_tokens,
    gain_time,
    query_time,
    key_time,
    value_time,
    output_time,
    gain_space,
    query_space,
    key_space,
    value_space,
    output_space,
    neighbours,
):
    frames_here, tokens_here, width = state_tokens.shape
    frame_count = lax.axis_size("frame")
    tile_count = lax.axis_size("tile")
    me = lax.axis_index("frame")
    tile = lax.axis_index("tile")
    chunks = FRAME_CHUNKS if frames_here % FRAME_CHUNKS == 0 else 1
    rows = tokens_here // frame_count

    def swap(value, k):
        return lax.ppermute(value, "frame", [(i, i ^ k) for i in range(frame_count)])

    pieces = []
    for k in range(frame_count):
        part = lax.dynamic_slice_in_dim(state_tokens, (me ^ k) * rows, rows, axis=1)
        pieces.append(part if k == 0 else swap(part, k))
    outs = time_stage(
        pieces, chunks, gain_time.reshape(1, width), query_time, key_time, value_time, output_time
    )

    pairs = [(i, i ^ 1) for i in range(tile_count)]
    onward = [(i, (i + 2) % tile_count if i % 2 == 0 else (i - 2) % tile_count) for i in range(tile_count)]
    split = rows % BLOCK == 0
    places = me ^ jnp.arange(frame_count, dtype=jnp.int32)
    owns, nears = [], []
    for j in range(chunks):
        own = [outs[k * chunks + j] for k in range(frame_count)]
        own = [p if k == 0 else swap(p, k) for k, p in enumerate(own)]
        if not split:
            stacked = jnp.stack(own, axis=1)[:, places]
            own = [stacked.reshape(-1, tokens_here, width)]
        owns.append(own)
        normed = norm_stage(own, gain_space.reshape(1, width))
        nears.append((normed, lax.ppermute(normed, "tile", pairs)))

    blocks = tokens_here // BLOCK
    total = blocks * tile_count
    even = tile % 2 == 0
    offset = (neighbours - (tile - 1) * blocks) % total
    side_of = offset // blocks
    side_at = jnp.where(side_of == 1, 0, jnp.where((side_of == 2) == even, 1, 2))
    inner = offset % blocks
    own_inner = jnp.arange(blocks, dtype=jnp.int32)
    if split:
        per = rows // BLOCK
        inner = ((inner // per) ^ me) * per + inner % per
        own_inner = ((own_inner // per) ^ me) * per + own_inner % per
        pos = (places * rows).astype(jnp.int32)
    else:
        pos = jnp.zeros((1,), jnp.int32)
    present = neighbours >= 0
    ids = jnp.where(present, side_at * blocks + inner, own_inner[:, None])
    ids = jnp.concatenate(
        [ids, present[:, -1:].astype(jnp.int32), own_inner[:, None]], axis=1
    ).reshape(-1)
    cos, sin = rotary_tables(tokens_here, width)
    result = None
    far = lax.ppermute(nears[0][1], "tile", onward)
    for j in range(chunks):
        later = None
        normed, near = nears[j]
        if j + 1 < chunks:
            if result is None:
                normed, nears[j + 1] = lax.optimization_barrier((normed, nears[j + 1]))
            else:
                normed, nears[j + 1], result = lax.optimization_barrier((normed, nears[j + 1], result))
            later = lax.ppermute(nears[j + 1][1], "tile", onward)
        result = space_stage(
            owns[j], (normed, near, far), ids, pos, query_space, key_space, value_space,
            output_space, cos, sin, result, j, chunks,
        )
        far = later
    return result


def solution(mesh):
    rows = P("frame", "tile", None)
    return jax.shard_map(
        body,
        mesh=mesh,
        in_specs=(rows,) + (P(),) * 10 + (P("tile", None),),
        out_specs=rows,
        check_vma=False,
    )
```

```python
import functools

import jax
import jax.numpy as jnp
import numpy as np
from jax import lax
from jax.experimental import pallas as pl
from jax.experimental.pallas import tpu as pltpu
from jax.sharding import PartitionSpec as P

HEADS = 8
BLOCK = 128
NEIGHBOUR_COUNT = 9
EPS = 1e-05
ROT_PERIOD = 1024
LOG2E = 1.4426950408889634
SAFE_SCORE = 64.0
TIME_UNROLL = 4
SPACE_UNROLL = 1
BF16 = jnp.bfloat16
F32 = jnp.float32


def rms_rows(x, gain):
    square_mean = jnp.mean(x * x, axis=-1, keepdims=True)
    return (x * lax.rsqrt(square_mean + EPS) * gain).astype(BF16)


def mm(a, b):
    return jnp.dot(a, b, preferred_element_type=F32)


def mm_t(a, b):
    return lax.dot_general(a, b, (((1,), (1,)), ((), ())), preferred_element_type=F32)


def iota(shape, dim):
    return lax.broadcasted_iota(jnp.int32, shape, dim)


def two_halves(rows):
    half = rows.shape[1] // 2
    zero = jnp.zeros((rows.shape[0], half), rows.dtype)
    first = jnp.concatenate([rows[:, :half], zero], axis=1)
    second = jnp.concatenate([zero, rows[:, half:]], axis=1)
    return jnp.concatenate([first, second], axis=0)


def head_squares(rows, one_head):
    return jnp.max(mm((rows * rows).astype(BF16), one_head), axis=0, keepdims=True)


def cost(us):
    return pl.CostEstimate(flops=int(us * 900e6), transcendentals=0, bytes_accessed=int(us * 1e6))


def time_kernel(scale, pieces, splits, gain_ref, wq_ref, wk_ref, wv_ref, wo_ref, *refs):
    x_refs = refs[:pieces]
    o_refs = refs[pieces : pieces + pieces * len(splits)]
    q_s, k_s, v_s, a_s = refs[pieces + pieces * len(splits) :]
    tokens, width = x_refs[0].shape[1:]
    head_dim = width // HEADS
    frames = q_s.shape[0]
    x = jnp.concatenate([r[...].astype(F32) for r in x_refs], axis=0)
    normed = rms_rows(x, gain_ref[...]).reshape(frames * tokens, width)
    q = mm(normed, wq_ref[...]) * scale
    k = mm(normed, wk_ref[...])
    q_s[...] = q.reshape(frames, tokens, width)
    k_s[...] = k.reshape(frames, tokens, width)
    v_s[...] = mm(normed, wv_ref[...]).reshape(frames, tokens, width)
    half = width // 2
    pairs = HEADS // 2
    one_head = jnp.where(
        iota((width, half), 0) // head_dim == iota((width, half), 1) // (half // HEADS), 1.0, 0.0
    ).astype(BF16)
    bound = jnp.max(head_squares(q, one_head) * head_squares(k, one_head))
    rows = frames * 8
    pair_of = (iota((1, width), 1) % half) // head_dim
    same = (iota((pairs * rows, 2 * rows), 0) % 8) == (iota((pairs * rows, 2 * rows), 1) % 8)
    ones = jnp.ones((rows, half), BF16)

    def attend(shift):
        def group(g, _):
            part = pl.ds(pl.multiple_of(g * 8, 8), 8)
            q = q_s[:, part, :].reshape(rows, width).astype(BF16)
            k = two_halves(k_s[:, part, :].reshape(rows, width).astype(BF16))
            v = two_halves(v_s[:, part, :].reshape(rows, width).astype(BF16))
            qm = jnp.concatenate([jnp.where(pair_of == h, q, 0).astype(BF16) for h in range(pairs)], axis=0)
            s = mm_t(qm, k)
            if shift:
                s = jnp.where(same, s, -1e30)
                tops = [jnp.max(s[:, i * rows : (i + 1) * rows], axis=1, keepdims=True) for i in range(2)]
                tops = [jnp.broadcast_to(t, (pairs * rows, rows)) for t in tops]
                s = s - jnp.concatenate(tops, axis=1)
            p = jnp.where(same, jnp.exp2(s), 0.0).astype(BF16)
            o = mm(p, v)
            d = mm(p, two_halves(jnp.concatenate([ones, ones], axis=1)))
            top, low = o[:rows], d[:rows]
            for h in range(1, pairs):
                top = jnp.where(pair_of == h, o[h * rows : (h + 1) * rows], top)
                low = jnp.where(pair_of == h, d[h * rows : (h + 1) * rows], low)
            a_s[:, part, :] = (top / low).reshape(frames, 8, width)
            return 0

        lax.fori_loop(0, tokens // 8, group, 0, unroll=TIME_UNROLL)

    safe = bound <= SAFE_SCORE * SAFE_SCORE

    @pl.when(safe)
    def _():
        attend(False)

    @pl.when(jnp.logical_not(safe))
    def _():
        attend(True)

    attended = a_s[...].reshape(frames * tokens, width).astype(BF16)
    middle = x + mm(attended, wo_ref[...]).reshape(frames, tokens, width)
    low = 0
    for i, o_ref in enumerate(o_refs):
        step = splits[i % len(splits)]
        o_ref[...] = middle[low : low + step].astype(BF16)
        low += step


def time_stage(pieces, splits, gain, wq, wk, wv, wo):
    frames_here, tokens, width = pieces[0].shape
    frames = frames_here * len(pieces)
    tile = min(tokens, 128)
    scale = LOG2E / float(np.sqrt(width // HEADS))
    full = pl.BlockSpec((width, width), lambda t: (0, 0))
    steps = list(splits) * len(pieces)
    return pl.pallas_call(
        functools.partial(time_kernel, scale, len(pieces), splits),
        grid=(tokens // tile,),
        in_specs=[pl.BlockSpec((1, width), lambda t: (0, 0))]
        + [full] * 4
        + [pl.BlockSpec((frames_here, tile, width), lambda t: (0, t, 0))] * len(pieces),
        out_specs=[pl.BlockSpec((step, tile, width), lambda t: (0, t, 0)) for step in steps],
        out_shape=[jax.ShapeDtypeStruct((step, tokens, width), BF16) for step in steps],
        scratch_shapes=[pltpu.VMEM((frames, tile, width), F32)] * 4,
        compiler_params=pltpu.CompilerParams(vmem_limit_bytes=48 << 20),
        cost_estimate=cost(8),
        name="time_attention",
    )(gain, wq, wk, wv, wo, *pieces)


def ordered(weight):
    width = weight.shape[0]
    quarter = width // HEADS // 2
    src = iota((width, width), 0)
    dst = iota((width, width), 1)
    within = dst % (width // 2)
    head = dst // (width // 2) * (HEADS // 2) + within % (width // 4) // quarter
    wanted = head * 2 * quarter + within // (width // 4) * quarter + dst % quarter
    return mm(weight, jnp.where(src == wanted, 1.0, 0.0).astype(BF16)).astype(BF16)


def ordered_t(weight):
    return ordered(weight).astype(F32).T.astype(BF16)


def ordered_heads(width):
    lane = iota((width, width // 2), 0)
    quarter = width // HEADS // 2
    head = lane // (width // 2) * (HEADS // 2) + lane % (width // 4) // quarter
    return jnp.where(head == iota((width, width // 2), 1) // (width // 2 // HEADS), 1.0, 0.0).astype(BF16)


def turned(rows, c, s):
    half = rows.shape[1] // 2
    parts = [rows[:, :half], rows[:, half:]]
    return jnp.concatenate([p * c + pltpu.roll(p, half // 2, 1) * s for p in parts], axis=1)


def made_key(normed, wk_t, c, s):
    made = mm_t(wk_t, normed)
    width = made.shape[0]
    q = width // 4
    parts = []
    for low in (0, 2 * q):
        u, w = made[low : low + q], made[low + q : low + 2 * q]
        parts += [u * c - w * s, u * s + w * c]
    squares = []
    for i in (0, 2):
        both = parts[i] * parts[i] + parts[i + 1] * parts[i + 1]
        rows = q // (HEADS // 2)
        squares += [jnp.sum(both[j * rows : (j + 1) * rows], axis=0, keepdims=True) for j in range(HEADS // 2)]
    squares = jnp.concatenate(squares, axis=0)
    lanes = [squares[:, j : j + BLOCK] for j in range(0, squares.shape[1], BLOCK)]
    return jnp.concatenate(parts, axis=0).astype(BF16), functools.reduce(jnp.maximum, lanes)


def own_kernel(scale, pieces, pos, n_ref, wq_ref, wk_ref, wv_ref, cos_ref, sin_ref, cost_ref, sint_ref, *refs):
    q_ref, k_ref, v_ref, top_ref = refs
    tokens, width = n_ref.shape[1:]
    rows = tokens // pieces
    wq, wk_t = ordered(wq_ref[...]), ordered_t(wk_ref[...])
    one_head = ordered_heads(width)
    q_top, k_top = None, None
    for i in range(pieces):
        part = slice(i * rows, (i + 1) * rows)
        at = pl.ds(pl.multiple_of(pos[i], rows), rows)
        normed = n_ref[0, part, :]
        v_ref[0, part, :] = mm(normed, wv_ref[...]).astype(BF16)
        made = turned(mm(normed, wq) * scale, cos_ref[at, :], sin_ref[at, :])
        q_ref[0, part, :] = made.astype(BF16)
        top = head_squares(made, one_head)
        q_top = top if q_top is None else jnp.maximum(q_top, top)
        made, top = made_key(normed, wk_t, cost_ref[:, at], sint_ref[:, at])
        for j in range(rows // BLOCK):
            k_ref[0, i * rows // BLOCK + j] = made[:, j * BLOCK : (j + 1) * BLOCK]
        k_top = top if k_top is None else jnp.maximum(k_top, top)
    top_ref[0] = jnp.concatenate([q_top, jnp.zeros((7, width // 2), F32), k_top], axis=0)


def own_stage(normed, pos, wq, wk, wv, tables):
    step, tokens, width = normed.shape
    scale = LOG2E / float(np.sqrt(width // HEADS))
    full = pl.BlockSpec((width, width), lambda f, *_: (0, 0))
    table = [pl.BlockSpec(t.shape, lambda f, *_: (0, 0)) for t in tables]
    rows = pl.BlockSpec((1, tokens, width), lambda f, *_: (f, 0, 0))
    shape = jax.ShapeDtypeStruct(normed.shape, BF16)
    k_shape = (step, tokens // BLOCK, width, BLOCK)
    return pl.pallas_call(
        functools.partial(own_kernel, scale, pos.shape[0]),
        grid_spec=pltpu.PrefetchScalarGridSpec(
            num_scalar_prefetch=1,
            grid=(step,),
            in_specs=[rows, full, full, full, *table],
            out_specs=[
                rows,
                pl.BlockSpec((1,) + k_shape[1:], lambda f, *_: (f, 0, 0, 0)),
                rows,
                pl.BlockSpec((1, 16, width // 2), lambda f, *_: (f, 0, 0)),
            ],
        ),
        out_shape=[
            shape,
            jax.ShapeDtypeStruct(k_shape, BF16),
            shape,
            jax.ShapeDtypeStruct((step, 16, width // 2), F32),
        ],
        compiler_params=pltpu.CompilerParams(vmem_limit_bytes=48 << 20),
        cost_estimate=cost(3),
        name="own_rows",
    )(pos, normed, wq, wk, wv, *tables)


def space_kernel(scale, pieces, has_prev, ids, pos, wk_ref, wv_ref, wo_ref, cost_ref, sint_ref, *refs):
    x_refs, n_refs = refs[:pieces], refs[pieces : pieces + 2]
    q_ref, ko_ref, vo_ref, top_ref = refs[pieces + 2 : pieces + 6]
    refs = refs[pieces + 6 + (1 if has_prev else 0) :]
    o_ref, wk_s, k_s, v_s, x_s, kg, vg = refs
    piece_rows, width = x_refs[0].shape[1:]
    tokens = pieces * piece_rows
    half = width // 2
    head_dim = width // HEADS
    pairs = HEADS // 2

    wk_s[...] = ordered_t(wk_ref[...])
    kg[...] = jnp.zeros_like(kg)
    vg[...] = jnp.zeros_like(vg)

    per_tile = tokens // BLOCK
    k_s[:per_tile] = ko_ref[0]
    v_s[:tokens, :] = vo_ref[0]
    k_top = top_ref[0, 8:16, :]
    for side in range(2):
        for i in range(pieces):
            low = i * piece_rows
            normed = n_refs[side][0, low : low + piece_rows, :]
            at = pl.ds(pl.multiple_of(pos[i], piece_rows), piece_rows)
            if side == 0:
                x_s[low : low + piece_rows, :] = x_refs[i][0]
            low += (side + 1) * tokens
            rows = slice(low, low + piece_rows)
            made, top = made_key(normed, wk_s[...], cost_ref[:, at], sint_ref[:, at])
            for j in range(piece_rows // BLOCK):
                k_s[low // BLOCK + j] = made[:, j * BLOCK : (j + 1) * BLOCK]
            k_top = jnp.maximum(k_top, top)
            v_s[rows, :] = mm(normed, wv_ref[...]).astype(BF16)
    top = jnp.max(k_top) * jnp.max(top_ref[0, 0:1, :])

    wide = 2 * NEIGHBOUR_COUNT * BLOCK
    lane = iota((1, width), 1)
    rot_pair = (lane % (half // 2)) // (head_dim // 2)
    pair_of = (lane % half) // head_dim
    def attend(shift, block):
        base = block * (NEIGHBOUR_COUNT + 2)
        for m in range(NEIGHBOUR_COUNT):
            at = pl.ds(pl.multiple_of(ids[base + m] * BLOCK, BLOCK), BLOCK)
            first = slice(2 * m * BLOCK, (2 * m + 1) * BLOCK)
            second = slice((2 * m + 1) * BLOCK, (2 * m + 2) * BLOCK)
            kg[:half, first] = k_s[ids[base + m], :half, :]
            kg[half:, second] = k_s[ids[base + m], half:, :]
            vg[first, :half] = v_s[at, :half]
            vg[second, half:] = v_s[at, half:]
        present = ids[base + NEIGHBOUR_COUNT] > 0
        own = pl.ds(pl.multiple_of(ids[base + NEIGHBOUR_COUNT + 1] * BLOCK, BLOCK), BLOCK)
        bias = jnp.where(present | (iota((1, wide), 1) < wide - 2 * BLOCK), 0.0, -1e30)
        q = q_ref[0, own, :]
        qm = jnp.concatenate([jnp.where(rot_pair == h, q, 0).astype(BF16) for h in range(pairs)], axis=0)
        s = mm(qm, kg[...]) + bias
        parts = [s[:, i * BLOCK : (i + 1) * BLOCK] for i in range(2 * NEIGHBOUR_COUNT)]
        if shift:
            tops = []
            for i in range(2):
                top = functools.reduce(jnp.maximum, parts[i::2])
                tops.append(jnp.max(top, axis=1, keepdims=True))
            parts = [x - tops[i % 2] for i, x in enumerate(parts)]
        parts = [jnp.exp2(x) for x in parts]
        d = [jnp.sum(functools.reduce(jnp.add, parts[i::2]), axis=1, keepdims=True) for i in range(2)]
        p = jnp.concatenate([x.astype(BF16) for x in parts], axis=1)
        o = mm(p, vg[...])
        o = jnp.concatenate([o[:, :half] / d[0], o[:, half:] / d[1]], axis=1)
        acc = o[:BLOCK]
        for h in range(1, pairs):
            acc = jnp.where(pair_of == h, o[h * BLOCK : (h + 1) * BLOCK], acc)
        y = mm(acc.astype(BF16), wo_ref[...])
        at = pl.ds(pl.multiple_of(block * BLOCK, BLOCK), BLOCK)
        o_ref[0, at, :] = (x_s[own, :].astype(F32) + y).astype(BF16)

    def all_blocks(shift, unroll):
        def step(block, _):
            attend(shift, block)
            return 0

        lax.fori_loop(0, tokens // BLOCK, step, 0, unroll=unroll)

    safe = top <= SAFE_SCORE * SAFE_SCORE

    @pl.when(safe)
    def _():
        all_blocks(False, SPACE_UNROLL)

    @pl.when(jnp.logical_not(safe))
    def _():
        all_blocks(True, 1)


def norm_kernel(pieces, gain_ref, *refs):
    rows = refs[0].shape[1]
    for i in range(pieces):
        refs[pieces][:, i * rows : (i + 1) * rows, :] = rms_rows(refs[i][...].astype(F32), gain_ref[...])


def piece_specs(own):
    return [pl.BlockSpec((1,) + p.shape[1:], lambda f, *_, at=at: (at, 0, 0)) for p, at in own]


def norm_stage(own, gain):
    rows, width = own[0][0].shape[1:]
    shape = (1, rows * len(own), width)
    return pl.pallas_call(
        functools.partial(norm_kernel, len(own)),
        grid=(1,),
        in_specs=[pl.BlockSpec((1, width), lambda f: (0, 0))] + piece_specs(own),
        out_specs=pl.BlockSpec(shape, lambda f: (0, 0, 0)),
        out_shape=jax.ShapeDtypeStruct(shape, BF16),
        compiler_params=pltpu.CompilerParams(vmem_limit_bytes=48 << 20),
        cost_estimate=cost(2),
        name="norm_join",
    )(gain, *[p for p, _ in own])


def space_stage(own, normed, made, ids, pos, wk, wv, wo, tables, prev, frame, frames):
    pieces = len(own)
    piece_rows, width = own[0][0].shape[1:]
    tokens = pieces * piece_rows
    scale = LOG2E / float(np.sqrt(width // HEADS))
    full = pl.BlockSpec((width, width), lambda f, *_: (0, 0))
    table = [pl.BlockSpec(t.shape, lambda f, *_: (0, 0)) for t in tables]
    keys = pl.BlockSpec((1,) + made[1].shape[1:], lambda f, *_: (f, 0, 0, 0))
    whole = pl.BlockSpec((1, tokens, width), lambda f, *_: (f, 0, 0))
    tops = pl.BlockSpec((1, 16, width // 2), lambda f, *_: (f, 0, 0))
    in_specs = [full] * 3 + table + piece_specs(own) + [whole] * 3 + [keys, whole, tops]
    args = [wk, wv, wo, *tables, *[p for p, _ in own], *normed, *made]
    aliases = {}
    if prev is not None:
        in_specs.append(pl.BlockSpec(memory_space=pl.ANY))
        aliases = {2 + len(args): 0}
        args.append(prev)
    wide = 2 * NEIGHBOUR_COUNT * BLOCK
    spec = pltpu.PrefetchScalarGridSpec(
        num_scalar_prefetch=2,
        grid=(1,),
        in_specs=in_specs,
        out_specs=pl.BlockSpec((1, tokens, width), lambda f, *_: (frame, 0, 0)),
        scratch_shapes=[
            pltpu.VMEM((width, width), BF16),
            pltpu.VMEM((3 * tokens // BLOCK, width, BLOCK), BF16),
            pltpu.VMEM((3 * tokens, width), BF16),
            pltpu.VMEM((tokens, width), BF16),
            pltpu.VMEM((width, wide), BF16),
            pltpu.VMEM((wide, width), BF16),
        ],
    )
    return pl.pallas_call(
        functools.partial(space_kernel, scale, pieces, prev is not None),
        grid_spec=spec,
        out_shape=jax.ShapeDtypeStruct((frames, tokens, width), BF16),
        input_output_aliases=aliases,
        compiler_params=pltpu.CompilerParams(vmem_limit_bytes=56 << 20),
        cost_estimate=cost(18),
        name="space_attention",
    )(ids, pos, *args)


def rotary_tables(tokens, width):
    half = width // HEADS // 2
    freqs = np.power(10000.0, -np.arange(half, dtype=np.float64) / half)
    angle = (np.arange(tokens) % ROT_PERIOD)[:, None] * freqs[None, :]
    cos = np.tile(np.cos(angle).astype(np.float32), (1, HEADS))
    sin = np.sin(angle).astype(np.float32)
    sin = np.concatenate([np.tile(-sin, (1, HEADS // 2)), np.tile(sin, (1, HEADS // 2))], axis=1)
    turned_over = np.concatenate([np.cos(angle), np.sin(angle)], axis=1).astype(np.float32).T
    cos_t, sin_t = (np.tile(turned_over[i * half : (i + 1) * half], (HEADS // 2, 1)) for i in range(2))
    return [jnp.asarray(t) for t in (cos, sin, cos_t, sin_t)]


def body(
    state_tokens,
    gain_time,
    query_time,
    key_time,
    value_time,
    output_time,
    gain_space,
    query_space,
    key_space,
    value_space,
    output_space,
    neighbours,
):
    frames_here, tokens_here, width = state_tokens.shape
    frame_count = lax.axis_size("frame")
    tile_count = lax.axis_size("tile")
    me = lax.axis_index("frame")
    tile = lax.axis_index("tile")
    rows = tokens_here // frame_count
    parts = 2 if rows % (2 * BLOCK) == 0 else 1
    part_rows = rows // parts

    def swap(value, k):
        return value if k == 0 else lax.ppermute(value, "frame", [(i, i ^ k) for i in range(frame_count)])

    last_cut = [1] * frames_here if frames_here < 3 else [1, 1, frames_here - 2]
    held = []
    for part in range(parts):
        pieces = []
        for k in range(frame_count):
            low = (me ^ k) * rows + part * part_rows
            pieces.append(swap(lax.dynamic_slice_in_dim(state_tokens, low, part_rows, axis=1), k))
        cut = last_cut if part == parts - 1 else [frames_here]
        outs = time_stage(
            pieces, cut, gain_time.reshape(1, width), query_time, key_time, value_time, output_time
        )
        back = [[swap(outs[k * len(cut) + c], k) for c in range(len(cut))] for k in range(frame_count)]
        held.append((cut, back))

    def frame_pieces(frame):
        own = []
        for k in range(frame_count):
            for cut, back in held:
                low = 0
                for c, step in enumerate(cut):
                    if low <= frame < low + step:
                        own.append((back[k][c], frame - low))
                    low += step
        return own

    pairs = [(i, i ^ 1) for i in range(tile_count)]
    onward = [(i, (i + 2) % tile_count if i % 2 == 0 else (i - 2) % tile_count) for i in range(tile_count)]
    split = part_rows % BLOCK == 0
    places = me ^ jnp.arange(frame_count, dtype=jnp.int32)
    if split:
        pos = (places[:, None] * rows + jnp.arange(parts, dtype=jnp.int32) * part_rows).reshape(-1)
    else:
        pos = jnp.zeros((1,), jnp.int32)
    tables = rotary_tables(tokens_here, width)
    owns, nears, mades = [], [], []
    for frame in range(frames_here):
        own = frame_pieces(frame)
        if not split:
            stacked = jnp.stack([p[at] for p, at in own])[places]
            own = [(stacked.reshape(1, tokens_here, width), 0)]
        normed = norm_stage(own, gain_space.reshape(1, width))
        owns.append(own)
        nears.append(lax.ppermute(normed, "tile", pairs))
        mades.append(own_stage(normed, pos, query_space, key_space, value_space, tables))

    blocks = tokens_here // BLOCK
    total = blocks * tile_count
    even = tile % 2 == 0
    offset = (neighbours - (tile - 1) * blocks) % total
    side_of = offset // blocks
    side_at = jnp.where(side_of == 1, 0, jnp.where((side_of == 2) == even, 1, 2))
    inner = offset % blocks
    own_inner = jnp.arange(blocks, dtype=jnp.int32)
    if split:
        per = rows // BLOCK
        inner = ((inner // per) ^ me) * per + inner % per
        own_inner = ((own_inner // per) ^ me) * per + own_inner % per
    present = neighbours >= 0
    ids = jnp.where(present, side_at * blocks + inner, own_inner[:, None])
    ids = jnp.concatenate(
        [ids, present[:, -1:].astype(jnp.int32), own_inner[:, None]], axis=1
    ).reshape(-1)
    result = None
    far = lax.ppermute(nears[0], "tile", onward)
    for frame in range(frames_here):
        later = None
        near = nears[frame]
        if frame + 1 < frames_here:
            if result is None:
                near, nears[frame + 1] = lax.optimization_barrier((near, nears[frame + 1]))
            else:
                near, nears[frame + 1], result = lax.optimization_barrier((near, nears[frame + 1], result))
            later = lax.ppermute(nears[frame + 1], "tile", onward)
        result = space_stage(
            owns[frame], (near, far), mades[frame], ids, pos, key_space, value_space, output_space,
            tables[2:], result, frame, frames_here,
        )
        far = later
    return result


def solution(mesh):
    rows = P("frame", "tile", None)
    return jax.shard_map(
        body,
        mesh=mesh,
        in_specs=(rows,) + (P(),) * 10 + (P("tile", None),),
        out_specs=rows,
        check_vma=False,
    )
```

```python
import functools

import jax
import jax.numpy as jnp
import numpy as np
from jax import lax
from jax.experimental import pallas as pl
from jax.experimental.pallas import tpu as pltpu
from jax.sharding import PartitionSpec as P

HEADS = 8
BLOCK = 128
NEIGHBOUR_COUNT = 9
EPS = 1e-05
ROT_PERIOD = 1024
LOG2E = 1.4426950408889634
SAFE_SCORE = 64.0
TIME_UNROLL = 4
SPACE_UNROLL = 1
BF16 = jnp.bfloat16
F32 = jnp.float32


def rms_rows(x, gain):
    square_mean = jnp.mean(x * x, axis=-1, keepdims=True)
    return (x * lax.rsqrt(square_mean + EPS) * gain).astype(BF16)


def mm(a, b):
    return jnp.dot(a, b, preferred_element_type=F32)


def mm_t(a, b):
    return lax.dot_general(a, b, (((1,), (1,)), ((), ())), preferred_element_type=F32)


def iota(shape, dim):
    return lax.broadcasted_iota(jnp.int32, shape, dim)


def two_halves(rows):
    half = rows.shape[1] // 2
    zero = jnp.zeros((rows.shape[0], half), rows.dtype)
    first = jnp.concatenate([rows[:, :half], zero], axis=1)
    second = jnp.concatenate([zero, rows[:, half:]], axis=1)
    return jnp.concatenate([first, second], axis=0)


def head_squares(rows, one_head):
    return jnp.max(mm((rows * rows).astype(BF16), one_head), axis=0, keepdims=True)


def cost(us):
    return pl.CostEstimate(flops=int(us * 900e6), transcendentals=0, bytes_accessed=int(us * 1e6))


def time_kernel(scale, pieces, splits, gain_ref, wq_ref, wk_ref, wv_ref, wo_ref, *refs):
    x_refs = refs[:pieces]
    o_refs = refs[pieces : pieces + pieces * len(splits)]
    q_s, k_s, v_s, a_s = refs[pieces + pieces * len(splits) :]
    tokens, width = x_refs[0].shape[1:]
    head_dim = width // HEADS
    frames = q_s.shape[0]
    x = jnp.concatenate([r[...].astype(F32) for r in x_refs], axis=0)
    normed = rms_rows(x, gain_ref[...]).reshape(frames * tokens, width)
    q = mm(normed, wq_ref[...]) * scale
    k = mm(normed, wk_ref[...])
    q_s[...] = q.reshape(frames, tokens, width)
    k_s[...] = k.reshape(frames, tokens, width)
    v_s[...] = mm(normed, wv_ref[...]).reshape(frames, tokens, width)
    half = width // 2
    pairs = HEADS // 2
    one_head = jnp.where(
        iota((width, half), 0) // head_dim == iota((width, half), 1) // (half // HEADS), 1.0, 0.0
    ).astype(BF16)
    bound = jnp.max(head_squares(q, one_head) * head_squares(k, one_head))
    rows = frames * 8
    pair_of = (iota((1, width), 1) % half) // head_dim
    same = (iota((pairs * rows, 2 * rows), 0) % 8) == (iota((pairs * rows, 2 * rows), 1) % 8)
    ones = jnp.ones((rows, half), BF16)

    def attend(shift):
        def group(g, _):
            part = pl.ds(pl.multiple_of(g * 8, 8), 8)
            q = q_s[:, part, :].reshape(rows, width).astype(BF16)
            k = two_halves(k_s[:, part, :].reshape(rows, width).astype(BF16))
            v = two_halves(v_s[:, part, :].reshape(rows, width).astype(BF16))
            qm = jnp.concatenate([jnp.where(pair_of == h, q, 0).astype(BF16) for h in range(pairs)], axis=0)
            s = mm_t(qm, k)
            if shift:
                s = jnp.where(same, s, -1e30)
                tops = [jnp.max(s[:, i * rows : (i + 1) * rows], axis=1, keepdims=True) for i in range(2)]
                tops = [jnp.broadcast_to(t, (pairs * rows, rows)) for t in tops]
                s = s - jnp.concatenate(tops, axis=1)
            p = jnp.where(same, jnp.exp2(s), 0.0).astype(BF16)
            o = mm(p, v)
            d = mm(p, two_halves(jnp.concatenate([ones, ones], axis=1)))
            top, low = o[:rows], d[:rows]
            for h in range(1, pairs):
                top = jnp.where(pair_of == h, o[h * rows : (h + 1) * rows], top)
                low = jnp.where(pair_of == h, d[h * rows : (h + 1) * rows], low)
            a_s[:, part, :] = (top / low).reshape(frames, 8, width)
            return 0

        lax.fori_loop(0, tokens // 8, group, 0, unroll=TIME_UNROLL)

    safe = bound <= SAFE_SCORE * SAFE_SCORE

    @pl.when(safe)
    def _():
        attend(False)

    @pl.when(jnp.logical_not(safe))
    def _():
        attend(True)

    attended = a_s[...].reshape(frames * tokens, width).astype(BF16)
    middle = x + mm(attended, wo_ref[...]).reshape(frames, tokens, width)
    low = 0
    for i, o_ref in enumerate(o_refs):
        step = splits[i % len(splits)]
        o_ref[...] = middle[low : low + step].astype(BF16)
        low += step


def time_stage(pieces, splits, gain, wq, wk, wv, wo):
    frames_here, tokens, width = pieces[0].shape
    frames = frames_here * len(pieces)
    tile = min(tokens, 128)
    scale = LOG2E / float(np.sqrt(width // HEADS))
    full = pl.BlockSpec((width, width), lambda t: (0, 0))
    steps = list(splits) * len(pieces)
    return pl.pallas_call(
        functools.partial(time_kernel, scale, len(pieces), splits),
        grid=(tokens // tile,),
        in_specs=[pl.BlockSpec((1, width), lambda t: (0, 0))]
        + [full] * 4
        + [pl.BlockSpec((frames_here, tile, width), lambda t: (0, t, 0))] * len(pieces),
        out_specs=[pl.BlockSpec((step, tile, width), lambda t: (0, t, 0)) for step in steps],
        out_shape=[jax.ShapeDtypeStruct((step, tokens, width), BF16) for step in steps],
        scratch_shapes=[pltpu.VMEM((frames, tile, width), F32)] * 4,
        compiler_params=pltpu.CompilerParams(vmem_limit_bytes=48 << 20),
        cost_estimate=cost(8),
        name="time_attention",
    )(gain, wq, wk, wv, wo, *pieces)


def ordered(weight):
    width = weight.shape[0]
    quarter = width // HEADS // 2
    src = iota((width, width), 0)
    dst = iota((width, width), 1)
    within = dst % (width // 2)
    head = dst // (width // 2) * (HEADS // 2) + within % (width // 4) // quarter
    wanted = head * 2 * quarter + within // (width // 4) * quarter + dst % quarter
    return mm(weight, jnp.where(src == wanted, 1.0, 0.0).astype(BF16)).astype(BF16)


def ordered_t(weight):
    return ordered(weight).astype(F32).T.astype(BF16)


def ordered_heads(width):
    lane = iota((width, width // 2), 0)
    quarter = width // HEADS // 2
    head = lane // (width // 2) * (HEADS // 2) + lane % (width // 4) // quarter
    return jnp.where(head == iota((width, width // 2), 1) // (width // 2 // HEADS), 1.0, 0.0).astype(BF16)


def turned(rows, c, s):
    half = rows.shape[1] // 2
    parts = [rows[:, :half], rows[:, half:]]
    return jnp.concatenate([p * c + pltpu.roll(p, half // 2, 1) * s for p in parts], axis=1)


def made_key(normed, wk_t, c, s):
    made = mm_t(wk_t, normed)
    width = made.shape[0]
    q = width // 4
    parts = []
    for low in (0, 2 * q):
        u, w = made[low : low + q], made[low + q : low + 2 * q]
        parts += [u * c - w * s, u * s + w * c]
    squares = []
    for i in (0, 2):
        both = parts[i] * parts[i] + parts[i + 1] * parts[i + 1]
        rows = q // (HEADS // 2)
        squares += [jnp.sum(both[j * rows : (j + 1) * rows], axis=0, keepdims=True) for j in range(HEADS // 2)]
    squares = jnp.concatenate(squares, axis=0)
    lanes = [squares[:, j : j + BLOCK] for j in range(0, squares.shape[1], BLOCK)]
    return jnp.concatenate(parts, axis=0).astype(BF16), functools.reduce(jnp.maximum, lanes)


def own_kernel(scale, pieces, pos, n_ref, wq_ref, wk_ref, wv_ref, cos_ref, sin_ref, cost_ref, sint_ref, *refs):
    q_ref, k_ref, v_ref, top_ref = refs
    tokens, width = n_ref.shape[1:]
    rows = tokens // pieces
    wq, wk_t = ordered(wq_ref[...]), ordered_t(wk_ref[...])
    one_head = ordered_heads(width)
    q_top, k_top = None, None
    for i in range(pieces):
        part = slice(i * rows, (i + 1) * rows)
        at = pl.ds(pl.multiple_of(pos[i], rows), rows)
        normed = n_ref[0, part, :]
        v_ref[0, part, :] = mm(normed, wv_ref[...]).astype(BF16)
        made = turned(mm(normed, wq) * scale, cos_ref[at, :], sin_ref[at, :])
        q_ref[0, part, :] = made.astype(BF16)
        top = head_squares(made, one_head)
        q_top = top if q_top is None else jnp.maximum(q_top, top)
        made, top = made_key(normed, wk_t, cost_ref[:, at], sint_ref[:, at])
        for j in range(rows // BLOCK):
            k_ref[0, i * rows // BLOCK + j] = made[:, j * BLOCK : (j + 1) * BLOCK]
        k_top = top if k_top is None else jnp.maximum(k_top, top)
    top_ref[0] = jnp.concatenate([q_top, jnp.zeros((7, width // 2), F32), k_top], axis=0)


def own_stage(normed, pos, wq, wk, wv, tables):
    step, tokens, width = normed.shape
    scale = LOG2E / float(np.sqrt(width // HEADS))
    full = pl.BlockSpec((width, width), lambda f, *_: (0, 0))
    table = [pl.BlockSpec(t.shape, lambda f, *_: (0, 0)) for t in tables]
    rows = pl.BlockSpec((1, tokens, width), lambda f, *_: (f, 0, 0))
    shape = jax.ShapeDtypeStruct(normed.shape, BF16)
    k_shape = (step, tokens // BLOCK, width, BLOCK)
    return pl.pallas_call(
        functools.partial(own_kernel, scale, pos.shape[0]),
        grid_spec=pltpu.PrefetchScalarGridSpec(
            num_scalar_prefetch=1,
            grid=(step,),
            in_specs=[rows, full, full, full, *table],
            out_specs=[
                rows,
                pl.BlockSpec((1,) + k_shape[1:], lambda f, *_: (f, 0, 0, 0)),
                rows,
                pl.BlockSpec((1, 16, width // 2), lambda f, *_: (f, 0, 0)),
            ],
        ),
        out_shape=[
            shape,
            jax.ShapeDtypeStruct(k_shape, BF16),
            shape,
            jax.ShapeDtypeStruct((step, 16, width // 2), F32),
        ],
        compiler_params=pltpu.CompilerParams(vmem_limit_bytes=48 << 20),
        cost_estimate=cost(3),
        name="own_rows",
    )(pos, normed, wq, wk, wv, *tables)


def space_kernel(scale, pieces, has_prev, ids, pos, wk_ref, wv_ref, wo_ref, cost_ref, sint_ref, *refs):
    x_refs, n_refs = refs[:pieces], refs[pieces : pieces + 2]
    q_ref, ko_ref, vo_ref, top_ref = refs[pieces + 2 : pieces + 6]
    refs = refs[pieces + 6 + (1 if has_prev else 0) :]
    o_ref, wk_s, k_s, v_s, x_s, kg, vg = refs
    piece_rows, width = x_refs[0].shape[1:]
    tokens = pieces * piece_rows
    half = width // 2
    head_dim = width // HEADS
    pairs = HEADS // 2

    wk_s[...] = ordered_t(wk_ref[...])
    kg[...] = jnp.zeros_like(kg)
    vg[...] = jnp.zeros_like(vg)

    per_tile = tokens // BLOCK
    k_s[:per_tile] = ko_ref[0]
    v_s[:tokens, :] = vo_ref[0]
    k_top = top_ref[0, 8:16, :]
    for side in range(2):
        for i in range(pieces):
            low = i * piece_rows
            normed = n_refs[side][0, low : low + piece_rows, :]
            at = pl.ds(pl.multiple_of(pos[i], piece_rows), piece_rows)
            if side == 0:
                x_s[low : low + piece_rows, :] = x_refs[i][0]
            low += (side + 1) * tokens
            rows = slice(low, low + piece_rows)
            made, top = made_key(normed, wk_s[...], cost_ref[:, at], sint_ref[:, at])
            for j in range(piece_rows // BLOCK):
                k_s[low // BLOCK + j] = made[:, j * BLOCK : (j + 1) * BLOCK]
            k_top = jnp.maximum(k_top, top)
            v_s[rows, :] = mm(normed, wv_ref[...]).astype(BF16)
    top = jnp.max(k_top) * jnp.max(top_ref[0, 0:1, :])

    wide = 2 * NEIGHBOUR_COUNT * BLOCK
    lane = iota((1, width), 1)
    rot_pair = (lane % (half // 2)) // (head_dim // 2)
    pair_of = (lane % half) // head_dim
    def attend(shift, block):
        base = block * (NEIGHBOUR_COUNT + 2)
        for m in range(NEIGHBOUR_COUNT):
            at = pl.ds(pl.multiple_of(ids[base + m] * BLOCK, BLOCK), BLOCK)
            first = slice(2 * m * BLOCK, (2 * m + 1) * BLOCK)
            second = slice((2 * m + 1) * BLOCK, (2 * m + 2) * BLOCK)
            kg[:half, first] = k_s[ids[base + m], :half, :]
            kg[half:, second] = k_s[ids[base + m], half:, :]
            vg[first, :half] = v_s[at, :half]
            vg[second, half:] = v_s[at, half:]
        present = ids[base + NEIGHBOUR_COUNT] > 0
        own = pl.ds(pl.multiple_of(ids[base + NEIGHBOUR_COUNT + 1] * BLOCK, BLOCK), BLOCK)
        bias = jnp.where(present | (iota((1, wide), 1) < wide - 2 * BLOCK), 0.0, -1e30)
        q = q_ref[0, own, :]
        qm = jnp.concatenate([jnp.where(rot_pair == h, q, 0).astype(BF16) for h in range(pairs)], axis=0)
        s = mm(qm, kg[...]) + bias
        parts = [s[:, i * BLOCK : (i + 1) * BLOCK] for i in range(2 * NEIGHBOUR_COUNT)]
        if shift:
            tops = []
            for i in range(2):
                top = functools.reduce(jnp.maximum, parts[i::2])
                tops.append(jnp.max(top, axis=1, keepdims=True))
            parts = [x - tops[i % 2] for i, x in enumerate(parts)]
        parts = [jnp.exp2(x) for x in parts]
        d = [jnp.sum(functools.reduce(jnp.add, parts[i::2]), axis=1, keepdims=True) for i in range(2)]
        p = jnp.concatenate([x.astype(BF16) for x in parts], axis=1)
        o = mm(p, vg[...])
        o = jnp.concatenate([o[:, :half] / d[0], o[:, half:] / d[1]], axis=1)
        acc = o[:BLOCK]
        for h in range(1, pairs):
            acc = jnp.where(pair_of == h, o[h * BLOCK : (h + 1) * BLOCK], acc)
        y = mm(acc.astype(BF16), wo_ref[...])
        at = pl.ds(pl.multiple_of(block * BLOCK, BLOCK), BLOCK)
        o_ref[0, at, :] = (x_s[own, :].astype(F32) + y).astype(BF16)

    def all_blocks(shift, unroll):
        def step(block, _):
            attend(shift, block)
            return 0

        lax.fori_loop(0, tokens // BLOCK, step, 0, unroll=unroll)

    safe = top <= SAFE_SCORE * SAFE_SCORE

    @pl.when(safe)
    def _():
        all_blocks(False, SPACE_UNROLL)

    @pl.when(jnp.logical_not(safe))
    def _():
        all_blocks(True, 1)


def norm_kernel(pieces, gain_ref, *refs):
    rows = refs[0].shape[1]
    for i in range(pieces):
        refs[pieces][:, i * rows : (i + 1) * rows, :] = rms_rows(refs[i][...].astype(F32), gain_ref[...])


def piece_specs(own):
    return [pl.BlockSpec((1,) + p.shape[1:], lambda f, *_, at=at: (at, 0, 0)) for p, at in own]


def norm_stage(own, gain):
    rows, width = own[0][0].shape[1:]
    shape = (1, rows * len(own), width)
    return pl.pallas_call(
        functools.partial(norm_kernel, len(own)),
        grid=(1,),
        in_specs=[pl.BlockSpec((1, width), lambda f: (0, 0))] + piece_specs(own),
        out_specs=pl.BlockSpec(shape, lambda f: (0, 0, 0)),
        out_shape=jax.ShapeDtypeStruct(shape, BF16),
        compiler_params=pltpu.CompilerParams(vmem_limit_bytes=48 << 20),
        cost_estimate=cost(2),
        name="norm_join",
    )(gain, *[p for p, _ in own])


def space_stage(own, normed, made, ids, pos, wk, wv, wo, tables, prev, frame, frames):
    pieces = len(own)
    piece_rows, width = own[0][0].shape[1:]
    tokens = pieces * piece_rows
    scale = LOG2E / float(np.sqrt(width // HEADS))
    full = pl.BlockSpec((width, width), lambda f, *_: (0, 0))
    table = [pl.BlockSpec(t.shape, lambda f, *_: (0, 0)) for t in tables]
    keys = pl.BlockSpec((1,) + made[1].shape[1:], lambda f, *_: (f, 0, 0, 0))
    whole = pl.BlockSpec((1, tokens, width), lambda f, *_: (f, 0, 0))
    tops = pl.BlockSpec((1, 16, width // 2), lambda f, *_: (f, 0, 0))
    in_specs = [full] * 3 + table + piece_specs(own) + [whole] * 3 + [keys, whole, tops]
    args = [wk, wv, wo, *tables, *[p for p, _ in own], *normed, *made]
    aliases = {}
    if prev is not None:
        in_specs.append(pl.BlockSpec(memory_space=pl.ANY))
        aliases = {2 + len(args): 0}
        args.append(prev)
    wide = 2 * NEIGHBOUR_COUNT * BLOCK
    spec = pltpu.PrefetchScalarGridSpec(
        num_scalar_prefetch=2,
        grid=(1,),
        in_specs=in_specs,
        out_specs=pl.BlockSpec((1, tokens, width), lambda f, *_: (frame, 0, 0)),
        scratch_shapes=[
            pltpu.VMEM((width, width), BF16),
            pltpu.VMEM((3 * tokens // BLOCK, width, BLOCK), BF16),
            pltpu.VMEM((3 * tokens, width), BF16),
            pltpu.VMEM((tokens, width), BF16),
            pltpu.VMEM((width, wide), BF16),
            pltpu.VMEM((wide, width), BF16),
        ],
    )
    return pl.pallas_call(
        functools.partial(space_kernel, scale, pieces, prev is not None),
        grid_spec=spec,
        out_shape=jax.ShapeDtypeStruct((frames, tokens, width), BF16),
        input_output_aliases=aliases,
        compiler_params=pltpu.CompilerParams(vmem_limit_bytes=56 << 20),
        cost_estimate=cost(18),
        name="space_attention",
    )(ids, pos, *args)


def rotary_tables(tokens, width):
    half = width // HEADS // 2
    freqs = np.power(10000.0, -np.arange(half, dtype=np.float64) / half)
    angle = (np.arange(tokens) % ROT_PERIOD)[:, None] * freqs[None, :]
    cos = np.tile(np.cos(angle).astype(np.float32), (1, HEADS))
    sin = np.sin(angle).astype(np.float32)
    sin = np.concatenate([np.tile(-sin, (1, HEADS // 2)), np.tile(sin, (1, HEADS // 2))], axis=1)
    turned_over = np.concatenate([np.cos(angle), np.sin(angle)], axis=1).astype(np.float32).T
    cos_t, sin_t = (np.tile(turned_over[i * half : (i + 1) * half], (HEADS // 2, 1)) for i in range(2))
    return [jnp.asarray(t) for t in (cos, sin, cos_t, sin_t)]


def after(value, *earlier):
    return lax.optimization_barrier((value, *earlier))[0]


def body(
    state_tokens,
    gain_time,
    query_time,
    key_time,
    value_time,
    output_time,
    gain_space,
    query_space,
    key_space,
    value_space,
    output_space,
    neighbours,
):
    frames_here, tokens_here, width = state_tokens.shape
    frame_count = lax.axis_size("frame")
    tile_count = lax.axis_size("tile")
    me = lax.axis_index("frame")
    tile = lax.axis_index("tile")
    rows = tokens_here // frame_count
    parts = 2 if rows % (2 * BLOCK) == 0 else 1
    part_rows = rows // parts

    def swap(value, k):
        return value if k == 0 else lax.ppermute(value, "frame", [(i, i ^ k) for i in range(frame_count)])

    last_cut = [1] * frames_here if frames_here < 3 else [1, 1, frames_here - 2]
    held = []
    pieces = []
    for part in range(parts):
        source = after(state_tokens, pieces[1]) if part else state_tokens
        pieces = []
        for k in range(frame_count):
            low = (me ^ k) * rows + part * part_rows
            pieces.append(swap(lax.dynamic_slice_in_dim(source, low, part_rows, axis=1), k))
        cut = last_cut if part == parts - 1 else [frames_here]
        outs = time_stage(
            pieces, cut, gain_time.reshape(1, width), query_time, key_time, value_time, output_time
        )
        back = [[] for _ in range(frame_count)]
        for c in range(len(cut)):
            first = [b[c - 1] for b in back[1:]] if c else []
            for k in range(frame_count):
                out = outs[k * len(cut) + c]
                back[k].append(swap(after(out, *first) if k and c else out, k))
        held.append((cut, back))

    def frame_pieces(frame):
        own = []
        for k in range(frame_count):
            for cut, back in held:
                low = 0
                for c, step in enumerate(cut):
                    if low <= frame < low + step:
                        own.append((back[k][c], frame - low))
                    low += step
        return own

    pairs = [(i, i ^ 1) for i in range(tile_count)]
    onward = [(i, (i + 2) % tile_count if i % 2 == 0 else (i - 2) % tile_count) for i in range(tile_count)]
    split = part_rows % BLOCK == 0
    places = me ^ jnp.arange(frame_count, dtype=jnp.int32)
    if split:
        pos = (places[:, None] * rows + jnp.arange(parts, dtype=jnp.int32) * part_rows).reshape(-1)
    else:
        pos = jnp.zeros((1,), jnp.int32)
    tables = rotary_tables(tokens_here, width)
    owns, nears, mades = [], [], []
    for frame in range(frames_here):
        own = frame_pieces(frame)
        if not split:
            stacked = jnp.stack([p[at] for p, at in own])[places]
            own = [(stacked.reshape(1, tokens_here, width), 0)]
        normed = norm_stage(own, gain_space.reshape(1, width))
        owns.append(own)
        nears.append(lax.ppermute(after(normed, nears[-1]) if frame else normed, "tile", pairs))
        mades.append(own_stage(normed, pos, query_space, key_space, value_space, tables))

    blocks = tokens_here // BLOCK
    total = blocks * tile_count
    even = tile % 2 == 0
    offset = (neighbours - (tile - 1) * blocks) % total
    side_of = offset // blocks
    side_at = jnp.where(side_of == 1, 0, jnp.where((side_of == 2) == even, 1, 2))
    inner = offset % blocks
    own_inner = jnp.arange(blocks, dtype=jnp.int32)
    if split:
        per = rows // BLOCK
        inner = ((inner // per) ^ me) * per + inner % per
        own_inner = ((own_inner // per) ^ me) * per + own_inner % per
    present = neighbours >= 0
    ids = jnp.where(present, side_at * blocks + inner, own_inner[:, None])
    ids = jnp.concatenate(
        [ids, present[:, -1:].astype(jnp.int32), own_inner[:, None]], axis=1
    ).reshape(-1)
    result = None
    far = lax.ppermute(nears[0], "tile", onward)
    for frame in range(frames_here):
        later = None
        near = nears[frame]
        if frame + 1 < frames_here:
            if result is None:
                near, nears[frame + 1] = lax.optimization_barrier((near, nears[frame + 1]))
            else:
                near, nears[frame + 1], result = lax.optimization_barrier((near, nears[frame + 1], result))
            later = lax.ppermute(nears[frame + 1], "tile", onward)
        result = space_stage(
            owns[frame], (near, far), mades[frame], ids, pos, key_space, value_space, output_space,
            tables[2:], result, frame, frames_here,
        )
        far = later
    return result


def solution(mesh):
    rows = P("frame", "tile", None)
    return jax.shard_map(
        body,
        mesh=mesh,
        in_specs=(rows,) + (P(),) * 10 + (P("tile", None),),
        out_specs=rows,
        check_vma=False,
    )
```

```python
import functools

import jax
import jax.numpy as jnp
import numpy as np
from jax import lax
from jax.experimental import pallas as pl
from jax.experimental.pallas import tpu as pltpu
from jax.sharding import PartitionSpec as P

HEADS = 8
BLOCK = 128
NEIGHBOUR_COUNT = 9
EPS = 1e-05
ROT_PERIOD = 1024
LOG2E = 1.4426950408889634
SAFE_SCORE = 90.0
TIME_UNROLL = 4
BF16 = jnp.bfloat16
F32 = jnp.float32


def rms_rows(x, gain):
    square_mean = jnp.mean(x * x, axis=-1, keepdims=True)
    return (x * lax.rsqrt(square_mean + EPS) * gain).astype(BF16)


def mm(a, b):
    return jnp.dot(a, b, preferred_element_type=F32)


def mm_t(a, b):
    return lax.dot_general(a, b, (((1,), (1,)), ((), ())), preferred_element_type=F32)


def iota(shape, dim):
    return lax.broadcasted_iota(jnp.int32, shape, dim)


def two_halves(rows):
    half = rows.shape[1] // 2
    zero = jnp.zeros((rows.shape[0], half), rows.dtype)
    first = jnp.concatenate([rows[:, :half], zero], axis=1)
    second = jnp.concatenate([zero, rows[:, half:]], axis=1)
    return jnp.concatenate([first, second], axis=0)


def head_squares(rows, one_head):
    return jnp.max(mm((rows * rows).astype(BF16), one_head), axis=0, keepdims=True)


def cost(us):
    return pl.CostEstimate(flops=int(us * 900e6), transcendentals=0, bytes_accessed=int(us * 1e6))


def time_kernel(scale, pieces, splits, gain_ref, wq_ref, wk_ref, wv_ref, wo_ref, *refs):
    x_refs = refs[:pieces]
    o_refs = refs[pieces : pieces + pieces * len(splits)]
    q_s, k_s, v_s, a_s = refs[pieces + pieces * len(splits) :]
    tokens, width = x_refs[0].shape[1:]
    head_dim = width // HEADS
    frames = q_s.shape[0]
    x = jnp.concatenate([r[...].astype(F32) for r in x_refs], axis=0)
    normed = rms_rows(x, gain_ref[...]).reshape(frames * tokens, width)
    q = mm(normed, wq_ref[...]) * scale
    k = mm(normed, wk_ref[...])
    q_s[...] = q.reshape(frames, tokens, width)
    k_s[...] = k.reshape(frames, tokens, width)
    v_s[...] = mm(normed, wv_ref[...]).reshape(frames, tokens, width)
    half = width // 2
    pairs = HEADS // 2
    one_head = jnp.where(
        iota((width, half), 0) // head_dim == iota((width, half), 1) // (half // HEADS), 1.0, 0.0
    ).astype(BF16)
    bound = jnp.max(head_squares(q, one_head) * head_squares(k, one_head))
    rows = frames * 8
    pair_of = (iota((1, width), 1) % half) // head_dim
    same = (iota((pairs * rows, 2 * rows), 0) % 8) == (iota((pairs * rows, 2 * rows), 1) % 8)
    ones = jnp.ones((rows, half), BF16)

    def attend(shift):
        def group(g, _):
            part = pl.ds(pl.multiple_of(g * 8, 8), 8)
            q = q_s[:, part, :].reshape(rows, width).astype(BF16)
            k = two_halves(k_s[:, part, :].reshape(rows, width).astype(BF16))
            v = two_halves(v_s[:, part, :].reshape(rows, width).astype(BF16))
            qm = jnp.concatenate([jnp.where(pair_of == h, q, 0).astype(BF16) for h in range(pairs)], axis=0)
            s = mm_t(qm, k)
            if shift:
                s = jnp.where(same, s, -1e30)
                tops = [jnp.max(s[:, i * rows : (i + 1) * rows], axis=1, keepdims=True) for i in range(2)]
                tops = [jnp.broadcast_to(t, (pairs * rows, rows)) for t in tops]
                s = s - jnp.concatenate(tops, axis=1)
            p = jnp.where(same, jnp.exp2(s), 0.0).astype(BF16)
            o = mm(p, v)
            d = mm(p, two_halves(jnp.concatenate([ones, ones], axis=1)))
            top, low = o[:rows], d[:rows]
            for h in range(1, pairs):
                top = jnp.where(pair_of == h, o[h * rows : (h + 1) * rows], top)
                low = jnp.where(pair_of == h, d[h * rows : (h + 1) * rows], low)
            a_s[:, part, :] = (top / low).reshape(frames, 8, width)
            return 0

        lax.fori_loop(0, tokens // 8, group, 0, unroll=TIME_UNROLL)

    safe = bound <= SAFE_SCORE * SAFE_SCORE

    @pl.when(safe)
    def _():
        attend(False)

    @pl.when(jnp.logical_not(safe))
    def _():
        attend(True)

    attended = a_s[...].reshape(frames * tokens, width).astype(BF16)
    middle = x + mm(attended, wo_ref[...]).reshape(frames, tokens, width)
    low = 0
    for i, o_ref in enumerate(o_refs):
        step = splits[i % len(splits)]
        o_ref[...] = middle[low : low + step].astype(BF16)
        low += step


def time_stage(pieces, splits, gain, wq, wk, wv, wo):
    frames_here, tokens, width = pieces[0].shape
    frames = frames_here * len(pieces)
    tile = min(tokens, 128)
    scale = LOG2E / float(np.sqrt(width // HEADS))
    full = pl.BlockSpec((width, width), lambda t: (0, 0))
    steps = list(splits) * len(pieces)
    return pl.pallas_call(
        functools.partial(time_kernel, scale, len(pieces), splits),
        grid=(tokens // tile,),
        in_specs=[pl.BlockSpec((1, width), lambda t: (0, 0))]
        + [full] * 4
        + [pl.BlockSpec((frames_here, tile, width), lambda t: (0, t, 0))] * len(pieces),
        out_specs=[pl.BlockSpec((step, tile, width), lambda t: (0, t, 0)) for step in steps],
        out_shape=[jax.ShapeDtypeStruct((step, tokens, width), BF16) for step in steps],
        scratch_shapes=[pltpu.VMEM((frames, tile, width), F32)] * 4,
        compiler_params=pltpu.CompilerParams(vmem_limit_bytes=48 << 20),
        cost_estimate=cost(8),
        name="time_attention",
    )(gain, wq, wk, wv, wo, *pieces)


def ordered(weight):
    width = weight.shape[0]
    head_dim = width // HEADS
    quarter = head_dim // 2
    src = iota((width, width), 0)
    dst = iota((width, width), 1)
    within = dst % (width // 2)
    wanted = within // quarter * head_dim + dst // (width // 2) * quarter + within % quarter
    return mm(weight, jnp.where(src == wanted, 1.0, 0.0).astype(BF16)).astype(BF16)


def transposed(weight):
    return weight.astype(F32).T.astype(BF16)


def store_keys(normed, wk, pos, cos_ref, sin_ref, store, peak):
    tokens, width = normed.shape
    half = width // 2
    pieces = pos.shape[0]
    rows = tokens // pieces
    made = mm(normed, wk)
    for i in range(pieces):
        part = slice(i * rows, (i + 1) * rows)
        at = pl.ds(pl.multiple_of(pos[i], rows), rows)
        c, s = cos_ref[at, :], sin_ref[at, :]
        u, w = made[part, :half], made[part, half:]
        u, w = u * c - w * s, u * s + w * c
        store(part, u.astype(BF16), w.astype(BF16))
        top = jnp.concatenate([u, w], axis=1)
        top = jnp.max(jnp.abs(top).reshape(rows // 8, 8, width), axis=0)
        peak = top if peak is None else jnp.maximum(peak, top)
    return peak


def store_values(normed, wv_t, store):
    made = mm_t(wv_t, normed).astype(BF16)
    for j in range(made.shape[1] // BLOCK):
        store(j, made[:, j * BLOCK : (j + 1) * BLOCK])


def own_kernel(scale, pos, n_ref, wq_ref, wk_ref, wv_ref, cos_ref, sin_ref, cos_t_ref, sin_t_ref, *refs):
    q_ref, k_ref, v_ref, top_ref = refs
    normed = n_ref[0]
    tokens, width = normed.shape
    half = width // 2
    pieces = pos.shape[0]
    rows = tokens // pieces

    def put_value(j, value):
        v_ref[0, j] = value

    def put_key(part, u, w):
        k_ref[0, part, :half] = u
        k_ref[0, part, half:] = w

    store_values(normed, transposed(wv_ref[...]), put_value)
    peak = store_keys(normed, ordered(wk_ref[...]), pos, cos_ref, sin_ref, put_key, None)
    made = mm_t(transposed(ordered(wq_ref[...])), normed) * scale
    squares = None
    for i in range(pieces):
        at = pl.ds(pl.multiple_of(pos[i], rows), rows)
        c, s = cos_t_ref[:, at], sin_t_ref[:, at]
        u, w = made[:half, i * rows : (i + 1) * rows], made[half:, i * rows : (i + 1) * rows]
        u, w = u * c - w * s, u * s + w * c
        for j in range(rows // BLOCK):
            part = slice(j * BLOCK, (j + 1) * BLOCK)
            q_ref[0, i * rows // BLOCK + j, :half, :] = u[:, part].astype(BF16)
            q_ref[0, i * rows // BLOCK + j, half:, :] = w[:, part].astype(BF16)
            both = u[:, part] * u[:, part] + w[:, part] * w[:, part]
            both = both.reshape(HEADS, half // HEADS, BLOCK)
            top = jnp.sum(both, axis=1)
            squares = top if squares is None else jnp.maximum(squares, top)
    top_ref[0, :8, :] = peak
    top_ref[0, 8:, :half] = squares
    top_ref[0, 8:, half:] = squares


def own_stage(normed, pos, wq, wk, wv, tables):
    _, tokens, width = normed.shape
    scale = LOG2E / float(np.sqrt(width // HEADS))
    full = pl.BlockSpec((width, width), lambda f, *_: (0, 0))
    table = [pl.BlockSpec(t.shape, lambda f, *_: (0, 0)) for t in tables]
    shapes = [(1, tokens // BLOCK, width, BLOCK), (1, tokens, width), (1, tokens // BLOCK, width, BLOCK), (1, 16, width)]
    types = [BF16, BF16, BF16, F32]
    return pl.pallas_call(
        functools.partial(own_kernel, scale),
        grid_spec=pltpu.PrefetchScalarGridSpec(
            num_scalar_prefetch=1,
            grid=(1,),
            in_specs=[pl.BlockSpec((1, tokens, width), lambda f, *_: (0, 0, 0)), full, full, full, *table],
            out_specs=[pl.BlockSpec(x, lambda f, *_, n=len(x): (0,) * n) for x in shapes],
        ),
        out_shape=[jax.ShapeDtypeStruct(x, t) for x, t in zip(shapes, types)],
        compiler_params=pltpu.CompilerParams(vmem_limit_bytes=48 << 20),
        cost_estimate=cost(3),
        name="own_rows",
    )(pos, normed, wq, wk, wv, *tables)


def space_kernel(places, frame, has_prev, ids, pos, wk_ref, wv_ref, wo_ref, cos_ref, sin_ref, top_ref, *refs):
    pieces = len(places)
    x_refs, n_refs = refs[:pieces], refs[pieces : pieces + 2]
    q_ref, ko_ref, vo_ref = refs[pieces + 2 : pieces + 5]
    refs = refs[pieces + 5 + (1 if has_prev else 0) :]
    o_ref, x_s, n_s, q_s, k_s, v_s, o_s, kg0, kg1, vg0, vg1, qm0, qm1, p0, p1, sem, out_sem = refs
    tokens, width = x_s.shape
    blocks = tokens // BLOCK
    piece_rows = tokens // pieces
    half = width // 2
    head_dim = width // HEADS
    quarter = head_dim // 2
    wide = NEIGHBOUR_COUNT * BLOCK

    copies = [
        (n_refs[0].at[0], n_s.at[0]),
        (n_refs[1].at[0], n_s.at[1]),
        (ko_ref.at[0], k_s.at[pl.ds(0, tokens)]),
        (q_ref.at[0], q_s),
        (vo_ref.at[0], v_s.at[pl.ds(0, blocks)]),
    ]
    copies += [
        (x_refs[i].at[places[i]], x_s.at[pl.ds(i * piece_rows, piece_rows)]) for i in range(pieces)
    ]
    copies = [pltpu.make_async_copy(src, dst, sem.at[i]) for i, (src, dst) in enumerate(copies)]
    for copy in copies:
        copy.start()

    wk, wv_t = ordered(wk_ref[...]), transposed(wv_ref[...])
    pairs = HEADS // 2
    sums = slice(2 * head_dim, 2 * head_dim + 16)
    for vg in (vg0, vg1):
        for h in range(pairs):
            vg[h, sums, :] = jnp.ones((16, wide), BF16)
    peak = top_ref[0, :8, :]
    for side in range(2):
        copies[side].wait()
        normed = n_s[side]

        def put_value(j, value, low=(side + 1) * blocks):
            v_s[low + j] = value

        def put_key(part, u, w, low=(side + 1) * tokens):
            rows = slice(low + part.start, low + part.stop)
            k_s[rows, :half] = u
            k_s[rows, half:] = w

        store_values(normed, wv_t, put_value)
        peak = store_keys(normed, wk, pos, cos_ref, sin_ref, put_key, peak)
    head_row = iota((HEADS, width), 0)
    head_lane = iota((HEADS, width), 1) % half // quarter
    peak = jnp.max(peak, axis=0, keepdims=True)
    k_bound = jnp.sum(jnp.where(head_row == head_lane, peak * peak, 0.0), axis=1, keepdims=True)
    bound = jnp.max(k_bound * top_ref[0, 8:, :])
    for copy in copies[2:]:
        copy.wait()

    head_of = iota((width, 1), 0) % half // quarter

    def entry(block, m):
        return ids[block * (NEIGHBOUR_COUNT + 2) + m]

    def scores(block, kg, qm, p, shift):
        for m in range(NEIGHBOUR_COUNT):
            at = pl.ds(pl.multiple_of(entry(block, m) * BLOCK, BLOCK), BLOCK)
            kg[m * BLOCK : (m + 1) * BLOCK, :] = k_s[at, :]
        q = q_s[entry(block, NEIGHBOUR_COUNT + 1)]
        for h in range(HEADS):
            qm[:, h * BLOCK : (h + 1) * BLOCK] = jnp.where(head_of == h, q, 0).astype(BF16)
        s = mm(kg[...], qm[...])
        if shift:
            s = s - jnp.max(s, axis=0, keepdims=True)
        p[...] = jnp.exp2(s).astype(BF16)

    def values(block, vg, p):
        present = jnp.where(entry(block, NEIGHBOUR_COUNT) > 0, 1.0, 0.0).astype(BF16)
        last = slice(wide - BLOCK, wide)
        for m in range(NEIGHBOUR_COUNT):
            value = v_s[entry(block, m)]
            if m == NEIGHBOUR_COUNT - 1:
                value = value * present
            for h in range(pairs):
                vg[h, : 2 * head_dim, m * BLOCK : (m + 1) * BLOCK] = value[2 * h * head_dim : 2 * (h + 1) * head_dim]
        parts = []
        for h in range(pairs):
            vg[h, sums, last] = jnp.ones((16, BLOCK), BF16) * present
            o = mm(vg[h], p[:, 2 * h * BLOCK : 2 * (h + 1) * BLOCK])
            d = o[2 * head_dim : 2 * head_dim + 1]
            parts.append(o[:head_dim, :BLOCK] / d[:, :BLOCK])
            parts.append(o[head_dim : 2 * head_dim, BLOCK:] / d[:, BLOCK:])
        attended = jnp.concatenate(parts, axis=0).T.astype(BF16)
        own = pl.ds(pl.multiple_of(entry(block, NEIGHBOUR_COUNT + 1) * BLOCK, BLOCK), BLOCK)
        o_s[block] = (x_s[own, :].astype(F32) + mm(attended, wo_ref[...])).astype(BF16)
        send(block).start()

    def send(block):
        at = pl.ds(pl.multiple_of(block * BLOCK, BLOCK), BLOCK)
        return pltpu.make_async_copy(o_s.at[block], o_ref.at[frame, at], out_sem.at[block])

    safe = bound <= SAFE_SCORE * SAFE_SCORE

    @pl.when(safe)
    def _():
        slots = [(kg0, qm0, p0, vg0), (kg1, qm1, p1, vg1)]
        for block in range(blocks + 1):
            if block < blocks:
                kg, qm, p, _ = slots[block % 2]
                scores(block, kg, qm, p, False)
            if block > 0:
                _, _, p, vg = slots[(block - 1) % 2]
                values(block - 1, vg, p)

    @pl.when(jnp.logical_not(safe))
    def _():
        def step(block, _):
            scores(block, kg0, qm0, p0, True)
            values(block, vg0, p0)
            return 0

        lax.fori_loop(0, blocks, step, 0)

    for block in range(blocks):
        send(block).wait()


def norm_kernel(pieces, gain_ref, *refs):
    rows = refs[0].shape[1]
    for i in range(pieces):
        refs[pieces][:, i * rows : (i + 1) * rows, :] = rms_rows(refs[i][...].astype(F32), gain_ref[...])


def piece_specs(own):
    return [pl.BlockSpec((1,) + p.shape[1:], lambda f, *_, at=at: (at, 0, 0)) for p, at in own]


def norm_stage(own, gain):
    rows, width = own[0][0].shape[1:]
    shape = (1, rows * len(own), width)
    return pl.pallas_call(
        functools.partial(norm_kernel, len(own)),
        grid=(1,),
        in_specs=[pl.BlockSpec((1, width), lambda f: (0, 0))] + piece_specs(own),
        out_specs=pl.BlockSpec(shape, lambda f: (0, 0, 0)),
        out_shape=jax.ShapeDtypeStruct(shape, BF16),
        compiler_params=pltpu.CompilerParams(vmem_limit_bytes=48 << 20),
        cost_estimate=cost(2),
        name="norm_join",
    )(gain, *[p for p, _ in own])


def space_stage(own, normed, made, ids, pos, wk, wv, wo, tables, prev, frame, frames):
    pieces = len(own)
    piece_rows, width = own[0][0].shape[1:]
    tokens = pieces * piece_rows
    blocks = tokens // BLOCK
    wide = NEIGHBOUR_COUNT * BLOCK
    sum_rows = 2 * (width // HEADS) + 16
    full = pl.BlockSpec((width, width), lambda f, *_: (0, 0))
    table = [pl.BlockSpec(t.shape, lambda f, *_: (0, 0)) for t in tables]
    top = pl.BlockSpec(made[3].shape, lambda f, *_: (0, 0, 0))
    args = [wk, wv, wo, *tables, made[3], *[p for p, _ in own], *normed, *made[:3]]
    aliases = {}
    if prev is not None:
        aliases = {2 + len(args): 0}
        args.append(prev)
    in_specs = [full] * 3 + table + [top]
    in_specs += [pl.BlockSpec(memory_space=pl.ANY)] * (len(args) - len(in_specs))
    spec = pltpu.PrefetchScalarGridSpec(
        num_scalar_prefetch=2,
        grid=(1,),
        in_specs=in_specs,
        out_specs=pl.BlockSpec(memory_space=pl.ANY),
        scratch_shapes=[
            pltpu.VMEM((tokens, width), BF16),
            pltpu.VMEM((2, tokens, width), BF16),
            pltpu.VMEM((blocks, width, BLOCK), BF16),
            pltpu.VMEM((3 * tokens, width), BF16),
            pltpu.VMEM((3 * blocks, width, BLOCK), BF16),
            pltpu.VMEM((blocks, BLOCK, width), BF16),
        ]
        + [pltpu.VMEM((wide, width), BF16)] * 2
        + [pltpu.VMEM((HEADS // 2, sum_rows, wide), BF16)] * 2
        + [pltpu.VMEM((width, HEADS * BLOCK), BF16)] * 2
        + [pltpu.VMEM((wide, HEADS * BLOCK), BF16)] * 2
        + [pltpu.SemaphoreType.DMA((5 + pieces,)), pltpu.SemaphoreType.DMA((blocks,))],
    )
    return pl.pallas_call(
        functools.partial(space_kernel, [at for _, at in own], frame, prev is not None),
        grid_spec=spec,
        out_shape=jax.ShapeDtypeStruct((frames, tokens, width), BF16),
        input_output_aliases=aliases,
        compiler_params=pltpu.CompilerParams(vmem_limit_bytes=56 << 20),
        cost_estimate=cost(14),
        name="space_attention",
    )(ids, pos, *args)


def rotary_tables(tokens, width):
    half = width // HEADS // 2
    freqs = np.power(10000.0, -np.arange(half, dtype=np.float64) / half)
    angle = (np.arange(tokens) % ROT_PERIOD)[:, None] * freqs[None, :]
    by_rows = [np.tile(f(angle).astype(np.float32), (1, HEADS)) for f in (np.cos, np.sin)]
    return [jnp.asarray(t) for t in by_rows] + [jnp.asarray(np.ascontiguousarray(t.T)) for t in by_rows]


def after(value, *earlier):
    return lax.optimization_barrier((value, *earlier))[0]


def body(
    state_tokens,
    gain_time,
    query_time,
    key_time,
    value_time,
    output_time,
    gain_space,
    query_space,
    key_space,
    value_space,
    output_space,
    neighbours,
):
    frames_here, tokens_here, width = state_tokens.shape
    frame_count = lax.axis_size("frame")
    tile_count = lax.axis_size("tile")
    me = lax.axis_index("frame")
    tile = lax.axis_index("tile")
    rows = tokens_here // frame_count
    parts = 2 if rows % (2 * BLOCK) == 0 else 1
    part_rows = rows // parts

    def swap(value, k):
        return value if k == 0 else lax.ppermute(value, "frame", [(i, i ^ k) for i in range(frame_count)])

    last_cut = [1] * frames_here if frames_here < 3 else [1, 1, frames_here - 2]
    held = []
    pieces = []
    for part in range(parts):
        source = after(state_tokens, pieces[1]) if part else state_tokens
        pieces = []
        for k in range(frame_count):
            low = (me ^ k) * rows + part * part_rows
            pieces.append(swap(lax.dynamic_slice_in_dim(source, low, part_rows, axis=1), k))
        cut = last_cut if part == parts - 1 else [frames_here]
        outs = time_stage(
            pieces, cut, gain_time.reshape(1, width), query_time, key_time, value_time, output_time
        )
        back = [[] for _ in range(frame_count)]
        for c in range(len(cut)):
            first = [b[c - 1] for b in back[1:]] if c else []
            for k in range(frame_count):
                out = outs[k * len(cut) + c]
                back[k].append(swap(after(out, *first) if k and c else out, k))
        held.append((cut, back))

    def frame_pieces(frame):
        own = []
        for k in range(frame_count):
            for cut, back in held:
                low = 0
                for c, step in enumerate(cut):
                    if low <= frame < low + step:
                        own.append((back[k][c], frame - low))
                    low += step
        return own

    pairs = [(i, i ^ 1) for i in range(tile_count)]
    onward = [(i, (i + 2) % tile_count if i % 2 == 0 else (i - 2) % tile_count) for i in range(tile_count)]
    split = part_rows % BLOCK == 0
    places = me ^ jnp.arange(frame_count, dtype=jnp.int32)
    if split:
        pos = (places[:, None] * rows + jnp.arange(parts, dtype=jnp.int32) * part_rows).reshape(-1)
    else:
        pos = jnp.zeros((1,), jnp.int32)
    tables = rotary_tables(tokens_here, width)
    owns, nears, mades = [], [], []
    for frame in range(frames_here):
        own = frame_pieces(frame)
        if not split:
            stacked = jnp.stack([p[at] for p, at in own])[places]
            own = [(stacked.reshape(1, tokens_here, width), 0)]
        normed = norm_stage(own, gain_space.reshape(1, width))
        owns.append(own)
        nears.append(lax.ppermute(after(normed, nears[-1]) if frame else normed, "tile", pairs))
        mades.append(own_stage(normed, pos, query_space, key_space, value_space, tables))

    blocks = tokens_here // BLOCK
    total = blocks * tile_count
    even = tile % 2 == 0
    offset = (neighbours - (tile - 1) * blocks) % total
    side_of = offset // blocks
    side_at = jnp.where(side_of == 1, 0, jnp.where((side_of == 2) == even, 1, 2))
    inner = offset % blocks
    own_inner = jnp.arange(blocks, dtype=jnp.int32)
    if split:
        per = rows // BLOCK
        inner = ((inner // per) ^ me) * per + inner % per
        own_inner = ((own_inner // per) ^ me) * per + own_inner % per
    present = neighbours >= 0
    ids = jnp.where(present, side_at * blocks + inner, own_inner[:, None])
    ids = jnp.concatenate(
        [ids, present[:, -1:].astype(jnp.int32), own_inner[:, None]], axis=1
    ).reshape(-1)
    result = None
    far = lax.ppermute(nears[0], "tile", onward)
    for frame in range(frames_here):
        later = None
        near = nears[frame]
        if frame + 1 < frames_here:
            if result is None:
                near, nears[frame + 1] = lax.optimization_barrier((near, nears[frame + 1]))
            else:
                near, nears[frame + 1], result = lax.optimization_barrier((near, nears[frame + 1], result))
            later = lax.ppermute(nears[frame + 1], "tile", onward)
        result = space_stage(
            owns[frame], (near, far), mades[frame], ids, pos, key_space, value_space, output_space,
            tables[:2], result, frame, frames_here,
        )
        far = later
    return result


def solution(mesh):
    rows = P("frame", "tile", None)
    return jax.shard_map(
        body,
        mesh=mesh,
        in_specs=(rows,) + (P(),) * 10 + (P("tile", None),),
        out_specs=rows,
        check_vma=False,
    )
```

```python
import functools

import jax
import jax.numpy as jnp
import numpy as np
from jax import lax
from jax.experimental import pallas as pl
from jax.experimental.pallas import tpu as pltpu
from jax.sharding import PartitionSpec as P

HEADS = 8
BLOCK = 128
NEIGHBOUR_COUNT = 9
EPS = 1e-05
ROT_PERIOD = 1024
LOG2E = 1.4426950408889634
SAFE_SCORE = 90.0
TIME_UNROLL = 4
BF16 = jnp.bfloat16
F32 = jnp.float32


def rms_rows(x, gain):
    square_mean = jnp.mean(x * x, axis=-1, keepdims=True)
    return (x * lax.rsqrt(square_mean + EPS) * gain).astype(BF16)


def mm(a, b):
    return jnp.dot(a, b, preferred_element_type=F32)


def mm_t(a, b):
    return lax.dot_general(a, b, (((1,), (1,)), ((), ())), preferred_element_type=F32)


def iota(shape, dim):
    return lax.broadcasted_iota(jnp.int32, shape, dim)


def two_halves(rows):
    half = rows.shape[1] // 2
    zero = jnp.zeros((rows.shape[0], half), rows.dtype)
    first = jnp.concatenate([rows[:, :half], zero], axis=1)
    second = jnp.concatenate([zero, rows[:, half:]], axis=1)
    return jnp.concatenate([first, second], axis=0)


def head_squares(rows, one_head):
    return jnp.max(mm((rows * rows).astype(BF16), one_head), axis=0, keepdims=True)


def cost(us):
    return pl.CostEstimate(flops=int(us * 900e6), transcendentals=0, bytes_accessed=int(us * 1e6))


def time_kernel(scale, pieces, splits, gain_ref, wq_ref, wk_ref, wv_ref, wo_ref, *refs):
    x_refs = refs[:pieces]
    o_refs = refs[pieces : pieces + pieces * len(splits)]
    q_s, k_s, v_s, a_s = refs[pieces + pieces * len(splits) :]
    tokens, width = x_refs[0].shape[1:]
    head_dim = width // HEADS
    frames = q_s.shape[0]
    x = jnp.concatenate([r[...].astype(F32) for r in x_refs], axis=0)
    normed = rms_rows(x, gain_ref[...]).reshape(frames * tokens, width)
    q = mm(normed, wq_ref[...]) * scale
    k = mm(normed, wk_ref[...])
    q_s[...] = q.reshape(frames, tokens, width)
    k_s[...] = k.reshape(frames, tokens, width)
    v_s[...] = mm(normed, wv_ref[...]).reshape(frames, tokens, width)
    half = width // 2
    pairs = HEADS // 2
    one_head = jnp.where(
        iota((width, half), 0) // head_dim == iota((width, half), 1) // (half // HEADS), 1.0, 0.0
    ).astype(BF16)
    bound = jnp.max(head_squares(q, one_head) * head_squares(k, one_head))
    rows = frames * 8
    pair_of = (iota((1, width), 1) % half) // head_dim
    same = (iota((pairs * rows, 2 * rows), 0) % 8) == (iota((pairs * rows, 2 * rows), 1) % 8)
    ones = jnp.ones((rows, half), BF16)

    def attend(shift):
        def group(g, _):
            part = pl.ds(pl.multiple_of(g * 8, 8), 8)
            q = q_s[:, part, :].reshape(rows, width).astype(BF16)
            k = two_halves(k_s[:, part, :].reshape(rows, width).astype(BF16))
            v = two_halves(v_s[:, part, :].reshape(rows, width).astype(BF16))
            qm = jnp.concatenate([jnp.where(pair_of == h, q, 0).astype(BF16) for h in range(pairs)], axis=0)
            s = mm_t(qm, k)
            if shift:
                s = jnp.where(same, s, -1e30)
                tops = [jnp.max(s[:, i * rows : (i + 1) * rows], axis=1, keepdims=True) for i in range(2)]
                tops = [jnp.broadcast_to(t, (pairs * rows, rows)) for t in tops]
                s = s - jnp.concatenate(tops, axis=1)
            p = jnp.where(same, jnp.exp2(s), 0.0).astype(BF16)
            o = mm(p, v)
            d = mm(p, two_halves(jnp.concatenate([ones, ones], axis=1)))
            top, low = o[:rows], d[:rows]
            for h in range(1, pairs):
                top = jnp.where(pair_of == h, o[h * rows : (h + 1) * rows], top)
                low = jnp.where(pair_of == h, d[h * rows : (h + 1) * rows], low)
            a_s[:, part, :] = (top / low).reshape(frames, 8, width)
            return 0

        lax.fori_loop(0, tokens // 8, group, 0, unroll=TIME_UNROLL)

    safe = bound <= SAFE_SCORE * SAFE_SCORE

    @pl.when(safe)
    def _():
        attend(False)

    @pl.when(jnp.logical_not(safe))
    def _():
        attend(True)

    attended = a_s[...].reshape(frames * tokens, width).astype(BF16)
    middle = x + mm(attended, wo_ref[...]).reshape(frames, tokens, width)
    low = 0
    for i, o_ref in enumerate(o_refs):
        step = splits[i % len(splits)]
        o_ref[...] = middle[low : low + step].astype(BF16)
        low += step


def time_stage(pieces, splits, gain, wq, wk, wv, wo):
    frames_here, tokens, width = pieces[0].shape
    frames = frames_here * len(pieces)
    tile = min(tokens, 128)
    scale = LOG2E / float(np.sqrt(width // HEADS))
    full = pl.BlockSpec((width, width), lambda t: (0, 0))
    steps = list(splits) * len(pieces)
    return pl.pallas_call(
        functools.partial(time_kernel, scale, len(pieces), splits),
        grid=(tokens // tile,),
        in_specs=[pl.BlockSpec((1, width), lambda t: (0, 0))]
        + [full] * 4
        + [pl.BlockSpec((frames_here, tile, width), lambda t: (0, t, 0))] * len(pieces),
        out_specs=[pl.BlockSpec((step, tile, width), lambda t: (0, t, 0)) for step in steps],
        out_shape=[jax.ShapeDtypeStruct((step, tokens, width), BF16) for step in steps],
        scratch_shapes=[pltpu.VMEM((frames, tile, width), F32)] * 4,
        compiler_params=pltpu.CompilerParams(vmem_limit_bytes=48 << 20),
        cost_estimate=cost(8),
        name="time_attention",
    )(gain, wq, wk, wv, wo, *pieces)


def ordered(weight):
    width = weight.shape[0]
    head_dim = width // HEADS
    quarter = head_dim // 2
    src = iota((width, width), 0)
    dst = iota((width, width), 1)
    within = dst % (width // 2)
    wanted = within // quarter * head_dim + dst // (width // 2) * quarter + within % quarter
    return mm(weight, jnp.where(src == wanted, 1.0, 0.0).astype(BF16)).astype(BF16)


def transposed(weight):
    return weight.astype(F32).T.astype(BF16)


def weights_kernel(wq_ref, wk_ref, wv_ref, q_ref, k_ref, v_ref):
    q_ref[...] = transposed(ordered(wq_ref[...]))
    k_ref[...] = ordered(wk_ref[...])
    v_ref[...] = transposed(wv_ref[...])


def weights_stage(wq, wk, wv):
    return pl.pallas_call(
        weights_kernel,
        out_shape=[jax.ShapeDtypeStruct(wq.shape, BF16)] * 3,
        cost_estimate=cost(0.1),
        name="space_weights",
    )(wq, wk, wv)


def store_keys(normed, wk, starts, cos_ref, sin_ref, store, peak):
    tokens, width = normed.shape
    half = width // 2
    rows = tokens // len(starts)
    made = mm(normed, wk)
    for i, start in enumerate(starts):
        part = slice(i * rows, (i + 1) * rows)
        at = pl.ds(pl.multiple_of(start, rows), rows)
        c, s = cos_ref[at, :], sin_ref[at, :]
        u, w = made[part, :half], made[part, half:]
        u, w = u * c - w * s, u * s + w * c
        store(part, u.astype(BF16), w.astype(BF16))
        top = jnp.concatenate([u, w], axis=1)
        top = jnp.max(jnp.abs(top).reshape(rows // 8, 8, width), axis=0)
        peak = top if peak is None else jnp.maximum(peak, top)
    return peak


def store_values(normed, wv_t, store):
    made = mm_t(wv_t, normed).astype(BF16)
    for j in range(made.shape[1] // BLOCK):
        store(j, made[:, j * BLOCK : (j + 1) * BLOCK])


def own_kernel(scale, halves, pos, *refs):
    n_refs = refs[:halves]
    wq_ref, wk_ref, wv_ref, cos_ref, sin_ref, cos_t_ref, sin_t_ref, q_ref, k_ref, v_ref, top_ref = refs[halves:]
    tokens, width = n_refs[0].shape[1:]
    half = width // 2
    pieces = pos.shape[0] // halves
    rows = tokens // pieces
    peak, squares = None, None
    for n in range(halves):
        normed = n_refs[n][0]

        def put_value(j, value, low=n * tokens // BLOCK):
            v_ref[0, low + j] = value

        def put_key(part, u, w, low=n * tokens):
            at = slice(low + part.start, low + part.stop)
            k_ref[0, at, :half] = u
            k_ref[0, at, half:] = w

        starts = [pos[n * pieces + i] for i in range(pieces)]
        store_values(normed, wv_ref[...], put_value)
        peak = store_keys(normed, wk_ref[...], starts, cos_ref, sin_ref, put_key, peak)
        made = mm_t(wq_ref[...], normed) * scale
        for i in range(pieces):
            at = pl.ds(pl.multiple_of(starts[i], rows), rows)
            c, s = cos_t_ref[:, at], sin_t_ref[:, at]
            u, w = made[:half, i * rows : (i + 1) * rows], made[half:, i * rows : (i + 1) * rows]
            u, w = u * c - w * s, u * s + w * c
            for j in range(rows // BLOCK):
                part = slice(j * BLOCK, (j + 1) * BLOCK)
                block = (n * tokens + i * rows) // BLOCK + j
                q_ref[0, block, :half, :] = u[:, part].astype(BF16)
                q_ref[0, block, half:, :] = w[:, part].astype(BF16)
                both = u[:, part] * u[:, part] + w[:, part] * w[:, part]
                both = both.reshape(HEADS, half // HEADS, BLOCK)
                top = jnp.sum(both, axis=1)
                squares = top if squares is None else jnp.maximum(squares, top)
    top_ref[0, :8, :] = peak
    top_ref[0, 8:, :half] = squares
    top_ref[0, 8:, half:] = squares


def own_stage(normed, pos, wq, wk, wv, tables):
    part, width = normed[0].shape[1:]
    tokens = part * len(normed)
    scale = LOG2E / float(np.sqrt(width // HEADS))
    full = pl.BlockSpec((width, width), lambda f, *_: (0, 0))
    table = [pl.BlockSpec(t.shape, lambda f, *_: (0, 0)) for t in tables]
    shapes = [(1, tokens // BLOCK, width, BLOCK), (1, tokens, width), (1, tokens // BLOCK, width, BLOCK), (1, 16, width)]
    types = [BF16, BF16, BF16, F32]
    return pl.pallas_call(
        functools.partial(own_kernel, scale, len(normed)),
        grid_spec=pltpu.PrefetchScalarGridSpec(
            num_scalar_prefetch=1,
            grid=(1,),
            in_specs=[pl.BlockSpec((1, part, width), lambda f, *_: (0, 0, 0))] * len(normed) + [full] * 3 + table,
            out_specs=[pl.BlockSpec(x, lambda f, *_, n=len(x): (0,) * n) for x in shapes],
        ),
        out_shape=[jax.ShapeDtypeStruct(x, t) for x, t in zip(shapes, types)],
        compiler_params=pltpu.CompilerParams(vmem_limit_bytes=48 << 20),
        cost_estimate=cost(0.2),
        name="own_rows",
    )(pos, *normed, wq, wk, wv, *tables)


def space_kernel(places, halves, frame, has_prev, ids, pos, wk_ref, wv_ref, wo_ref, cos_ref, sin_ref, top_ref, *refs):
    pieces = len(places)
    far_at = pieces + 2 * halves
    x_refs, n_refs = refs[:pieces], refs[pieces:far_at]
    q_ref, ko_ref, vo_ref = refs[far_at : far_at + 3]
    refs = refs[far_at + 3 + (1 if has_prev else 0) :]
    o_ref, x_s, n_s, q_s, k_s, v_s, o_s, kg0, kg1, vg0, vg1, qm0, qm1, p0, p1, sem, out_sem = refs
    tokens, width = x_s.shape
    blocks = tokens // BLOCK
    piece_rows = tokens // pieces
    half = width // 2
    head_dim = width // HEADS
    quarter = head_dim // 2
    wide = NEIGHBOUR_COUNT * BLOCK

    part_rows = tokens // halves
    copies = [
        (n_refs[i].at[0], n_s.at[i // halves, pl.ds(i % halves * part_rows, part_rows)]) for i in range(2 * halves)
    ]
    copies += [
        (ko_ref.at[0], k_s.at[pl.ds(0, tokens)]),
        (q_ref.at[0], q_s),
        (vo_ref.at[0], v_s.at[pl.ds(0, blocks)]),
    ]
    copies += [
        (x_refs[i].at[places[i]], x_s.at[pl.ds(i * piece_rows, piece_rows)]) for i in range(pieces)
    ]
    copies = [pltpu.make_async_copy(src, dst, sem.at[i]) for i, (src, dst) in enumerate(copies)]
    for copy in copies:
        copy.start()

    wk, wv_t = wk_ref[...], wv_ref[...]
    pairs = HEADS // 2
    sums = slice(2 * head_dim, 2 * head_dim + 16)
    for vg in (vg0, vg1):
        for h in range(pairs):
            vg[h, sums, :] = jnp.ones((16, wide), BF16)
    peak = top_ref[0, :8, :]
    for side in range(2):
        for copy in copies[side * halves : (side + 1) * halves]:
            copy.wait()
        normed = n_s[side]

        def put_value(j, value, low=(side + 1) * blocks):
            v_s[low + j] = value

        def put_key(part, u, w, low=(side + 1) * tokens):
            rows = slice(low + part.start, low + part.stop)
            k_s[rows, :half] = u
            k_s[rows, half:] = w

        store_values(normed, wv_t, put_value)
        starts = [pos[i] for i in range(pos.shape[0])]
        peak = store_keys(normed, wk, starts, cos_ref, sin_ref, put_key, peak)
    head_row = iota((HEADS, width), 0)
    head_lane = iota((HEADS, width), 1) % half // quarter
    peak = jnp.max(peak, axis=0, keepdims=True)
    k_bound = jnp.sum(jnp.where(head_row == head_lane, peak * peak, 0.0), axis=1, keepdims=True)
    bound = jnp.max(k_bound * top_ref[0, 8:, :])
    for copy in copies[2 * halves :]:
        copy.wait()

    head_of = iota((width, 1), 0) % half // quarter

    def entry(block, m):
        return ids[block * (NEIGHBOUR_COUNT + 2) + m]

    def scores(block, kg, qm, p, shift):
        for m in range(NEIGHBOUR_COUNT):
            at = pl.ds(pl.multiple_of(entry(block, m) * BLOCK, BLOCK), BLOCK)
            kg[m * BLOCK : (m + 1) * BLOCK, :] = k_s[at, :]
        q = q_s[entry(block, NEIGHBOUR_COUNT + 1)]
        for h in range(HEADS):
            qm[:, h * BLOCK : (h + 1) * BLOCK] = jnp.where(head_of == h, q, 0).astype(BF16)
        s = mm(kg[...], qm[...])
        if shift:
            s = s - jnp.max(s, axis=0, keepdims=True)
        p[...] = jnp.exp2(s).astype(BF16)

    def values(block, vg, p):
        present = jnp.where(entry(block, NEIGHBOUR_COUNT) > 0, 1.0, 0.0).astype(BF16)
        last = slice(wide - BLOCK, wide)
        for m in range(NEIGHBOUR_COUNT):
            value = v_s[entry(block, m)]
            if m == NEIGHBOUR_COUNT - 1:
                value = value * present
            for h in range(pairs):
                vg[h, : 2 * head_dim, m * BLOCK : (m + 1) * BLOCK] = value[2 * h * head_dim : 2 * (h + 1) * head_dim]
        parts = []
        for h in range(pairs):
            vg[h, sums, last] = jnp.ones((16, BLOCK), BF16) * present
            o = mm(vg[h], p[:, 2 * h * BLOCK : 2 * (h + 1) * BLOCK])
            d = o[2 * head_dim : 2 * head_dim + 1]
            parts.append(o[:head_dim, :BLOCK] / d[:, :BLOCK])
            parts.append(o[head_dim : 2 * head_dim, BLOCK:] / d[:, BLOCK:])
        attended = jnp.concatenate(parts, axis=0).T.astype(BF16)
        own = pl.ds(pl.multiple_of(entry(block, NEIGHBOUR_COUNT + 1) * BLOCK, BLOCK), BLOCK)
        o_s[block] = (x_s[own, :].astype(F32) + mm(attended, wo_ref[...])).astype(BF16)
        send(block).start()

    def send(block):
        at = pl.ds(pl.multiple_of(block * BLOCK, BLOCK), BLOCK)
        return pltpu.make_async_copy(o_s.at[block], o_ref.at[frame, at], out_sem.at[block])

    safe = bound <= SAFE_SCORE * SAFE_SCORE

    @pl.when(safe)
    def _():
        slots = [(kg0, qm0, p0, vg0), (kg1, qm1, p1, vg1)]
        for block in range(blocks + 1):
            if block < blocks:
                kg, qm, p, _ = slots[block % 2]
                scores(block, kg, qm, p, False)
            if block > 0:
                _, _, p, vg = slots[(block - 1) % 2]
                values(block - 1, vg, p)

    @pl.when(jnp.logical_not(safe))
    def _():
        def step(block, _):
            scores(block, kg0, qm0, p0, True)
            values(block, vg0, p0)
            return 0

        lax.fori_loop(0, blocks, step, 0)

    for block in range(blocks):
        send(block).wait()


def norm_kernel(pieces, gain_ref, *refs):
    rows = refs[0].shape[1]
    for i in range(pieces):
        refs[pieces][:, i * rows : (i + 1) * rows, :] = rms_rows(refs[i][...].astype(F32), gain_ref[...])


def piece_specs(own):
    return [pl.BlockSpec((1,) + p.shape[1:], lambda f, *_, at=at: (at, 0, 0)) for p, at in own]


def norm_stage(own, gain):
    rows, width = own[0][0].shape[1:]
    shape = (1, rows * len(own), width)
    return pl.pallas_call(
        functools.partial(norm_kernel, len(own)),
        grid=(1,),
        in_specs=[pl.BlockSpec((1, width), lambda f: (0, 0))] + piece_specs(own),
        out_specs=pl.BlockSpec(shape, lambda f: (0, 0, 0)),
        out_shape=jax.ShapeDtypeStruct(shape, BF16),
        compiler_params=pltpu.CompilerParams(vmem_limit_bytes=48 << 20),
        cost_estimate=cost(0.1),
        name="norm_join",
    )(gain, *[p for p, _ in own])


def space_stage(own, normed, made, ids, pos, wk, wv, wo, tables, prev, frame, frames):
    pieces, halves = len(own), len(normed[0])
    piece_rows, width = own[0][0].shape[1:]
    tokens = pieces * piece_rows
    blocks = tokens // BLOCK
    wide = NEIGHBOUR_COUNT * BLOCK
    sum_rows = 2 * (width // HEADS) + 16
    full = pl.BlockSpec((width, width), lambda f, *_: (0, 0))
    table = [pl.BlockSpec(t.shape, lambda f, *_: (0, 0)) for t in tables]
    top = pl.BlockSpec(made[3].shape, lambda f, *_: (0, 0, 0))
    args = [wk, wv, wo, *tables, made[3], *[p for p, _ in own], *normed[0], *normed[1], *made[:3]]
    aliases = {}
    if prev is not None:
        aliases = {2 + len(args): 0}
        args.append(prev)
    in_specs = [full] * 3 + table + [top]
    in_specs += [pl.BlockSpec(memory_space=pltpu.HBM)] * (len(args) - len(in_specs))
    spec = pltpu.PrefetchScalarGridSpec(
        num_scalar_prefetch=2,
        grid=(1,),
        in_specs=in_specs,
        out_specs=pl.BlockSpec(memory_space=pltpu.HBM),
        scratch_shapes=[
            pltpu.VMEM((tokens, width), BF16),
            pltpu.VMEM((2, tokens, width), BF16),
            pltpu.VMEM((blocks, width, BLOCK), BF16),
            pltpu.VMEM((3 * tokens, width), BF16),
            pltpu.VMEM((3 * blocks, width, BLOCK), BF16),
            pltpu.VMEM((blocks, BLOCK, width), BF16),
        ]
        + [pltpu.VMEM((wide, width), BF16)] * 2
        + [pltpu.VMEM((HEADS // 2, sum_rows, wide), BF16)] * 2
        + [pltpu.VMEM((width, HEADS * BLOCK), BF16)] * 2
        + [pltpu.VMEM((wide, HEADS * BLOCK), BF16)] * 2
        + [pltpu.SemaphoreType.DMA((3 + 2 * halves + pieces,)), pltpu.SemaphoreType.DMA((blocks,))],
    )
    return pl.pallas_call(
        functools.partial(space_kernel, [at for _, at in own], halves, frame, prev is not None),
        grid_spec=spec,
        out_shape=jax.ShapeDtypeStruct((frames, tokens, width), BF16),
        input_output_aliases=aliases,
        compiler_params=pltpu.CompilerParams(vmem_limit_bytes=56 << 20),
        cost_estimate=cost(14),
        name="space_attention",
    )(ids, pos, *args)


def rotary_tables(tokens, width):
    half = width // HEADS // 2
    freqs = np.power(10000.0, -np.arange(half, dtype=np.float64) / half)
    angle = (np.arange(tokens) % ROT_PERIOD)[:, None] * freqs[None, :]
    by_rows = [np.tile(f(angle).astype(np.float32), (1, HEADS)) for f in (np.cos, np.sin)]
    return [jnp.asarray(t) for t in by_rows] + [jnp.asarray(np.ascontiguousarray(t.T)) for t in by_rows]


def after(value, *earlier):
    return lax.optimization_barrier((value, *earlier))[0]


def body(
    state_tokens,
    gain_time,
    query_time,
    key_time,
    value_time,
    output_time,
    gain_space,
    query_space,
    key_space,
    value_space,
    output_space,
    neighbours,
):
    frames_here, tokens_here, width = state_tokens.shape
    frame_count = lax.axis_size("frame")
    tile_count = lax.axis_size("tile")
    me = lax.axis_index("frame")
    tile = lax.axis_index("tile")
    rows = tokens_here // frame_count
    parts = 2 if rows % (2 * BLOCK) == 0 else 1
    part_rows = rows // parts

    def swap(value, k):
        return value if k == 0 else lax.ppermute(value, "frame", [(i, i ^ k) for i in range(frame_count)])

    last_cut = [1] * frames_here if frames_here < 3 else [1, 1, frames_here - 2]
    def give_back(one, c, earlier):
        cut, outs, back = one
        for k in range(frame_count):
            out = outs[k * len(cut) + c]
            back[k][c] = swap(after(out, *earlier) if k and earlier else out, k)

    held = []
    pieces = []
    for part in range(parts):
        source = after(state_tokens, pieces[1]) if part else state_tokens
        pieces = []
        for k in range(frame_count):
            low = (me ^ k) * rows + part * part_rows
            pieces.append(swap(lax.dynamic_slice_in_dim(source, low, part_rows, axis=1), k))
        cut = last_cut if part == parts - 1 else [frames_here]
        outs = time_stage(
            pieces, cut, gain_time.reshape(1, width), query_time, key_time, value_time, output_time
        )
        held.append((cut, outs, [[None] * len(cut) for _ in range(frame_count)]))
        if part < parts - 1:
            give_back(held[-1], 0, ())

    def frame_pieces(frame):
        own = []
        for k in range(frame_count):
            for cut, _, back in held:
                low = 0
                for c, step in enumerate(cut):
                    if low <= frame < low + step:
                        own.append((back[k][c], frame - low))
                    low += step
        return own

    pairs = [(i, i ^ 1) for i in range(tile_count)]
    onward = [(i, (i + 2) % tile_count if i % 2 == 0 else (i - 2) % tile_count) for i in range(tile_count)]
    split = part_rows % BLOCK == 0
    places = me ^ jnp.arange(frame_count, dtype=jnp.int32)
    if split:
        pos = (places[:, None] * rows + jnp.arange(parts, dtype=jnp.int32) * part_rows).reshape(-1)
    else:
        pos = jnp.zeros((1,), jnp.int32)
    tables = rotary_tables(tokens_here, width)
    wq, wk, wv = weights_stage(query_space, key_space, value_space)
    gain = gain_space.reshape(1, width)
    owns, nears, mades = [], [], []
    sent, normed = -1, ()
    for frame in range(frames_here):
        low = 0
        for c, step in enumerate(last_cut):
            if low <= frame < low + step and c > sent:
                give_back(held[-1], c, normed)
                sent = c
            low += step
        own = frame_pieces(frame)
        if not split:
            stacked = jnp.stack([p[at] for p, at in own])[places]
            own = [(stacked.reshape(1, tokens_here, width), 0)]
        own_normed = [norm_stage(own, gain)]
        if frame == 0:
            normed = own_normed
        owns.append(own)
        earlier = nears[-1] if nears else ()
        nears.append([lax.ppermute(after(n, *earlier) if frame else n, "tile", pairs) for n in own_normed])
        mades.append(own_stage(own_normed, pos, wq, wk, wv, tables))

    blocks = tokens_here // BLOCK
    total = blocks * tile_count
    even = tile % 2 == 0
    offset = (neighbours - (tile - 1) * blocks) % total
    side_of = offset // blocks
    side_at = jnp.where(side_of == 1, 0, jnp.where((side_of == 2) == even, 1, 2))
    inner = offset % blocks
    own_inner = jnp.arange(blocks, dtype=jnp.int32)
    if split:
        per = rows // BLOCK
        inner = ((inner // per) ^ me) * per + inner % per
        own_inner = ((own_inner // per) ^ me) * per + own_inner % per
    present = neighbours >= 0
    ids = jnp.where(present, side_at * blocks + inner, own_inner[:, None])
    ids = jnp.concatenate(
        [ids, present[:, -1:].astype(jnp.int32), own_inner[:, None]], axis=1
    ).reshape(-1)
    result = None
    far = [lax.ppermute(n, "tile", onward) for n in nears[0]]
    for frame in range(frames_here):
        later = None
        near = nears[frame]
        if frame + 1 < frames_here:
            if result is None:
                near, nears[frame + 1] = lax.optimization_barrier((near, nears[frame + 1]))
            else:
                near, nears[frame + 1], result = lax.optimization_barrier((near, nears[frame + 1], result))
            later = [lax.ppermute(n, "tile", onward) for n in nears[frame + 1]]
        result = space_stage(
            owns[frame], (near, far), mades[frame], ids, pos, wk, wv, output_space,
            tables[:2], result, frame, frames_here,
        )
        far = later
    return result


def solution(mesh):
    rows = P("frame", "tile", None)
    return jax.shard_map(
        body,
        mesh=mesh,
        in_specs=(rows,) + (P(),) * 10 + (P("tile", None),),
        out_specs=rows,
        check_vma=False,
    )
```

```python
import functools

import jax
import jax.numpy as jnp
import numpy as np
from jax import lax
from jax.experimental import pallas as pl
from jax.experimental.pallas import tpu as pltpu
from jax.sharding import PartitionSpec as P

HEADS = 8
BLOCK = 128
NEIGHBOUR_COUNT = 9
EPS = 1e-05
ROT_PERIOD = 1024
LOG2E = 1.4426950408889634
SAFE_SCORE = 90.0
VMEM_LIMIT = 36 << 20
TIME_UNROLL = 4
BF16 = jnp.bfloat16
F32 = jnp.float32


def rms_rows(x, gain):
    square_mean = jnp.mean(x * x, axis=-1, keepdims=True)
    return (x * lax.rsqrt(square_mean + EPS) * gain).astype(BF16)


def mm(a, b):
    return jnp.dot(a, b, preferred_element_type=F32)


def mm_t(a, b):
    return lax.dot_general(a, b, (((1,), (1,)), ((), ())), preferred_element_type=F32)


def iota(shape, dim):
    return lax.broadcasted_iota(jnp.int32, shape, dim)


def two_halves(rows):
    half = rows.shape[1] // 2
    zero = jnp.zeros((rows.shape[0], half), rows.dtype)
    first = jnp.concatenate([rows[:, :half], zero], axis=1)
    second = jnp.concatenate([zero, rows[:, half:]], axis=1)
    return jnp.concatenate([first, second], axis=0)


def head_squares(rows, one_head):
    return jnp.max(mm((rows * rows).astype(BF16), one_head), axis=0, keepdims=True)


def cost(us):
    return pl.CostEstimate(flops=int(us * 900e6), transcendentals=0, bytes_accessed=int(us * 1e6))


def time_kernel(scale, pieces, splits, gain_ref, wq_ref, wk_ref, wv_ref, wo_ref, *refs):
    x_refs = refs[:pieces]
    o_refs = refs[pieces : pieces + pieces * len(splits)]
    q_s, k_s, v_s, a_s = refs[pieces + pieces * len(splits) :]
    tokens, width = x_refs[0].shape[1:]
    head_dim = width // HEADS
    frames = q_s.shape[0]
    x = jnp.concatenate([r[...].astype(F32) for r in x_refs], axis=0)
    normed = rms_rows(x, gain_ref[...]).reshape(frames * tokens, width)
    q = mm(normed, wq_ref[...]) * scale
    k = mm(normed, wk_ref[...])
    q_s[...] = q.reshape(frames, tokens, width)
    k_s[...] = k.reshape(frames, tokens, width)
    v_s[...] = mm(normed, wv_ref[...]).reshape(frames, tokens, width)
    half = width // 2
    pairs = HEADS // 2
    one_head = jnp.where(
        iota((width, half), 0) // head_dim == iota((width, half), 1) // (half // HEADS), 1.0, 0.0
    ).astype(BF16)
    bound = jnp.max(head_squares(q, one_head) * head_squares(k, one_head))
    rows = frames * 8
    pair_of = (iota((1, width), 1) % half) // head_dim
    same = (iota((pairs * rows, 2 * rows), 0) % 8) == (iota((pairs * rows, 2 * rows), 1) % 8)
    ones = jnp.ones((rows, half), BF16)

    def attend(shift):
        def group(g, _):
            part = pl.ds(pl.multiple_of(g * 8, 8), 8)
            q = q_s[:, part, :].reshape(rows, width).astype(BF16)
            k = two_halves(k_s[:, part, :].reshape(rows, width).astype(BF16))
            v = two_halves(v_s[:, part, :].reshape(rows, width).astype(BF16))
            qm = jnp.concatenate([jnp.where(pair_of == h, q, 0).astype(BF16) for h in range(pairs)], axis=0)
            s = mm_t(qm, k)
            if shift:
                s = jnp.where(same, s, -1e30)
                tops = [jnp.max(s[:, i * rows : (i + 1) * rows], axis=1, keepdims=True) for i in range(2)]
                tops = [jnp.broadcast_to(t, (pairs * rows, rows)) for t in tops]
                s = s - jnp.concatenate(tops, axis=1)
            p = jnp.where(same, jnp.exp2(s), 0.0).astype(BF16)
            o = mm(p, v)
            d = mm(p, two_halves(jnp.concatenate([ones, ones], axis=1)))
            top, low = o[:rows], d[:rows]
            for h in range(1, pairs):
                top = jnp.where(pair_of == h, o[h * rows : (h + 1) * rows], top)
                low = jnp.where(pair_of == h, d[h * rows : (h + 1) * rows], low)
            a_s[:, part, :] = (top / low).reshape(frames, 8, width)
            return 0

        lax.fori_loop(0, tokens // 8, group, 0, unroll=TIME_UNROLL)

    safe = bound <= SAFE_SCORE * SAFE_SCORE

    @pl.when(safe)
    def _():
        attend(False)

    @pl.when(jnp.logical_not(safe))
    def _():
        attend(True)

    attended = a_s[...].reshape(frames * tokens, width).astype(BF16)
    middle = x + mm(attended, wo_ref[...]).reshape(frames, tokens, width)
    low = 0
    for i, o_ref in enumerate(o_refs):
        step = splits[i % len(splits)]
        o_ref[...] = middle[low : low + step].astype(BF16)
        low += step


def time_stage(pieces, splits, gain, wq, wk, wv, wo):
    frames_here, tokens, width = pieces[0].shape
    frames = frames_here * len(pieces)
    scale = LOG2E / float(np.sqrt(width // HEADS))
    steps = list(splits) * len(pieces)
    return pl.pallas_call(
        functools.partial(time_kernel, scale, len(pieces), splits),
        out_shape=[jax.ShapeDtypeStruct((step, tokens, width), BF16) for step in steps],
        scratch_shapes=[pltpu.VMEM((frames, tokens, width), F32)] * 4,
        compiler_params=pltpu.CompilerParams(vmem_limit_bytes=VMEM_LIMIT),
        cost_estimate=cost(8),
        name="time_attention",
    )(gain, wq, wk, wv, wo, *pieces)


def ordered(weight):
    width = weight.shape[0]
    head_dim = width // HEADS
    quarter = head_dim // 2
    src = iota((width, width), 0)
    dst = iota((width, width), 1)
    within = dst % (width // 2)
    wanted = within // quarter * head_dim + dst // (width // 2) * quarter + within % quarter
    return mm(weight, jnp.where(src == wanted, 1.0, 0.0).astype(BF16)).astype(BF16)


def transposed(weight):
    return weight.astype(F32).T.astype(BF16)


def weights_kernel(wq_ref, wk_ref, wv_ref, q_ref, k_ref, v_ref):
    q_ref[...] = transposed(ordered(wq_ref[...]))
    k_ref[...] = ordered(wk_ref[...])
    v_ref[...] = transposed(wv_ref[...])


def weights_stage(wq, wk, wv):
    return pl.pallas_call(
        weights_kernel,
        out_shape=[jax.ShapeDtypeStruct(wq.shape, BF16)] * 3,
        cost_estimate=cost(1),
        name="space_weights",
    )(wq, wk, wv)


def store_keys(normed, wk, starts, cos_ref, sin_ref, store, peak):
    tokens, width = normed.shape
    half = width // 2
    rows = tokens // len(starts)
    made = mm(normed, wk)
    for i, start in enumerate(starts):
        part = slice(i * rows, (i + 1) * rows)
        at = pl.ds(pl.multiple_of(start, rows), rows)
        c, s = cos_ref[at, :], sin_ref[at, :]
        u, w = made[part, :half], made[part, half:]
        u, w = u * c - w * s, u * s + w * c
        store(part, u.astype(BF16), w.astype(BF16))
        top = jnp.concatenate([u, w], axis=1)
        top = jnp.max(jnp.abs(top).reshape(rows // 8, 8, width), axis=0)
        peak = top if peak is None else jnp.maximum(peak, top)
    return peak


def store_values(normed, wv_t, store):
    made = mm_t(wv_t, normed).astype(BF16)
    for j in range(made.shape[1] // BLOCK):
        store(j, made[:, j * BLOCK : (j + 1) * BLOCK])


def own_kernel(scale, halves, pos, *refs):
    n_refs = refs[:halves]
    wq_ref, wk_ref, wv_ref, cos_ref, sin_ref, cos_t_ref, sin_t_ref, q_ref, k_ref, v_ref, top_ref = refs[halves:]
    tokens, width = n_refs[0].shape[1:]
    half = width // 2
    pieces = pos.shape[0] // halves
    rows = tokens // pieces
    peak, squares = None, None
    for n in range(halves):
        normed = n_refs[n][0]

        def put_value(j, value, low=n * tokens // BLOCK):
            v_ref[0, low + j] = value

        def put_key(part, u, w, low=n * tokens):
            at = slice(low + part.start, low + part.stop)
            k_ref[0, at, :half] = u
            k_ref[0, at, half:] = w

        starts = [pos[n * pieces + i] for i in range(pieces)]
        store_values(normed, wv_ref[...], put_value)
        peak = store_keys(normed, wk_ref[...], starts, cos_ref, sin_ref, put_key, peak)
        made = mm_t(wq_ref[...], normed) * scale
        for i in range(pieces):
            at = pl.ds(pl.multiple_of(starts[i], rows), rows)
            c, s = cos_t_ref[:, at], sin_t_ref[:, at]
            u, w = made[:half, i * rows : (i + 1) * rows], made[half:, i * rows : (i + 1) * rows]
            u, w = u * c - w * s, u * s + w * c
            for j in range(rows // BLOCK):
                part = slice(j * BLOCK, (j + 1) * BLOCK)
                block = (n * tokens + i * rows) // BLOCK + j
                q_ref[0, block, :half, :] = u[:, part].astype(BF16)
                q_ref[0, block, half:, :] = w[:, part].astype(BF16)
                both = u[:, part] * u[:, part] + w[:, part] * w[:, part]
                both = both.reshape(HEADS, half // HEADS, BLOCK)
                top = jnp.sum(both, axis=1)
                squares = top if squares is None else jnp.maximum(squares, top)
    top_ref[0, :8, :] = peak
    top_ref[0, 8:, :half] = squares
    top_ref[0, 8:, half:] = squares


def own_stage(normed, pos, wq, wk, wv, tables):
    part, width = normed[0].shape[1:]
    tokens = part * len(normed)
    scale = LOG2E / float(np.sqrt(width // HEADS))
    shapes = [(1, tokens // BLOCK, width, BLOCK), (1, tokens, width), (1, tokens // BLOCK, width, BLOCK), (1, 16, width)]
    types = [BF16, BF16, BF16, F32]
    args = [*normed, wq, wk, wv, *tables]
    return pl.pallas_call(
        functools.partial(own_kernel, scale, len(normed)),
        in_specs=[pl.BlockSpec(memory_space=pltpu.SMEM)] + [pl.BlockSpec(memory_space=pltpu.VMEM)] * len(args),
        out_shape=[jax.ShapeDtypeStruct(x, t) for x, t in zip(shapes, types)],
        compiler_params=pltpu.CompilerParams(vmem_limit_bytes=VMEM_LIMIT),
        cost_estimate=cost(3),
        name="own_rows",
    )(pos, *args)


def space_kernel(places, halves, frame, has_prev, ids, pos, wk_ref, wv_ref, wo_ref, cos_ref, sin_ref, top_ref, *refs):
    pieces = len(places)
    far_at = pieces + 2 * halves
    x_refs, n_refs = refs[:pieces], refs[pieces:far_at]
    q_ref, ko_ref, vo_ref = refs[far_at : far_at + 3]
    refs = refs[far_at + 3 + (1 if has_prev else 0) :]
    o_ref, x_s, k_s, v_s, o_s, kg0, kg1, vg0, vg1, qm0, qm1, p0, p1, out_sem = refs
    tokens, width = x_s.shape
    blocks = tokens // BLOCK
    piece_rows = tokens // pieces
    half = width // 2
    head_dim = width // HEADS
    quarter = head_dim // 2
    wide = NEIGHBOUR_COUNT * BLOCK

    wk, wv_t = wk_ref[...], wv_ref[...]
    pairs = HEADS // 2
    sums = slice(2 * head_dim, 2 * head_dim + 16)
    for vg in (vg0, vg1):
        for h in range(pairs):
            vg[h, sums, :] = jnp.ones((16, wide), BF16)
    peak = top_ref[0, :8, :]
    for side in range(2):
        near = [n_refs[i][0] for i in range(side * halves, (side + 1) * halves)]
        normed = near[0] if halves == 1 else jnp.concatenate(near, axis=0)

        def put_value(j, value, low=(side + 1) * blocks):
            v_s[low + j] = value

        def put_key(part, u, w, low=(side + 1) * tokens):
            rows = slice(low + part.start, low + part.stop)
            k_s[rows, :half] = u
            k_s[rows, half:] = w

        store_values(normed, wv_t, put_value)
        starts = [pos[i] for i in range(pos.shape[0])]
        peak = store_keys(normed, wk, starts, cos_ref, sin_ref, put_key, peak)
    head_row = iota((HEADS, width), 0)
    head_lane = iota((HEADS, width), 1) % half // quarter
    peak = jnp.max(peak, axis=0, keepdims=True)
    k_bound = jnp.sum(jnp.where(head_row == head_lane, peak * peak, 0.0), axis=1, keepdims=True)
    bound = jnp.max(k_bound * top_ref[0, 8:, :])
    k_s[:tokens, :] = ko_ref[0]
    v_s[:blocks] = vo_ref[0]
    for i in range(pieces):
        x_s[i * piece_rows : (i + 1) * piece_rows, :] = x_refs[i][places[i]]

    head_of = iota((width, 1), 0) % half // quarter

    def entry(block, m):
        return ids[block * (NEIGHBOUR_COUNT + 2) + m]

    def scores(block, kg, qm, p, shift):
        for m in range(NEIGHBOUR_COUNT):
            at = pl.ds(pl.multiple_of(entry(block, m) * BLOCK, BLOCK), BLOCK)
            kg[m * BLOCK : (m + 1) * BLOCK, :] = k_s[at, :]
        q = q_ref[0, entry(block, NEIGHBOUR_COUNT + 1)]
        for h in range(HEADS):
            qm[:, h * BLOCK : (h + 1) * BLOCK] = jnp.where(head_of == h, q, 0).astype(BF16)
        s = mm(kg[...], qm[...])
        if shift:
            s = s - jnp.max(s, axis=0, keepdims=True)
        p[...] = jnp.exp2(s).astype(BF16)

    def values(block, vg, p):
        present = jnp.where(entry(block, NEIGHBOUR_COUNT) > 0, 1.0, 0.0).astype(BF16)
        last = slice(wide - BLOCK, wide)
        for m in range(NEIGHBOUR_COUNT):
            value = v_s[entry(block, m)]
            if m == NEIGHBOUR_COUNT - 1:
                value = value * present
            for h in range(pairs):
                vg[h, : 2 * head_dim, m * BLOCK : (m + 1) * BLOCK] = value[2 * h * head_dim : 2 * (h + 1) * head_dim]
        parts = []
        for h in range(pairs):
            vg[h, sums, last] = jnp.ones((16, BLOCK), BF16) * present
            o = mm(vg[h], p[:, 2 * h * BLOCK : 2 * (h + 1) * BLOCK])
            d = o[2 * head_dim : 2 * head_dim + 1]
            parts.append(o[:head_dim, :BLOCK] / d[:, :BLOCK])
            parts.append(o[head_dim : 2 * head_dim, BLOCK:] / d[:, BLOCK:])
        attended = jnp.concatenate(parts, axis=0).T.astype(BF16)
        own = pl.ds(pl.multiple_of(entry(block, NEIGHBOUR_COUNT + 1) * BLOCK, BLOCK), BLOCK)
        o_s[block] = (x_s[own, :].astype(F32) + mm(attended, wo_ref[...])).astype(BF16)
        send(block).start()

    def send(block):
        at = pl.ds(pl.multiple_of(block * BLOCK, BLOCK), BLOCK)
        return pltpu.make_async_copy(o_s.at[block], o_ref.at[frame, at], out_sem.at[block])

    safe = bound <= SAFE_SCORE * SAFE_SCORE

    @pl.when(safe)
    def _():
        slots = [(kg0, qm0, p0, vg0), (kg1, qm1, p1, vg1)]
        for block in range(blocks + 1):
            if block < blocks:
                kg, qm, p, _ = slots[block % 2]
                scores(block, kg, qm, p, False)
            if block > 0:
                _, _, p, vg = slots[(block - 1) % 2]
                values(block - 1, vg, p)

    @pl.when(jnp.logical_not(safe))
    def _():
        def step(block, _):
            scores(block, kg0, qm0, p0, True)
            values(block, vg0, p0)
            return 0

        lax.fori_loop(0, blocks, step, 0)

    for block in range(blocks):
        send(block).wait()


def norm_kernel(places, gain_ref, *refs):
    rows = refs[0].shape[1]
    for i, at in enumerate(places):
        refs[-1][0, i * rows : (i + 1) * rows, :] = rms_rows(refs[i][at].astype(F32), gain_ref[...])


def norm_stage(own, gain):
    rows, width = own[0][0].shape[1:]
    return pl.pallas_call(
        functools.partial(norm_kernel, [at for _, at in own]),
        out_shape=jax.ShapeDtypeStruct((1, rows * len(own), width), BF16),
        compiler_params=pltpu.CompilerParams(vmem_limit_bytes=VMEM_LIMIT),
        cost_estimate=cost(2),
        name="norm_join",
    )(gain, *[p for p, _ in own])


def space_stage(own, normed, made, ids, pos, wk, wv, wo, tables, prev, frame, frames):
    pieces, halves = len(own), len(normed[0])
    piece_rows, width = own[0][0].shape[1:]
    tokens = pieces * piece_rows
    blocks = tokens // BLOCK
    wide = NEIGHBOUR_COUNT * BLOCK
    sum_rows = 2 * (width // HEADS) + 16
    args = [wk, wv, wo, *tables, made[3], *[p for p, _ in own], *normed[0], *normed[1], *made[:3]]
    in_specs = [pl.BlockSpec(memory_space=pltpu.SMEM)] * 2 + [pl.BlockSpec(memory_space=pltpu.VMEM)] * len(args)
    aliases = {}
    if prev is not None:
        aliases = {2 + len(args): 0}
        args.append(prev)
        in_specs.append(pl.BlockSpec(memory_space=pl.ANY))
    return pl.pallas_call(
        functools.partial(space_kernel, [at for _, at in own], halves, frame, prev is not None),
        in_specs=in_specs,
        out_specs=pl.BlockSpec(memory_space=pl.ANY),
        out_shape=jax.ShapeDtypeStruct((frames, tokens, width), BF16),
        scratch_shapes=[
            pltpu.VMEM((tokens, width), BF16),
            pltpu.VMEM((3 * tokens, width), BF16),
            pltpu.VMEM((3 * blocks, width, BLOCK), BF16),
            pltpu.VMEM((blocks, BLOCK, width), BF16),
        ]
        + [pltpu.VMEM((wide, width), BF16)] * 2
        + [pltpu.VMEM((HEADS // 2, sum_rows, wide), BF16)] * 2
        + [pltpu.VMEM((width, HEADS * BLOCK), BF16)] * 2
        + [pltpu.VMEM((wide, HEADS * BLOCK), BF16)] * 2
        + [pltpu.SemaphoreType.DMA((blocks,))],
        input_output_aliases=aliases,
        compiler_params=pltpu.CompilerParams(vmem_limit_bytes=VMEM_LIMIT),
        cost_estimate=cost(14),
        name="space_attention",
    )(ids, pos, *args)


def rotary_tables(tokens, width):
    half = width // HEADS // 2
    freqs = np.power(10000.0, -np.arange(half, dtype=np.float64) / half)
    angle = (np.arange(tokens) % ROT_PERIOD)[:, None] * freqs[None, :]
    by_rows = [np.tile(f(angle).astype(np.float32), (1, HEADS)) for f in (np.cos, np.sin)]
    return [jnp.asarray(t) for t in by_rows] + [jnp.asarray(np.ascontiguousarray(t.T)) for t in by_rows]


def after(value, *earlier):
    return lax.optimization_barrier((value, *earlier))[0]


def body(
    state_tokens,
    gain_time,
    query_time,
    key_time,
    value_time,
    output_time,
    gain_space,
    query_space,
    key_space,
    value_space,
    output_space,
    neighbours,
):
    frames_here, tokens_here, width = state_tokens.shape
    frame_count = lax.axis_size("frame")
    tile_count = lax.axis_size("tile")
    me = lax.axis_index("frame")
    tile = lax.axis_index("tile")
    rows = tokens_here // frame_count
    parts = 2 if rows % (2 * BLOCK) == 0 else 1
    part_rows = rows // parts

    def swap(value, k):
        return value if k == 0 else lax.ppermute(value, "frame", [(i, i ^ k) for i in range(frame_count)])

    last_cut = [1] * frames_here if frames_here < 3 else [1, 1, frames_here - 2]
    wq, wk, wv = weights_stage(query_space, key_space, value_space)

    def give_back(one, c, earlier):
        cut, outs, back = one
        for k in range(frame_count):
            out = outs[k * len(cut) + c]
            back[k][c] = swap(after(out, *earlier) if k and earlier else out, k)

    held = []
    pieces = []
    for part in range(parts):
        source = after(state_tokens, pieces[1]) if part else state_tokens
        pieces = []
        for k in range(frame_count):
            low = (me ^ k) * rows + part * part_rows
            pieces.append(swap(lax.dynamic_slice_in_dim(source, low, part_rows, axis=1), k))
        if part == 0:
            pieces[0] = after(pieces[0], wq, wk, wv)
        cut = last_cut if part == parts - 1 else [frames_here]
        outs = time_stage(
            pieces, cut, gain_time.reshape(1, width), query_time, key_time, value_time, output_time
        )
        held.append((cut, outs, [[None] * len(cut) for _ in range(frame_count)]))
        if part < parts - 1:
            give_back(held[-1], 0, ())

    def frame_pieces(frame):
        own = []
        for k in range(frame_count):
            for cut, _, back in held:
                low = 0
                for c, step in enumerate(cut):
                    if low <= frame < low + step:
                        own.append((back[k][c], frame - low))
                    low += step
        return own

    pairs = [(i, i ^ 1) for i in range(tile_count)]
    onward = [(i, (i + 2) % tile_count if i % 2 == 0 else (i - 2) % tile_count) for i in range(tile_count)]
    split = part_rows % BLOCK == 0
    places = me ^ jnp.arange(frame_count, dtype=jnp.int32)
    if split:
        pos = (places[:, None] * rows + jnp.arange(parts, dtype=jnp.int32) * part_rows).reshape(-1)
    else:
        pos = jnp.zeros((1,), jnp.int32)
    tables = rotary_tables(tokens_here, width)
    gain = gain_space.reshape(1, width)
    owns, nears, mades = [], [], []
    sent, normed = -1, ()
    for frame in range(frames_here):
        low = 0
        for c, step in enumerate(last_cut):
            if low <= frame < low + step and c > sent:
                give_back(held[-1], c, normed)
                sent = c
            low += step
        own = frame_pieces(frame)
        if not split:
            stacked = jnp.stack([p[at] for p, at in own])[places]
            own = [(stacked.reshape(1, tokens_here, width), 0)]
        own_normed = [norm_stage(own, gain)]
        if frame == 0:
            normed = own_normed
        owns.append(own)
        earlier = nears[-1] if nears else ()
        nears.append([lax.ppermute(after(n, *earlier) if frame else n, "tile", pairs) for n in own_normed])
        mades.append(own_stage(own_normed, pos, wq, wk, wv, tables))

    blocks = tokens_here // BLOCK
    total = blocks * tile_count
    even = tile % 2 == 0
    offset = (neighbours - (tile - 1) * blocks) % total
    side_of = offset // blocks
    side_at = jnp.where(side_of == 1, 0, jnp.where((side_of == 2) == even, 1, 2))
    inner = offset % blocks
    own_inner = jnp.arange(blocks, dtype=jnp.int32)
    if split:
        per = rows // BLOCK
        inner = ((inner // per) ^ me) * per + inner % per
        own_inner = ((own_inner // per) ^ me) * per + own_inner % per
    present = neighbours >= 0
    ids = jnp.where(present, side_at * blocks + inner, own_inner[:, None])
    ids = jnp.concatenate(
        [ids, present[:, -1:].astype(jnp.int32), own_inner[:, None]], axis=1
    ).reshape(-1)
    result = None
    far = [lax.ppermute(n, "tile", onward) for n in nears[0]]
    for frame in range(frames_here):
        later = None
        near = nears[frame]
        if frame + 1 < frames_here:
            if result is None:
                near, nears[frame + 1] = lax.optimization_barrier((near, nears[frame + 1]))
            else:
                near, nears[frame + 1], result = lax.optimization_barrier((near, nears[frame + 1], result))
            later = [lax.ppermute(n, "tile", onward) for n in nears[frame + 1]]
        result = space_stage(
            owns[frame], (near, far), mades[frame], ids, pos, wk, wv, output_space,
            tables[:2], result, frame, frames_here,
        )
        far = later
    return result


def solution(mesh):
    rows = P("frame", "tile", None)
    return jax.shard_map(
        body,
        mesh=mesh,
        in_specs=(rows,) + (P(),) * 10 + (P("tile", None),),
        out_specs=rows,
        check_vma=False,
    )
```

```python
import functools

import jax
import jax.numpy as jnp
import numpy as np
from jax import lax
from jax.experimental import pallas as pl
from jax.experimental.pallas import tpu as pltpu
from jax.sharding import PartitionSpec as P

HEADS = 8
BLOCK = 128
NEIGHBOUR_COUNT = 9
EPS = 1e-05
ROT_PERIOD = 1024
LOG2E = 1.4426950408889634
SAFE_SCORE = 90.0
VMEM_LIMIT = 36 << 20
TIME_UNROLL = 8
BF16 = jnp.bfloat16
F32 = jnp.float32


def rms_rows(x, gain):
    square_mean = jnp.mean(x * x, axis=-1, keepdims=True)
    return (x * lax.rsqrt(square_mean + EPS) * gain).astype(BF16)


def mm(a, b):
    return jnp.dot(a, b, preferred_element_type=F32)


def mm_t(a, b):
    return lax.dot_general(a, b, (((1,), (1,)), ((), ())), preferred_element_type=F32)


def iota(shape, dim):
    return lax.broadcasted_iota(jnp.int32, shape, dim)


def two_halves(rows):
    half = rows.shape[1] // 2
    zero = jnp.zeros((rows.shape[0], half), rows.dtype)
    first = jnp.concatenate([rows[:, :half], zero], axis=1)
    second = jnp.concatenate([zero, rows[:, half:]], axis=1)
    return jnp.concatenate([first, second], axis=0)


def cost(us):
    return pl.CostEstimate(flops=int(us * 900e6), transcendentals=0, bytes_accessed=int(us * 1e6))


def time_kernel(scale, pieces, splits, gain_ref, wq_ref, wk_ref, wv_ref, wo_ref, *refs):
    x_refs = refs[:pieces]
    o_refs = refs[pieces : pieces + pieces * len(splits)]
    x_s, n_s, q_s, k_s, v_s = refs[pieces + pieces * len(splits) :]
    frames, tokens, width = x_s.shape
    frames_here = frames // pieces
    head_dim = width // HEADS
    half = width // 2
    pairs = HEADS // 2
    groups = tokens // 8
    rows = frames * 8
    for i in range(pieces):
        x_s[i * frames_here : (i + 1) * frames_here] = x_refs[i][...].astype(F32)
    for g in range(groups):
        x = x_s[:, g * 8 : g * 8 + 8, :].reshape(rows, width)
        n_s[g * rows : (g + 1) * rows, :] = rms_rows(x, gain_ref[...])
    normed = n_s[...]
    k = mm(normed, wk_ref[...])
    k_s[...] = k.astype(BF16)
    q = mm_t(transposed(wq_ref[...]), normed) * scale
    q_s[...] = q.astype(BF16)
    v_s[...] = mm_t(transposed(wv_ref[...]), normed).astype(BF16)
    squares = jnp.sum((q * q).reshape(HEADS, head_dim, groups * rows), axis=1)
    peak = jnp.max(jnp.abs(k).reshape(groups * rows // 8, 8, width), axis=0)
    peak = jnp.max(peak, axis=0, keepdims=True)
    mine = iota((HEADS, width), 0) == iota((HEADS, width), 1) // head_dim
    k_bound = jnp.sum(jnp.where(mine, peak * peak, 0.0), axis=1, keepdims=True)
    bound = jnp.max(k_bound * jnp.max(squares, axis=1, keepdims=True))

    pair_of = iota((width, 1), 0) % half // head_dim
    same = (iota((2 * rows, pairs * rows), 0) % 8) == (iota((2 * rows, pairs * rows), 1) % 8)
    blank = jnp.zeros((2 * head_dim, rows), BF16)
    ones, zeros = jnp.ones((16, rows), BF16), jnp.zeros((16, rows), BF16)
    sums = jnp.concatenate([jnp.concatenate([ones, zeros], axis=1), jnp.concatenate([zeros, ones], axis=1)], axis=0)

    def attend(shift, unroll):
        def group(g, _):
            at = pl.ds(pl.multiple_of(g * rows, rows), rows)
            q, k, v = q_s[:, at], k_s[at, :], v_s[:, at]
            qm = jnp.concatenate([jnp.where(pair_of == h, q, 0).astype(BF16) for h in range(pairs)], axis=1)
            s = mm(two_halves(k), qm)
            if shift:
                s = jnp.where(same, s, -1e30)
                tops = [jnp.max(s[i * rows : (i + 1) * rows], axis=0, keepdims=True) for i in range(2)]
                s = jnp.concatenate([s[i * rows : (i + 1) * rows] - tops[i] for i in range(2)], axis=0)
            p = jnp.where(same, jnp.exp2(s), 0.0).astype(BF16)
            parts = [None] * HEADS
            for j in range(pairs // 2):
                low = 2 * j * head_dim
                first = jnp.concatenate([v[low : low + 2 * head_dim], blank], axis=1)
                second = jnp.concatenate([blank, v[half + low : half + low + 2 * head_dim]], axis=1)
                o = mm(jnp.concatenate([first, second, sums], axis=0), p[:, 2 * j * rows : 2 * (j + 1) * rows])
                for i in range(2):
                    d = o[4 * head_dim + 16 * i : 4 * head_dim + 16 * i + 1]
                    for h in range(2):
                        at_row = (2 * i + h) * head_dim
                        lanes = slice(h * rows, (h + 1) * rows)
                        parts[i * pairs + 2 * j + h] = o[at_row : at_row + head_dim, lanes] / d[:, lanes]
            n_s[at, :] = jnp.concatenate(parts, axis=0).T.astype(BF16)
            return 0

        lax.fori_loop(0, groups, group, 0, unroll=unroll)

    safe = bound <= SAFE_SCORE * SAFE_SCORE

    @pl.when(safe)
    def _():
        attend(False, TIME_UNROLL)

    @pl.when(jnp.logical_not(safe))
    def _():
        attend(True, 1)

    y = mm(n_s[...], wo_ref[...])
    for g in range(groups):
        part = slice(g * 8, g * 8 + 8)
        x_s[:, part, :] += y[g * rows : (g + 1) * rows].reshape(frames, 8, width)
    low = 0
    for i, o_ref in enumerate(o_refs):
        step = splits[i % len(splits)]
        o_ref[...] = x_s[low : low + step].astype(BF16)
        low += step


def time_stage(pieces, splits, gain, wq, wk, wv, wo):
    frames_here, tokens, width = pieces[0].shape
    frames = frames_here * len(pieces)
    scale = LOG2E / float(np.sqrt(width // HEADS))
    steps = list(splits) * len(pieces)
    return pl.pallas_call(
        functools.partial(time_kernel, scale, len(pieces), splits),
        out_shape=[jax.ShapeDtypeStruct((step, tokens, width), BF16) for step in steps],
        scratch_shapes=[
            pltpu.VMEM((frames, tokens, width), F32),
            pltpu.VMEM((frames * tokens, width), BF16),
            pltpu.VMEM((width, frames * tokens), BF16),
            pltpu.VMEM((frames * tokens, width), BF16),
            pltpu.VMEM((width, frames * tokens), BF16),
        ],
        compiler_params=pltpu.CompilerParams(vmem_limit_bytes=VMEM_LIMIT),
        cost_estimate=cost(8),
        name="time_attention",
    )(gain, wq, wk, wv, wo, *pieces)


def ordered(weight):
    width = weight.shape[0]
    head_dim = width // HEADS
    quarter = head_dim // 2
    src = iota((width, width), 0)
    dst = iota((width, width), 1)
    within = dst % (width // 2)
    wanted = within // quarter * head_dim + dst // (width // 2) * quarter + within % quarter
    return mm(weight, jnp.where(src == wanted, 1.0, 0.0).astype(BF16)).astype(BF16)


def transposed(weight):
    return weight.astype(F32).T.astype(BF16)


def weights_kernel(wq_ref, wk_ref, wv_ref, q_ref, k_ref, v_ref):
    q_ref[...] = transposed(ordered(wq_ref[...]))
    k_ref[...] = ordered(wk_ref[...])
    v_ref[...] = transposed(wv_ref[...])


def weights_stage(wq, wk, wv):
    return pl.pallas_call(
        weights_kernel,
        out_shape=[jax.ShapeDtypeStruct(wq.shape, BF16)] * 3,
        cost_estimate=cost(1),
        name="space_weights",
    )(wq, wk, wv)


def store_keys(normed, wk, starts, cos_ref, sin_ref, store, peak):
    tokens, width = normed.shape
    half = width // 2
    rows = tokens // len(starts)
    made = mm(normed, wk)
    for i, start in enumerate(starts):
        part = slice(i * rows, (i + 1) * rows)
        at = pl.ds(pl.multiple_of(start, rows), rows)
        c, s = cos_ref[at, :], sin_ref[at, :]
        u, w = made[part, :half], made[part, half:]
        u, w = u * c - w * s, u * s + w * c
        store(part, u.astype(BF16), w.astype(BF16))
        top = jnp.concatenate([u, w], axis=1)
        top = jnp.max(jnp.abs(top).reshape(rows // 8, 8, width), axis=0)
        peak = top if peak is None else jnp.maximum(peak, top)
    return peak


def store_values(normed, wv_t, store):
    made = mm_t(wv_t, normed).astype(BF16)
    for j in range(made.shape[1] // BLOCK):
        store(j, made[:, j * BLOCK : (j + 1) * BLOCK])


def own_kernel(scale, halves, pos, *refs):
    n_refs = refs[:halves]
    wq_ref, wk_ref, wv_ref, cos_ref, sin_ref, cos_t_ref, sin_t_ref, q_ref, k_ref, v_ref, top_ref = refs[halves:]
    tokens, width = n_refs[0].shape[1:]
    half = width // 2
    pieces = pos.shape[0] // halves
    rows = tokens // pieces
    peak, squares = None, None
    for n in range(halves):
        normed = n_refs[n][0]

        def put_value(j, value, low=n * tokens // BLOCK):
            v_ref[0, low + j] = value

        def put_key(part, u, w, low=n * tokens):
            at = slice(low + part.start, low + part.stop)
            k_ref[0, at, :half] = u
            k_ref[0, at, half:] = w

        starts = [pos[n * pieces + i] for i in range(pieces)]
        store_values(normed, wv_ref[...], put_value)
        peak = store_keys(normed, wk_ref[...], starts, cos_ref, sin_ref, put_key, peak)
        made = mm_t(wq_ref[...], normed) * scale
        for i in range(pieces):
            at = pl.ds(pl.multiple_of(starts[i], rows), rows)
            c, s = cos_t_ref[:, at], sin_t_ref[:, at]
            u, w = made[:half, i * rows : (i + 1) * rows], made[half:, i * rows : (i + 1) * rows]
            u, w = u * c - w * s, u * s + w * c
            for j in range(rows // BLOCK):
                part = slice(j * BLOCK, (j + 1) * BLOCK)
                block = (n * tokens + i * rows) // BLOCK + j
                q_ref[0, block, :half, :] = u[:, part].astype(BF16)
                q_ref[0, block, half:, :] = w[:, part].astype(BF16)
                both = u[:, part] * u[:, part] + w[:, part] * w[:, part]
                both = both.reshape(HEADS, half // HEADS, BLOCK)
                top = jnp.sum(both, axis=1)
                squares = top if squares is None else jnp.maximum(squares, top)
    top_ref[0, :8, :] = peak
    top_ref[0, 8:, :half] = squares
    top_ref[0, 8:, half:] = squares


def own_stage(normed, pos, wq, wk, wv, tables):
    part, width = normed[0].shape[1:]
    tokens = part * len(normed)
    scale = LOG2E / float(np.sqrt(width // HEADS))
    shapes = [(1, tokens // BLOCK, width, BLOCK), (1, tokens, width), (1, tokens // BLOCK, width, BLOCK), (1, 16, width)]
    types = [BF16, BF16, BF16, F32]
    args = [*normed, wq, wk, wv, *tables]
    return pl.pallas_call(
        functools.partial(own_kernel, scale, len(normed)),
        in_specs=[pl.BlockSpec(memory_space=pltpu.SMEM)] + [pl.BlockSpec(memory_space=pltpu.VMEM)] * len(args),
        out_shape=[jax.ShapeDtypeStruct(x, t) for x, t in zip(shapes, types)],
        compiler_params=pltpu.CompilerParams(vmem_limit_bytes=VMEM_LIMIT),
        cost_estimate=cost(3),
        name="own_rows",
    )(pos, *args)


def space_kernel(places, halves, frame, has_prev, ids, pos, wk_ref, wv_ref, wo_ref, cos_ref, sin_ref, top_ref, *refs):
    pieces = len(places)
    far_at = pieces + 2 * halves
    x_refs, n_refs = refs[:pieces], refs[pieces:far_at]
    q_ref, ko_ref, vo_ref = refs[far_at : far_at + 3]
    refs = refs[far_at + 3 + (1 if has_prev else 0) :]
    o_ref, x_s, k_s, v_s, o_s, kg0, kg1, vg0, vg1, qm0, qm1, p0, p1, out_sem = refs
    tokens, width = x_s.shape
    blocks = tokens // BLOCK
    piece_rows = tokens // pieces
    half = width // 2
    head_dim = width // HEADS
    quarter = head_dim // 2
    wide = NEIGHBOUR_COUNT * BLOCK

    wk, wv_t = wk_ref[...], wv_ref[...]
    pairs = HEADS // 2
    sums = slice(2 * head_dim, 2 * head_dim + 16)
    for vg in (vg0, vg1):
        for h in range(pairs):
            vg[h, sums, :] = jnp.ones((16, wide), BF16)
    peak = top_ref[0, :8, :]
    for side in range(2):
        near = [n_refs[i][0] for i in range(side * halves, (side + 1) * halves)]
        normed = near[0] if halves == 1 else jnp.concatenate(near, axis=0)

        def put_value(j, value, low=(side + 1) * blocks):
            v_s[low + j] = value

        def put_key(part, u, w, low=(side + 1) * tokens):
            rows = slice(low + part.start, low + part.stop)
            k_s[rows, :half] = u
            k_s[rows, half:] = w

        store_values(normed, wv_t, put_value)
        starts = [pos[i] for i in range(pos.shape[0])]
        peak = store_keys(normed, wk, starts, cos_ref, sin_ref, put_key, peak)
    head_row = iota((HEADS, width), 0)
    head_lane = iota((HEADS, width), 1) % half // quarter
    peak = jnp.max(peak, axis=0, keepdims=True)
    k_bound = jnp.sum(jnp.where(head_row == head_lane, peak * peak, 0.0), axis=1, keepdims=True)
    bound = jnp.max(k_bound * top_ref[0, 8:, :])
    k_s[:tokens, :] = ko_ref[0]
    v_s[:blocks] = vo_ref[0]
    for i in range(pieces):
        x_s[i * piece_rows : (i + 1) * piece_rows, :] = x_refs[i][places[i]]

    head_of = iota((width, 1), 0) % half // quarter

    def entry(block, m):
        return ids[block * (NEIGHBOUR_COUNT + 2) + m]

    def load(block, kg, qm):
        for m in range(NEIGHBOUR_COUNT):
            at = pl.ds(pl.multiple_of(entry(block, m) * BLOCK, BLOCK), BLOCK)
            kg[m * BLOCK : (m + 1) * BLOCK, :] = k_s[at, :]
        q = q_ref[0, entry(block, NEIGHBOUR_COUNT + 1)]
        for h in range(HEADS):
            qm[:, h * BLOCK : (h + 1) * BLOCK] = jnp.where(head_of == h, q, 0).astype(BF16)

    def weights_of(h, kg, qm, p, shift):
        cols = slice(2 * h * BLOCK, 2 * (h + 1) * BLOCK)
        s = mm(kg[...], qm[:, cols])
        if shift:
            s = s - jnp.max(s, axis=0, keepdims=True)
        p[:, cols] = jnp.exp2(s).astype(BF16)

    def values(block, vg, p, between):
        present = jnp.where(entry(block, NEIGHBOUR_COUNT) > 0, 1.0, 0.0).astype(BF16)
        last = slice(wide - BLOCK, wide)
        for m in range(NEIGHBOUR_COUNT):
            value = v_s[entry(block, m)]
            if m == NEIGHBOUR_COUNT - 1:
                value = value * present
            for h in range(pairs):
                vg[h, : 2 * head_dim, m * BLOCK : (m + 1) * BLOCK] = value[2 * h * head_dim : 2 * (h + 1) * head_dim]
        parts = []
        for h in range(pairs):
            vg[h, sums, last] = jnp.ones((16, BLOCK), BF16) * present
            between(h)
            o = mm(vg[h], p[:, 2 * h * BLOCK : 2 * (h + 1) * BLOCK])
            d = o[2 * head_dim : 2 * head_dim + 1]
            parts.append(o[:head_dim, :BLOCK] / d[:, :BLOCK])
            parts.append(o[head_dim : 2 * head_dim, BLOCK:] / d[:, BLOCK:])
        attended = jnp.concatenate(parts, axis=0).T.astype(BF16)
        own = pl.ds(pl.multiple_of(entry(block, NEIGHBOUR_COUNT + 1) * BLOCK, BLOCK), BLOCK)
        o_s[block] = (x_s[own, :].astype(F32) + mm(attended, wo_ref[...])).astype(BF16)
        send(block).start()

    def send(block):
        at = pl.ds(pl.multiple_of(block * BLOCK, BLOCK), BLOCK)
        return pltpu.make_async_copy(o_s.at[block], o_ref.at[frame, at], out_sem.at[block])

    safe = bound <= SAFE_SCORE * SAFE_SCORE

    @pl.when(safe)
    def _():
        slots = [(kg0, qm0, p0, vg0), (kg1, qm1, p1, vg1)]
        for block in range(blocks + 1):

            def between(h, block=block):
                kg, qm, p, _ = slots[block % 2]
                if block < blocks:
                    weights_of(h, kg, qm, p, False)

            if block < blocks:
                load(block, *slots[block % 2][:2])
            if block > 0:
                _, _, p, vg = slots[(block - 1) % 2]
                values(block - 1, vg, p, between)
            else:
                for h in range(pairs):
                    between(h)

    @pl.when(jnp.logical_not(safe))
    def _():
        def step(block, _):
            load(block, kg0, qm0)
            for h in range(pairs):
                weights_of(h, kg0, qm0, p0, True)
            values(block, vg0, p0, lambda h: None)
            return 0

        lax.fori_loop(0, blocks, step, 0)

    for block in range(blocks):
        send(block).wait()


def norm_kernel(places, gain_ref, *refs):
    rows = refs[0].shape[1]
    for i, at in enumerate(places):
        refs[-1][0, i * rows : (i + 1) * rows, :] = rms_rows(refs[i][at].astype(F32), gain_ref[...])


def norm_stage(own, gain):
    rows, width = own[0][0].shape[1:]
    return pl.pallas_call(
        functools.partial(norm_kernel, [at for _, at in own]),
        out_shape=jax.ShapeDtypeStruct((1, rows * len(own), width), BF16),
        compiler_params=pltpu.CompilerParams(vmem_limit_bytes=VMEM_LIMIT),
        cost_estimate=cost(2),
        name="norm_join",
    )(gain, *[p for p, _ in own])


def space_stage(own, normed, made, ids, pos, wk, wv, wo, tables, prev, frame, frames):
    pieces, halves = len(own), len(normed[0])
    piece_rows, width = own[0][0].shape[1:]
    tokens = pieces * piece_rows
    blocks = tokens // BLOCK
    wide = NEIGHBOUR_COUNT * BLOCK
    sum_rows = 2 * (width // HEADS) + 16
    args = [wk, wv, wo, *tables, made[3], *[p for p, _ in own], *normed[0], *normed[1], *made[:3]]
    in_specs = [pl.BlockSpec(memory_space=pltpu.SMEM)] * 2 + [pl.BlockSpec(memory_space=pltpu.VMEM)] * len(args)
    aliases = {}
    if prev is not None:
        aliases = {2 + len(args): 0}
        args.append(prev)
        in_specs.append(pl.BlockSpec(memory_space=pl.ANY))
    return pl.pallas_call(
        functools.partial(space_kernel, [at for _, at in own], halves, frame, prev is not None),
        in_specs=in_specs,
        out_specs=pl.BlockSpec(memory_space=pl.ANY),
        out_shape=jax.ShapeDtypeStruct((frames, tokens, width), BF16),
        scratch_shapes=[
            pltpu.VMEM((tokens, width), BF16),
            pltpu.VMEM((3 * tokens, width), BF16),
            pltpu.VMEM((3 * blocks, width, BLOCK), BF16),
            pltpu.VMEM((blocks, BLOCK, width), BF16),
        ]
        + [pltpu.VMEM((wide, width), BF16)] * 2
        + [pltpu.VMEM((HEADS // 2, sum_rows, wide), BF16)] * 2
        + [pltpu.VMEM((width, HEADS * BLOCK), BF16)] * 2
        + [pltpu.VMEM((wide, HEADS * BLOCK), BF16)] * 2
        + [pltpu.SemaphoreType.DMA((blocks,))],
        input_output_aliases=aliases,
        compiler_params=pltpu.CompilerParams(vmem_limit_bytes=VMEM_LIMIT),
        cost_estimate=cost(14),
        name="space_attention",
    )(ids, pos, *args)


def rotary_tables(tokens, width):
    half = width // HEADS // 2
    freqs = np.power(10000.0, -np.arange(half, dtype=np.float64) / half)
    angle = (np.arange(tokens) % ROT_PERIOD)[:, None] * freqs[None, :]
    by_rows = [np.tile(f(angle).astype(np.float32), (1, HEADS)) for f in (np.cos, np.sin)]
    return [jnp.asarray(t) for t in by_rows] + [jnp.asarray(np.ascontiguousarray(t.T)) for t in by_rows]


def after(value, *earlier):
    return lax.optimization_barrier((value, *earlier))[0]


def body(
    state_tokens,
    gain_time,
    query_time,
    key_time,
    value_time,
    output_time,
    gain_space,
    query_space,
    key_space,
    value_space,
    output_space,
    neighbours,
):
    frames_here, tokens_here, width = state_tokens.shape
    frame_count = lax.axis_size("frame")
    tile_count = lax.axis_size("tile")
    me = lax.axis_index("frame")
    tile = lax.axis_index("tile")
    rows = tokens_here // frame_count
    parts = 2 if rows % (2 * BLOCK) == 0 else 1
    part_rows = rows // parts

    def swap(value, k):
        return value if k == 0 else lax.ppermute(value, "frame", [(i, i ^ k) for i in range(frame_count)])

    last_cut = [1] * frames_here if frames_here < 3 else [1, 1, frames_here - 2]
    wq, wk, wv = weights_stage(query_space, key_space, value_space)

    def give_back(one, c, earlier):
        cut, outs, back = one
        for k in range(frame_count):
            out = outs[k * len(cut) + c]
            back[k][c] = swap(after(out, *earlier) if k and earlier else out, k)

    held = []
    pieces = []
    for part in range(parts):
        source = after(state_tokens, pieces[1]) if part else state_tokens
        pieces = []
        for k in range(frame_count):
            low = (me ^ k) * rows + part * part_rows
            pieces.append(swap(lax.dynamic_slice_in_dim(source, low, part_rows, axis=1), k))
        if part == 0:
            pieces[0] = after(pieces[0], wq, wk, wv)
        cut = last_cut if part == parts - 1 else [frames_here]
        outs = time_stage(
            pieces, cut, gain_time.reshape(1, width), query_time, key_time, value_time, output_time
        )
        held.append((cut, outs, [[None] * len(cut) for _ in range(frame_count)]))
        if part < parts - 1:
            give_back(held[-1], 0, ())

    def frame_pieces(frame):
        own = []
        for k in range(frame_count):
            for cut, _, back in held:
                low = 0
                for c, step in enumerate(cut):
                    if low <= frame < low + step:
                        own.append((back[k][c], frame - low))
                    low += step
        return own

    pairs = [(i, i ^ 1) for i in range(tile_count)]
    onward = [(i, (i + 2) % tile_count if i % 2 == 0 else (i - 2) % tile_count) for i in range(tile_count)]
    split = part_rows % BLOCK == 0
    places = me ^ jnp.arange(frame_count, dtype=jnp.int32)
    if split:
        pos = (places[:, None] * rows + jnp.arange(parts, dtype=jnp.int32) * part_rows).reshape(-1)
    else:
        pos = jnp.zeros((1,), jnp.int32)
    tables = rotary_tables(tokens_here, width)
    gain = gain_space.reshape(1, width)
    owns, nears, mades = [], [], []
    sent, normed = -1, ()
    for frame in range(frames_here):
        low = 0
        for c, step in enumerate(last_cut):
            if low <= frame < low + step and c > sent:
                give_back(held[-1], c, normed)
                sent = c
            low += step
        own = frame_pieces(frame)
        if not split:
            stacked = jnp.stack([p[at] for p, at in own])[places]
            own = [(stacked.reshape(1, tokens_here, width), 0)]
        own_normed = [norm_stage(own, gain)]
        if frame == 0:
            normed = own_normed
        owns.append(own)
        earlier = nears[-1] if nears else ()
        nears.append([lax.ppermute(after(n, *earlier) if frame else n, "tile", pairs) for n in own_normed])
        mades.append(own_stage(own_normed, pos, wq, wk, wv, tables))

    blocks = tokens_here // BLOCK
    total = blocks * tile_count
    even = tile % 2 == 0
    offset = (neighbours - (tile - 1) * blocks) % total
    side_of = offset // blocks
    side_at = jnp.where(side_of == 1, 0, jnp.where((side_of == 2) == even, 1, 2))
    inner = offset % blocks
    own_inner = jnp.arange(blocks, dtype=jnp.int32)
    if split:
        per = rows // BLOCK
        inner = ((inner // per) ^ me) * per + inner % per
        own_inner = ((own_inner // per) ^ me) * per + own_inner % per
    present = neighbours >= 0
    ids = jnp.where(present, side_at * blocks + inner, own_inner[:, None])
    ids = jnp.concatenate(
        [ids, present[:, -1:].astype(jnp.int32), own_inner[:, None]], axis=1
    ).reshape(-1)
    result = None
    far = [lax.ppermute(n, "tile", onward) for n in nears[0]]
    for frame in range(frames_here):
        later = None
        near = nears[frame]
        if frame + 1 < frames_here:
            if result is None:
                near, nears[frame + 1] = lax.optimization_barrier((near, nears[frame + 1]))
            else:
                near, nears[frame + 1], result = lax.optimization_barrier((near, nears[frame + 1], result))
            later = [lax.ppermute(n, "tile", onward) for n in nears[frame + 1]]
        result = space_stage(
            owns[frame], (near, far), mades[frame], ids, pos, wk, wv, output_space,
            tables[:2], result, frame, frames_here,
        )
        far = later
    return result


def solution(mesh):
    rows = P("frame", "tile", None)
    return jax.shard_map(
        body,
        mesh=mesh,
        in_specs=(rows,) + (P(),) * 10 + (P("tile", None),),
        out_specs=rows,
        check_vma=False,
    )
```

```python
import functools

import jax
import jax.numpy as jnp
import numpy as np
from jax import lax
from jax.experimental import pallas as pl
from jax.experimental.pallas import tpu as pltpu
from jax.sharding import PartitionSpec as P

HEADS = 8
BLOCK = 128
NEIGHBOUR_COUNT = 9
EPS = 1e-05
ROT_PERIOD = 1024
LOG2E = 1.4426950408889634
SAFE_SCORE = 90.0
VMEM_LIMIT = 36 << 20
TIME_UNROLL = 8
BF16 = jnp.bfloat16
F32 = jnp.float32


def rms_rows(x, gain):
    square_mean = jnp.mean(x * x, axis=-1, keepdims=True)
    return (x * lax.rsqrt(square_mean + EPS) * gain).astype(BF16)


def mm(a, b):
    return jnp.dot(a, b, preferred_element_type=F32)


def mm_t(a, b):
    return lax.dot_general(a, b, (((1,), (1,)), ((), ())), preferred_element_type=F32)


def iota(shape, dim):
    return lax.broadcasted_iota(jnp.int32, shape, dim)


def two_halves(rows):
    half = rows.shape[1] // 2
    zero = jnp.zeros((rows.shape[0], half), rows.dtype)
    first = jnp.concatenate([rows[:, :half], zero], axis=1)
    second = jnp.concatenate([zero, rows[:, half:]], axis=1)
    return jnp.concatenate([first, second], axis=0)


def cost(us):
    return pl.CostEstimate(flops=int(us * 900e6), transcendentals=0, bytes_accessed=int(us * 1e6))


def time_kernel(scale, pieces, splits, gain_ref, wq_ref, wk_ref, wv_ref, wo_ref, *refs):
    x_refs = refs[:pieces]
    o_refs = refs[pieces : pieces + pieces * len(splits)]
    x_s, n_s, q_s, k_s, v_s = refs[pieces + pieces * len(splits) :]
    frames, tokens, width = x_s.shape
    frames_here = frames // pieces
    head_dim = width // HEADS
    half = width // 2
    pairs = HEADS // 2
    groups = tokens // 8
    rows = frames * 8
    for i in range(pieces):
        x_s[i * frames_here : (i + 1) * frames_here] = x_refs[i][...].astype(F32)
    for g in range(groups):
        x = x_s[:, g * 8 : g * 8 + 8, :].reshape(rows, width)
        n_s[g * rows : (g + 1) * rows, :] = rms_rows(x, gain_ref[...])
    normed = n_s[...]
    k = mm(normed, wk_ref[...])
    k_s[...] = k.astype(BF16)
    q = mm_t(transposed(wq_ref[...]), normed) * scale
    q_s[...] = q.astype(BF16)
    v_s[...] = mm_t(transposed(wv_ref[...]), normed).astype(BF16)
    squares = jnp.sum((q * q).reshape(HEADS, head_dim, groups * rows), axis=1)
    peak = jnp.max(jnp.abs(k).reshape(groups * rows // 8, 8, width), axis=0)
    peak = jnp.max(peak, axis=0, keepdims=True)
    mine = iota((HEADS, width), 0) == iota((HEADS, width), 1) // head_dim
    k_bound = jnp.sum(jnp.where(mine, peak * peak, 0.0), axis=1, keepdims=True)
    bound = jnp.max(k_bound * jnp.max(squares, axis=1, keepdims=True))

    pair_of = iota((width, 1), 0) % half // head_dim
    same = (iota((2 * rows, pairs * rows), 0) % 8) == (iota((2 * rows, pairs * rows), 1) % 8)
    blank = jnp.zeros((2 * head_dim, rows), BF16)
    ones, zeros = jnp.ones((16, rows), BF16), jnp.zeros((16, rows), BF16)
    sums = jnp.concatenate([jnp.concatenate([ones, zeros], axis=1), jnp.concatenate([zeros, ones], axis=1)], axis=0)

    def attend(shift, unroll):
        def group(g, _):
            at = pl.ds(pl.multiple_of(g * rows, rows), rows)
            q, k, v = q_s[:, at], k_s[at, :], v_s[:, at]
            qm = jnp.concatenate([jnp.where(pair_of == h, q, 0).astype(BF16) for h in range(pairs)], axis=1)
            s = mm(two_halves(k), qm)
            if shift:
                s = jnp.where(same, s, -1e30)
                tops = [jnp.max(s[i * rows : (i + 1) * rows], axis=0, keepdims=True) for i in range(2)]
                s = jnp.concatenate([s[i * rows : (i + 1) * rows] - tops[i] for i in range(2)], axis=0)
            p = jnp.where(same, jnp.exp2(s), 0.0).astype(BF16)
            parts = [None] * HEADS
            for j in range(pairs // 2):
                low = 2 * j * head_dim
                first = jnp.concatenate([v[low : low + 2 * head_dim], blank], axis=1)
                second = jnp.concatenate([blank, v[half + low : half + low + 2 * head_dim]], axis=1)
                o = mm(jnp.concatenate([first, second, sums], axis=0), p[:, 2 * j * rows : 2 * (j + 1) * rows])
                for i in range(2):
                    d = o[4 * head_dim + 16 * i : 4 * head_dim + 16 * i + 1]
                    for h in range(2):
                        at_row = (2 * i + h) * head_dim
                        lanes = slice(h * rows, (h + 1) * rows)
                        parts[i * pairs + 2 * j + h] = o[at_row : at_row + head_dim, lanes] / d[:, lanes]
            n_s[at, :] = jnp.concatenate(parts, axis=0).T.astype(BF16)
            return 0

        lax.fori_loop(0, groups, group, 0, unroll=unroll)

    safe = bound <= SAFE_SCORE * SAFE_SCORE

    @pl.when(safe)
    def _():
        attend(False, TIME_UNROLL)

    @pl.when(jnp.logical_not(safe))
    def _():
        attend(True, 1)

    y = mm(n_s[...], wo_ref[...])
    for g in range(groups):
        part = slice(g * 8, g * 8 + 8)
        x_s[:, part, :] += y[g * rows : (g + 1) * rows].reshape(frames, 8, width)
    low = 0
    for i, o_ref in enumerate(o_refs):
        step = splits[i % len(splits)]
        o_ref[...] = x_s[low : low + step].astype(BF16)
        low += step


def time_stage(pieces, splits, gain, wq, wk, wv, wo):
    frames_here, tokens, width = pieces[0].shape
    frames = frames_here * len(pieces)
    scale = LOG2E / float(np.sqrt(width // HEADS))
    steps = list(splits) * len(pieces)
    return pl.pallas_call(
        functools.partial(time_kernel, scale, len(pieces), splits),
        out_shape=[jax.ShapeDtypeStruct((step, tokens, width), BF16) for step in steps],
        scratch_shapes=[
            pltpu.VMEM((frames, tokens, width), F32),
            pltpu.VMEM((frames * tokens, width), BF16),
            pltpu.VMEM((width, frames * tokens), BF16),
            pltpu.VMEM((frames * tokens, width), BF16),
            pltpu.VMEM((width, frames * tokens), BF16),
        ],
        compiler_params=pltpu.CompilerParams(vmem_limit_bytes=VMEM_LIMIT),
        cost_estimate=cost(8),
        name="time_attention",
    )(gain, wq, wk, wv, wo, *pieces)


def ordered(weight):
    width = weight.shape[0]
    head_dim = width // HEADS
    quarter = head_dim // 2
    src = iota((width, width), 0)
    dst = iota((width, width), 1)
    within = dst % (width // 2)
    wanted = within // quarter * head_dim + dst // (width // 2) * quarter + within % quarter
    return mm(weight, jnp.where(src == wanted, 1.0, 0.0).astype(BF16)).astype(BF16)


def transposed(weight):
    return weight.astype(F32).T.astype(BF16)


def weights_kernel(wq_ref, wk_ref, wv_ref, q_ref, k_ref, v_ref):
    q_ref[...] = transposed(ordered(wq_ref[...]))
    k_ref[...] = ordered(wk_ref[...])
    v_ref[...] = transposed(wv_ref[...])


def weights_stage(wq, wk, wv):
    return pl.pallas_call(
        weights_kernel,
        out_shape=[jax.ShapeDtypeStruct(wq.shape, BF16)] * 3,
        cost_estimate=cost(1),
        name="space_weights",
    )(wq, wk, wv)


def store_keys(normed, wk, starts, cos_ref, sin_ref, store, peak):
    tokens, width = normed.shape
    half = width // 2
    rows = tokens // len(starts)
    made = mm(normed, wk)
    for i, start in enumerate(starts):
        part = slice(i * rows, (i + 1) * rows)
        at = pl.ds(pl.multiple_of(start, rows), rows)
        c, s = cos_ref[at, :], sin_ref[at, :]
        u, w = made[part, :half], made[part, half:]
        u, w = u * c - w * s, u * s + w * c
        store(part, u.astype(BF16), w.astype(BF16))
        top = jnp.concatenate([u, w], axis=1)
        top = jnp.max(jnp.abs(top).reshape(rows // 8, 8, width), axis=0)
        peak = top if peak is None else jnp.maximum(peak, top)
    return peak


def store_values(normed, wv_t, store):
    made = mm_t(wv_t, normed).astype(BF16)
    for j in range(made.shape[1] // BLOCK):
        store(j, made[:, j * BLOCK : (j + 1) * BLOCK])


def own_kernel(scale, halves, pos, *refs):
    n_refs = refs[:halves]
    wq_ref, wk_ref, wv_ref, cos_ref, sin_ref, cos_t_ref, sin_t_ref, q_ref, k_ref, v_ref, top_ref = refs[halves:]
    tokens, width = n_refs[0].shape[1:]
    half = width // 2
    pieces = pos.shape[0] // halves
    rows = tokens // pieces
    peak, squares = None, None
    for n in range(halves):
        normed = n_refs[n][0]

        def put_value(j, value, low=n * tokens // BLOCK):
            v_ref[0, low + j] = value

        def put_key(part, u, w, low=n * tokens):
            at = slice(low + part.start, low + part.stop)
            k_ref[0, at, :half] = u
            k_ref[0, at, half:] = w

        starts = [pos[n * pieces + i] for i in range(pieces)]
        store_values(normed, wv_ref[...], put_value)
        peak = store_keys(normed, wk_ref[...], starts, cos_ref, sin_ref, put_key, peak)
        made = mm_t(wq_ref[...], normed) * scale
        for i in range(pieces):
            at = pl.ds(pl.multiple_of(starts[i], rows), rows)
            c, s = cos_t_ref[:, at], sin_t_ref[:, at]
            u, w = made[:half, i * rows : (i + 1) * rows], made[half:, i * rows : (i + 1) * rows]
            u, w = u * c - w * s, u * s + w * c
            for j in range(rows // BLOCK):
                part = slice(j * BLOCK, (j + 1) * BLOCK)
                block = (n * tokens + i * rows) // BLOCK + j
                q_ref[0, block, :half, :] = u[:, part].astype(BF16)
                q_ref[0, block, half:, :] = w[:, part].astype(BF16)
                both = u[:, part] * u[:, part] + w[:, part] * w[:, part]
                both = both.reshape(HEADS, half // HEADS, BLOCK)
                top = jnp.sum(both, axis=1)
                squares = top if squares is None else jnp.maximum(squares, top)
    top_ref[0, :8, :] = peak
    top_ref[0, 8:, :half] = squares
    top_ref[0, 8:, half:] = squares


def own_stage(normed, pos, wq, wk, wv, tables):
    part, width = normed[0].shape[1:]
    tokens = part * len(normed)
    scale = LOG2E / float(np.sqrt(width // HEADS))
    shapes = [(1, tokens // BLOCK, width, BLOCK), (1, tokens, width), (1, tokens // BLOCK, width, BLOCK), (1, 16, width)]
    types = [BF16, BF16, BF16, F32]
    args = [*normed, wq, wk, wv, *tables]
    return pl.pallas_call(
        functools.partial(own_kernel, scale, len(normed)),
        in_specs=[pl.BlockSpec(memory_space=pltpu.SMEM)] + [pl.BlockSpec(memory_space=pltpu.VMEM)] * len(args),
        out_shape=[jax.ShapeDtypeStruct(x, t) for x, t in zip(shapes, types)],
        compiler_params=pltpu.CompilerParams(vmem_limit_bytes=VMEM_LIMIT),
        cost_estimate=cost(0.2),
        name="own_rows",
    )(pos, *args)


def space_kernel(places, halves, frame, has_prev, ids, pos, wk_ref, wv_ref, wo_ref, cos_ref, sin_ref, top_ref, *refs):
    pieces = len(places)
    far_at = pieces + 2 * halves
    x_refs, n_refs = refs[:pieces], refs[pieces:far_at]
    q_ref, ko_ref, vo_ref = refs[far_at : far_at + 3]
    refs = refs[far_at + 3 + (1 if has_prev else 0) :]
    o_ref, x_s, k_s, v_s, o_s, kg0, kg1, vg0, vg1, qm0, qm1, p0, p1, out_sem = refs
    tokens, width = x_s.shape
    blocks = tokens // BLOCK
    piece_rows = tokens // pieces
    half = width // 2
    head_dim = width // HEADS
    quarter = head_dim // 2
    wide = NEIGHBOUR_COUNT * BLOCK

    wk, wv_t = wk_ref[...], wv_ref[...]
    pairs = HEADS // 2
    sums = slice(2 * head_dim, 2 * head_dim + 16)
    for vg in (vg0, vg1):
        for h in range(pairs):
            vg[h, sums, :] = jnp.ones((16, wide), BF16)
    peak = top_ref[0, :8, :]
    for side in range(2):
        near = [n_refs[i][0] for i in range(side * halves, (side + 1) * halves)]
        normed = near[0] if halves == 1 else jnp.concatenate(near, axis=0)

        def put_value(j, value, low=(side + 1) * blocks):
            v_s[low + j] = value

        def put_key(part, u, w, low=(side + 1) * tokens):
            rows = slice(low + part.start, low + part.stop)
            k_s[rows, :half] = u
            k_s[rows, half:] = w

        store_values(normed, wv_t, put_value)
        starts = [pos[i] for i in range(pos.shape[0])]
        peak = store_keys(normed, wk, starts, cos_ref, sin_ref, put_key, peak)
    head_row = iota((HEADS, width), 0)
    head_lane = iota((HEADS, width), 1) % half // quarter
    peak = jnp.max(peak, axis=0, keepdims=True)
    k_bound = jnp.sum(jnp.where(head_row == head_lane, peak * peak, 0.0), axis=1, keepdims=True)
    bound = jnp.max(k_bound * top_ref[0, 8:, :])
    k_s[:tokens, :] = ko_ref[0]
    v_s[:blocks] = vo_ref[0]
    for i in range(pieces):
        x_s[i * piece_rows : (i + 1) * piece_rows, :] = x_refs[i][places[i]]

    head_of = iota((width, 1), 0) % half // quarter

    def entry(block, m):
        return ids[block * (NEIGHBOUR_COUNT + 2) + m]

    def load(block, kg, qm):
        for m in range(NEIGHBOUR_COUNT):
            at = pl.ds(pl.multiple_of(entry(block, m) * BLOCK, BLOCK), BLOCK)
            kg[m * BLOCK : (m + 1) * BLOCK, :] = k_s[at, :]
        q = q_ref[0, entry(block, NEIGHBOUR_COUNT + 1)]
        for h in range(HEADS):
            qm[:, h * BLOCK : (h + 1) * BLOCK] = jnp.where(head_of == h, q, 0).astype(BF16)

    def weights_of(h, kg, qm, p, shift):
        cols = slice(2 * h * BLOCK, 2 * (h + 1) * BLOCK)
        s = mm(kg[...], qm[:, cols])
        if shift:
            s = s - jnp.max(s, axis=0, keepdims=True)
        p[:, cols] = jnp.exp2(s).astype(BF16)

    def values(block, vg, p, between):
        present = jnp.where(entry(block, NEIGHBOUR_COUNT) > 0, 1.0, 0.0).astype(BF16)
        last = slice(wide - BLOCK, wide)
        for m in range(NEIGHBOUR_COUNT):
            value = v_s[entry(block, m)]
            if m == NEIGHBOUR_COUNT - 1:
                value = value * present
            for h in range(pairs):
                vg[h, : 2 * head_dim, m * BLOCK : (m + 1) * BLOCK] = value[2 * h * head_dim : 2 * (h + 1) * head_dim]
        parts = []
        for h in range(pairs):
            vg[h, sums, last] = jnp.ones((16, BLOCK), BF16) * present
            between(h)
            o = mm(vg[h], p[:, 2 * h * BLOCK : 2 * (h + 1) * BLOCK])
            d = o[2 * head_dim : 2 * head_dim + 1]
            parts.append(o[:head_dim, :BLOCK] / d[:, :BLOCK])
            parts.append(o[head_dim : 2 * head_dim, BLOCK:] / d[:, BLOCK:])
        attended = jnp.concatenate(parts, axis=0).T.astype(BF16)
        own = pl.ds(pl.multiple_of(entry(block, NEIGHBOUR_COUNT + 1) * BLOCK, BLOCK), BLOCK)
        o_s[block] = (x_s[own, :].astype(F32) + mm(attended, wo_ref[...])).astype(BF16)
        send(block).start()

    def send(block):
        at = pl.ds(pl.multiple_of(block * BLOCK, BLOCK), BLOCK)
        return pltpu.make_async_copy(o_s.at[block], o_ref.at[frame, at], out_sem.at[block])

    safe = bound <= SAFE_SCORE * SAFE_SCORE

    @pl.when(safe)
    def _():
        slots = [(kg0, qm0, p0, vg0), (kg1, qm1, p1, vg1)]
        for block in range(blocks + 1):

            def between(h, block=block):
                kg, qm, p, _ = slots[block % 2]
                if block < blocks:
                    weights_of(h, kg, qm, p, False)

            if block < blocks:
                load(block, *slots[block % 2][:2])
            if block > 0:
                _, _, p, vg = slots[(block - 1) % 2]
                values(block - 1, vg, p, between)
            else:
                for h in range(pairs):
                    between(h)

    @pl.when(jnp.logical_not(safe))
    def _():
        def step(block, _):
            load(block, kg0, qm0)
            for h in range(pairs):
                weights_of(h, kg0, qm0, p0, True)
            values(block, vg0, p0, lambda h: None)
            return 0

        lax.fori_loop(0, blocks, step, 0)

    for block in range(blocks):
        send(block).wait()


def norm_kernel(places, gain_ref, *refs):
    rows = refs[0].shape[1]
    for i, at in enumerate(places):
        refs[-1][0, i * rows : (i + 1) * rows, :] = rms_rows(refs[i][at].astype(F32), gain_ref[...])


def norm_stage(own, gain):
    rows, width = own[0][0].shape[1:]
    return pl.pallas_call(
        functools.partial(norm_kernel, [at for _, at in own]),
        out_shape=jax.ShapeDtypeStruct((1, rows * len(own), width), BF16),
        compiler_params=pltpu.CompilerParams(vmem_limit_bytes=VMEM_LIMIT),
        cost_estimate=cost(0.1),
        name="norm_join",
    )(gain, *[p for p, _ in own])


def space_stage(own, normed, made, ids, pos, wk, wv, wo, tables, prev, frame, frames):
    pieces, halves = len(own), len(normed[0])
    piece_rows, width = own[0][0].shape[1:]
    tokens = pieces * piece_rows
    blocks = tokens // BLOCK
    wide = NEIGHBOUR_COUNT * BLOCK
    sum_rows = 2 * (width // HEADS) + 16
    args = [wk, wv, wo, *tables, made[3], *[p for p, _ in own], *normed[0], *normed[1], *made[:3]]
    in_specs = [pl.BlockSpec(memory_space=pltpu.SMEM)] * 2 + [pl.BlockSpec(memory_space=pltpu.VMEM)] * len(args)
    aliases = {}
    if prev is not None:
        aliases = {2 + len(args): 0}
        args.append(prev)
        in_specs.append(pl.BlockSpec(memory_space=pl.ANY))
    return pl.pallas_call(
        functools.partial(space_kernel, [at for _, at in own], halves, frame, prev is not None),
        in_specs=in_specs,
        out_specs=pl.BlockSpec(memory_space=pl.ANY),
        out_shape=jax.ShapeDtypeStruct((frames, tokens, width), BF16),
        scratch_shapes=[
            pltpu.VMEM((tokens, width), BF16),
            pltpu.VMEM((3 * tokens, width), BF16),
            pltpu.VMEM((3 * blocks, width, BLOCK), BF16),
            pltpu.VMEM((blocks, BLOCK, width), BF16),
        ]
        + [pltpu.VMEM((wide, width), BF16)] * 2
        + [pltpu.VMEM((HEADS // 2, sum_rows, wide), BF16)] * 2
        + [pltpu.VMEM((width, HEADS * BLOCK), BF16)] * 2
        + [pltpu.VMEM((wide, HEADS * BLOCK), BF16)] * 2
        + [pltpu.SemaphoreType.DMA((blocks,))],
        input_output_aliases=aliases,
        compiler_params=pltpu.CompilerParams(vmem_limit_bytes=VMEM_LIMIT),
        cost_estimate=cost(14),
        name="space_attention",
    )(ids, pos, *args)


def rotary_tables(tokens, width):
    half = width // HEADS // 2
    freqs = np.power(10000.0, -np.arange(half, dtype=np.float64) / half)
    angle = (np.arange(tokens) % ROT_PERIOD)[:, None] * freqs[None, :]
    by_rows = [np.tile(f(angle).astype(np.float32), (1, HEADS)) for f in (np.cos, np.sin)]
    return [jnp.asarray(t) for t in by_rows] + [jnp.asarray(np.ascontiguousarray(t.T)) for t in by_rows]


def after(value, *earlier):
    return lax.optimization_barrier((value, *earlier))[0]


def body(
    state_tokens,
    gain_time,
    query_time,
    key_time,
    value_time,
    output_time,
    gain_space,
    query_space,
    key_space,
    value_space,
    output_space,
    neighbours,
):
    frames_here, tokens_here, width = state_tokens.shape
    frame_count = lax.axis_size("frame")
    tile_count = lax.axis_size("tile")
    me = lax.axis_index("frame")
    tile = lax.axis_index("tile")
    rows = tokens_here // frame_count
    parts = 2 if rows % (2 * BLOCK) == 0 else 1
    part_rows = rows // parts

    def swap(value, k):
        return value if k == 0 else lax.ppermute(value, "frame", [(i, i ^ k) for i in range(frame_count)])

    cut = [1] * frames_here if frames_here < 3 else [1, 1, frames_here - 2]
    wq, wk, wv = weights_stage(query_space, key_space, value_space)

    def give_back(one, c, earlier):
        cut, outs, back = one
        for k in range(frame_count):
            out = outs[k * len(cut) + c]
            back[k][c] = swap(after(out, *earlier) if k and earlier else out, k)

    held = []
    pieces = []
    for part in range(parts):
        source = after(state_tokens, pieces[1]) if part else state_tokens
        pieces = []
        for k in range(frame_count):
            low = (me ^ k) * rows + part * part_rows
            pieces.append(swap(lax.dynamic_slice_in_dim(source, low, part_rows, axis=1), k))
        if part == 0:
            pieces[0] = after(pieces[0], wq, wk, wv)
        outs = time_stage(
            pieces, cut, gain_time.reshape(1, width), query_time, key_time, value_time, output_time
        )
        held.append((cut, outs, [[None] * len(cut) for _ in range(frame_count)]))
        give_back(held[-1], 0, ())

    def frame_pieces(frame):
        own = []
        for k in range(frame_count):
            for cut, _, back in held:
                low = 0
                for c, step in enumerate(cut):
                    if low <= frame < low + step:
                        own.append((back[k][c], frame - low))
                    low += step
        return own

    pairs = [(i, i ^ 1) for i in range(tile_count)]
    onward = [(i, (i + 2) % tile_count if i % 2 == 0 else (i - 2) % tile_count) for i in range(tile_count)]
    split = part_rows % BLOCK == 0
    places = me ^ jnp.arange(frame_count, dtype=jnp.int32)
    if split:
        pos = (places[:, None] * rows + jnp.arange(parts, dtype=jnp.int32) * part_rows).reshape(-1)
    else:
        pos = jnp.zeros((1,), jnp.int32)
    tables = rotary_tables(tokens_here, width)
    gain = gain_space.reshape(1, width)
    owns, nears, mades = [], [], []
    sent, earlier = 0, ()
    for frame in range(frames_here):
        low = 0
        for c, step in enumerate(cut):
            if low <= frame < low + step and c > sent:
                for one in held:
                    give_back(one, c, earlier)
                earlier = (*earlier, *[back[1][c] for _, _, back in held])
                sent = c
            low += step
        own = frame_pieces(frame)
        if not split:
            stacked = jnp.stack([p[at] for p, at in own])[places]
            own = [(stacked.reshape(1, tokens_here, width), 0)]
        own_normed = [norm_stage(own, gain)]
        if frame == 0:
            earlier = tuple(own_normed)
        owns.append(own)
        before = nears[-1] if nears else ()
        nears.append([lax.ppermute(after(n, *before) if frame else n, "tile", pairs) for n in own_normed])
        mades.append(own_stage(own_normed, pos, wq, wk, wv, tables))

    blocks = tokens_here // BLOCK
    total = blocks * tile_count
    even = tile % 2 == 0
    offset = (neighbours - (tile - 1) * blocks) % total
    side_of = offset // blocks
    side_at = jnp.where(side_of == 1, 0, jnp.where((side_of == 2) == even, 1, 2))
    inner = offset % blocks
    own_inner = jnp.arange(blocks, dtype=jnp.int32)
    if split:
        per = rows // BLOCK
        inner = ((inner // per) ^ me) * per + inner % per
        own_inner = ((own_inner // per) ^ me) * per + own_inner % per
    present = neighbours >= 0
    ids = jnp.where(present, side_at * blocks + inner, own_inner[:, None])
    ids = jnp.concatenate(
        [ids, present[:, -1:].astype(jnp.int32), own_inner[:, None]], axis=1
    ).reshape(-1)
    result = None
    far = [lax.ppermute(n, "tile", onward) for n in nears[0]]
    for frame in range(frames_here):
        later = None
        near = nears[frame]
        if frame + 1 < frames_here:
            if result is None:
                near, nears[frame + 1] = lax.optimization_barrier((near, nears[frame + 1]))
            else:
                near, nears[frame + 1], result = lax.optimization_barrier((near, nears[frame + 1], result))
            later = [lax.ppermute(n, "tile", onward) for n in nears[frame + 1]]
        result = space_stage(
            owns[frame], (near, far), mades[frame], ids, pos, wk, wv, output_space,
            tables[:2], result, frame, frames_here,
        )
        far = later
    return result


def solution(mesh):
    rows = P("frame", "tile", None)
    return jax.shard_map(
        body,
        mesh=mesh,
        in_specs=(rows,) + (P(),) * 10 + (P("tile", None),),
        out_specs=rows,
        check_vma=False,
    )
```

```python
import functools

import jax
import jax.numpy as jnp
import numpy as np
from jax import lax
from jax.experimental import pallas as pl
from jax.experimental.pallas import tpu as pltpu
from jax.sharding import PartitionSpec as P

HEADS = 8
BLOCK = 128
NEIGHBOUR_COUNT = 9
EPS = 1e-05
ROT_PERIOD = 1024
LOG2E = 1.4426950408889634
SAFE_SCORE = 90.0
VMEM_LIMIT = 36 << 20
TIME_UNROLL = 8
BF16 = jnp.bfloat16
F32 = jnp.float32


def rms_rows(x, gain):
    square_mean = jnp.mean(x * x, axis=-1, keepdims=True)
    return (x * lax.rsqrt(square_mean + EPS) * gain).astype(BF16)


def mm(a, b):
    return jnp.dot(a, b, preferred_element_type=F32)


def mm_t(a, b):
    return lax.dot_general(a, b, (((1,), (1,)), ((), ())), preferred_element_type=F32)


def iota(shape, dim):
    return lax.broadcasted_iota(jnp.int32, shape, dim)


def two_halves(rows):
    half = rows.shape[1] // 2
    zero = jnp.zeros((rows.shape[0], half), rows.dtype)
    first = jnp.concatenate([rows[:, :half], zero], axis=1)
    second = jnp.concatenate([zero, rows[:, half:]], axis=1)
    return jnp.concatenate([first, second], axis=0)


def cost(us):
    return pl.CostEstimate(flops=int(us * 900e6), transcendentals=0, bytes_accessed=int(us * 1e6))


def time_kernel(scale, pieces, splits, gain_ref, wq_ref, wk_ref, wv_ref, wo_ref, *refs):
    x_refs = refs[:pieces]
    o_refs = refs[pieces : pieces + pieces * len(splits)]
    x_s, n_s, q_s, k_s, v_s = refs[pieces + pieces * len(splits) :]
    frames, tokens, width = x_s.shape
    frames_here = frames // pieces
    head_dim = width // HEADS
    half = width // 2
    pairs = HEADS // 2
    groups = tokens // 8
    rows = frames * 8
    for i in range(pieces):
        x_s[i * frames_here : (i + 1) * frames_here] = x_refs[i][...].astype(F32)
    for g in range(groups):
        x = x_s[:, g * 8 : g * 8 + 8, :].reshape(rows, width)
        n_s[g * rows : (g + 1) * rows, :] = rms_rows(x, gain_ref[...])
    normed = n_s[...]
    k = mm(normed, wk_ref[...])
    k_s[...] = k.astype(BF16)
    q = mm_t(transposed(wq_ref[...]), normed) * scale
    q_s[...] = q.astype(BF16)
    v_s[...] = mm_t(transposed(wv_ref[...]), normed).astype(BF16)
    squares = jnp.sum((q * q).reshape(HEADS, head_dim, groups * rows), axis=1)
    peak = jnp.max(jnp.abs(k).reshape(groups * rows // 8, 8, width), axis=0)
    peak = jnp.max(peak, axis=0, keepdims=True)
    mine = iota((HEADS, width), 0) == iota((HEADS, width), 1) // head_dim
    k_bound = jnp.sum(jnp.where(mine, peak * peak, 0.0), axis=1, keepdims=True)
    bound = jnp.max(k_bound * jnp.max(squares, axis=1, keepdims=True))

    pair_of = iota((width, 1), 0) % half // head_dim
    same = (iota((2 * rows, pairs * rows), 0) % 8) == (iota((2 * rows, pairs * rows), 1) % 8)
    blank = jnp.zeros((2 * head_dim, rows), BF16)
    ones, zeros = jnp.ones((16, rows), BF16), jnp.zeros((16, rows), BF16)
    sums = jnp.concatenate([jnp.concatenate([ones, zeros], axis=1), jnp.concatenate([zeros, ones], axis=1)], axis=0)

    def attend(shift, unroll):
        def group(g, _):
            at = pl.ds(pl.multiple_of(g * rows, rows), rows)
            q, k, v = q_s[:, at], k_s[at, :], v_s[:, at]
            qm = jnp.concatenate([jnp.where(pair_of == h, q, 0).astype(BF16) for h in range(pairs)], axis=1)
            s = mm(two_halves(k), qm)
            if shift:
                s = jnp.where(same, s, -1e30)
                tops = [jnp.max(s[i * rows : (i + 1) * rows], axis=0, keepdims=True) for i in range(2)]
                s = jnp.concatenate([s[i * rows : (i + 1) * rows] - tops[i] for i in range(2)], axis=0)
            p = jnp.where(same, jnp.exp2(s), 0.0).astype(BF16)
            parts = [None] * HEADS
            for j in range(pairs // 2):
                low = 2 * j * head_dim
                first = jnp.concatenate([v[low : low + 2 * head_dim], blank], axis=1)
                second = jnp.concatenate([blank, v[half + low : half + low + 2 * head_dim]], axis=1)
                o = mm(jnp.concatenate([first, second, sums], axis=0), p[:, 2 * j * rows : 2 * (j + 1) * rows])
                for i in range(2):
                    d = o[4 * head_dim + 16 * i : 4 * head_dim + 16 * i + 1]
                    for h in range(2):
                        at_row = (2 * i + h) * head_dim
                        lanes = slice(h * rows, (h + 1) * rows)
                        parts[i * pairs + 2 * j + h] = o[at_row : at_row + head_dim, lanes] / d[:, lanes]
            n_s[at, :] = jnp.concatenate(parts, axis=0).T.astype(BF16)
            return 0

        lax.fori_loop(0, groups, group, 0, unroll=unroll)

    safe = bound <= SAFE_SCORE * SAFE_SCORE

    @pl.when(safe)
    def _():
        attend(False, TIME_UNROLL)

    @pl.when(jnp.logical_not(safe))
    def _():
        attend(True, 1)

    y = mm(n_s[...], wo_ref[...])
    for g in range(groups):
        part = slice(g * 8, g * 8 + 8)
        x_s[:, part, :] += y[g * rows : (g + 1) * rows].reshape(frames, 8, width)
    low = 0
    for i, o_ref in enumerate(o_refs):
        step = splits[i % len(splits)]
        o_ref[...] = x_s[low : low + step].astype(BF16)
        low += step


def time_stage(pieces, splits, gain, wq, wk, wv, wo):
    frames_here, tokens, width = pieces[0].shape
    frames = frames_here * len(pieces)
    scale = LOG2E / float(np.sqrt(width // HEADS))
    steps = list(splits) * len(pieces)
    return pl.pallas_call(
        functools.partial(time_kernel, scale, len(pieces), splits),
        out_shape=[jax.ShapeDtypeStruct((step, tokens, width), BF16) for step in steps],
        scratch_shapes=[
            pltpu.VMEM((frames, tokens, width), F32),
            pltpu.VMEM((frames * tokens, width), BF16),
            pltpu.VMEM((width, frames * tokens), BF16),
            pltpu.VMEM((frames * tokens, width), BF16),
            pltpu.VMEM((width, frames * tokens), BF16),
        ],
        compiler_params=pltpu.CompilerParams(vmem_limit_bytes=VMEM_LIMIT),
        cost_estimate=cost(8),
        name="time_attention",
    )(gain, wq, wk, wv, wo, *pieces)


def ordered(weight):
    width = weight.shape[0]
    head_dim = width // HEADS
    quarter = head_dim // 2
    src = iota((width, width), 0)
    dst = iota((width, width), 1)
    within = dst % (width // 2)
    wanted = within // quarter * head_dim + dst // (width // 2) * quarter + within % quarter
    return mm(weight, jnp.where(src == wanted, 1.0, 0.0).astype(BF16)).astype(BF16)


def transposed(weight):
    return weight.astype(F32).T.astype(BF16)


def weights_kernel(wq_ref, wk_ref, wv_ref, q_ref, k_ref, v_ref):
    q_ref[...] = transposed(ordered(wq_ref[...]))
    k_ref[...] = ordered(wk_ref[...])
    v_ref[...] = transposed(wv_ref[...])


def weights_stage(wq, wk, wv):
    return pl.pallas_call(
        weights_kernel,
        out_shape=[jax.ShapeDtypeStruct(wq.shape, BF16)] * 3,
        cost_estimate=cost(1),
        name="space_weights",
    )(wq, wk, wv)


def store_keys(normed, wk, starts, cos_ref, sin_ref, store, peak):
    tokens, width = normed.shape
    half = width // 2
    rows = tokens // len(starts)
    made = mm(normed, wk)
    for i, start in enumerate(starts):
        part = slice(i * rows, (i + 1) * rows)
        at = pl.ds(pl.multiple_of(start, rows), rows)
        c, s = cos_ref[at, :], sin_ref[at, :]
        u, w = made[part, :half], made[part, half:]
        u, w = u * c - w * s, u * s + w * c
        store(part, u.astype(BF16), w.astype(BF16))
        top = jnp.concatenate([u, w], axis=1)
        top = jnp.max(jnp.abs(top).reshape(rows // 8, 8, width), axis=0)
        peak = top if peak is None else jnp.maximum(peak, top)
    return peak


def store_values(normed, wv_t, store):
    made = mm_t(wv_t, normed).astype(BF16)
    for j in range(made.shape[1] // BLOCK):
        store(j, made[:, j * BLOCK : (j + 1) * BLOCK])


def own_kernel(scale, halves, pos, *refs):
    n_refs = refs[:halves]
    wq_ref, wk_ref, wv_ref, cos_ref, sin_ref, cos_t_ref, sin_t_ref, q_ref, k_ref, v_ref, top_ref = refs[halves:]
    tokens, width = n_refs[0].shape[1:]
    half = width // 2
    pieces = pos.shape[0] // halves
    rows = tokens // pieces
    peak, squares = None, None
    for n in range(halves):
        normed = n_refs[n][0]

        def put_value(j, value, low=n * tokens // BLOCK):
            v_ref[0, low + j] = value

        def put_key(part, u, w, low=n * tokens):
            at = slice(low + part.start, low + part.stop)
            k_ref[0, at, :half] = u
            k_ref[0, at, half:] = w

        starts = [pos[n * pieces + i] for i in range(pieces)]
        store_values(normed, wv_ref[...], put_value)
        peak = store_keys(normed, wk_ref[...], starts, cos_ref, sin_ref, put_key, peak)
        made = mm_t(wq_ref[...], normed) * scale
        for i in range(pieces):
            at = pl.ds(pl.multiple_of(starts[i], rows), rows)
            c, s = cos_t_ref[:, at], sin_t_ref[:, at]
            u, w = made[:half, i * rows : (i + 1) * rows], made[half:, i * rows : (i + 1) * rows]
            u, w = u * c - w * s, u * s + w * c
            for j in range(rows // BLOCK):
                part = slice(j * BLOCK, (j + 1) * BLOCK)
                block = (n * tokens + i * rows) // BLOCK + j
                q_ref[0, block, :half, :] = u[:, part].astype(BF16)
                q_ref[0, block, half:, :] = w[:, part].astype(BF16)
                both = u[:, part] * u[:, part] + w[:, part] * w[:, part]
                both = both.reshape(HEADS, half // HEADS, BLOCK)
                top = jnp.sum(both, axis=1)
                squares = top if squares is None else jnp.maximum(squares, top)
    top_ref[0, :8, :] = peak
    top_ref[0, 8:, :half] = squares
    top_ref[0, 8:, half:] = squares


def own_stage(normed, pos, wq, wk, wv, tables):
    part, width = normed[0].shape[1:]
    tokens = part * len(normed)
    scale = LOG2E / float(np.sqrt(width // HEADS))
    shapes = [(1, tokens // BLOCK, width, BLOCK), (1, tokens, width), (1, tokens // BLOCK, width, BLOCK), (1, 16, width)]
    types = [BF16, BF16, BF16, F32]
    args = [*normed, wq, wk, wv, *tables]
    return pl.pallas_call(
        functools.partial(own_kernel, scale, len(normed)),
        in_specs=[pl.BlockSpec(memory_space=pltpu.SMEM)] + [pl.BlockSpec(memory_space=pltpu.VMEM)] * len(args),
        out_shape=[jax.ShapeDtypeStruct(x, t) for x, t in zip(shapes, types)],
        compiler_params=pltpu.CompilerParams(vmem_limit_bytes=VMEM_LIMIT),
        cost_estimate=cost(3),
        name="own_rows",
    )(pos, *args)


def space_kernel(places, halves, frame, has_prev, ids, pos, wk_ref, wv_ref, wo_ref, cos_ref, sin_ref, top_ref, *refs):
    pieces = len(places)
    far_at = pieces + 2 * halves
    x_refs, n_refs = refs[:pieces], refs[pieces:far_at]
    q_ref, ko_ref, vo_ref = refs[far_at : far_at + 3]
    refs = refs[far_at + 3 + (1 if has_prev else 0) :]
    o_ref, x_s, k_s, v_s, o_s, kg0, kg1, vg0, vg1, qm0, qm1, p0, p1, out_sem = refs
    tokens, width = x_s.shape
    blocks = tokens // BLOCK
    piece_rows = tokens // pieces
    half = width // 2
    head_dim = width // HEADS
    quarter = head_dim // 2
    wide = NEIGHBOUR_COUNT * BLOCK

    wk, wv_t = wk_ref[...], wv_ref[...]
    pairs = HEADS // 2
    sums = slice(2 * head_dim, 2 * head_dim + 16)
    for vg in (vg0, vg1):
        for h in range(pairs):
            vg[h, sums, :] = jnp.ones((16, wide), BF16)
    peak = top_ref[0, :8, :]
    for side in range(2):
        near = [n_refs[i][0] for i in range(side * halves, (side + 1) * halves)]
        normed = near[0] if halves == 1 else jnp.concatenate(near, axis=0)

        def put_value(j, value, low=(side + 1) * blocks):
            v_s[low + j] = value

        def put_key(part, u, w, low=(side + 1) * tokens):
            rows = slice(low + part.start, low + part.stop)
            k_s[rows, :half] = u
            k_s[rows, half:] = w

        store_values(normed, wv_t, put_value)
        starts = [pos[i] for i in range(pos.shape[0])]
        peak = store_keys(normed, wk, starts, cos_ref, sin_ref, put_key, peak)
    head_row = iota((HEADS, width), 0)
    head_lane = iota((HEADS, width), 1) % half // quarter
    peak = jnp.max(peak, axis=0, keepdims=True)
    k_bound = jnp.sum(jnp.where(head_row == head_lane, peak * peak, 0.0), axis=1, keepdims=True)
    bound = jnp.max(k_bound * top_ref[0, 8:, :])
    k_s[:tokens, :] = ko_ref[0]
    v_s[:blocks] = vo_ref[0]
    for i in range(pieces):
        x_s[i * piece_rows : (i + 1) * piece_rows, :] = x_refs[i][places[i]]

    head_of = iota((width, 1), 0) % half // quarter

    def entry(block, m):
        return ids[block * (NEIGHBOUR_COUNT + 2) + m]

    def load(block, kg, qm):
        for m in range(NEIGHBOUR_COUNT):
            at = pl.ds(pl.multiple_of(entry(block, m) * BLOCK, BLOCK), BLOCK)
            kg[m * BLOCK : (m + 1) * BLOCK, :] = k_s[at, :]
        q = q_ref[0, entry(block, NEIGHBOUR_COUNT + 1)]
        for h in range(HEADS):
            qm[:, h * BLOCK : (h + 1) * BLOCK] = jnp.where(head_of == h, q, 0).astype(BF16)

    def weights_of(h, kg, qm, p, shift):
        cols = slice(2 * h * BLOCK, 2 * (h + 1) * BLOCK)
        s = mm(kg[...], qm[:, cols])
        if shift:
            s = s - jnp.max(s, axis=0, keepdims=True)
        p[:, cols] = jnp.exp2(s).astype(BF16)

    def values(block, vg, p, between):
        present = jnp.where(entry(block, NEIGHBOUR_COUNT) > 0, 1.0, 0.0).astype(BF16)
        last = slice(wide - BLOCK, wide)
        for m in range(NEIGHBOUR_COUNT):
            value = v_s[entry(block, m)]
            if m == NEIGHBOUR_COUNT - 1:
                value = value * present
            for h in range(pairs):
                vg[h, : 2 * head_dim, m * BLOCK : (m + 1) * BLOCK] = value[2 * h * head_dim : 2 * (h + 1) * head_dim]
        parts = []
        for h in range(pairs):
            vg[h, sums, last] = jnp.ones((16, BLOCK), BF16) * present
            between(h)
            o = mm(vg[h], p[:, 2 * h * BLOCK : 2 * (h + 1) * BLOCK])
            d = o[2 * head_dim : 2 * head_dim + 1]
            parts.append(o[:head_dim, :BLOCK] / d[:, :BLOCK])
            parts.append(o[head_dim : 2 * head_dim, BLOCK:] / d[:, BLOCK:])
        attended = jnp.concatenate(parts, axis=0).T.astype(BF16)
        own = pl.ds(pl.multiple_of(entry(block, NEIGHBOUR_COUNT + 1) * BLOCK, BLOCK), BLOCK)
        o_s[block] = (x_s[own, :].astype(F32) + mm(attended, wo_ref[...])).astype(BF16)
        send(block).start()

    def send(block):
        at = pl.ds(pl.multiple_of(block * BLOCK, BLOCK), BLOCK)
        return pltpu.make_async_copy(o_s.at[block], o_ref.at[frame, at], out_sem.at[block])

    safe = bound <= SAFE_SCORE * SAFE_SCORE

    @pl.when(safe)
    def _():
        slots = [(kg0, qm0, p0, vg0), (kg1, qm1, p1, vg1)]
        for block in range(blocks + 1):

            def between(h, block=block):
                kg, qm, p, _ = slots[block % 2]
                if block < blocks:
                    weights_of(h, kg, qm, p, False)

            if block < blocks:
                load(block, *slots[block % 2][:2])
            if block > 0:
                _, _, p, vg = slots[(block - 1) % 2]
                values(block - 1, vg, p, between)
            else:
                for h in range(pairs):
                    between(h)

    @pl.when(jnp.logical_not(safe))
    def _():
        def step(block, _):
            load(block, kg0, qm0)
            for h in range(pairs):
                weights_of(h, kg0, qm0, p0, True)
            values(block, vg0, p0, lambda h: None)
            return 0

        lax.fori_loop(0, blocks, step, 0)

    for block in range(blocks):
        send(block).wait()


def norm_kernel(places, gain_ref, *refs):
    rows = refs[0].shape[1]
    for i, at in enumerate(places):
        refs[-1][0, i * rows : (i + 1) * rows, :] = rms_rows(refs[i][at].astype(F32), gain_ref[...])


def norm_stage(own, gain):
    rows, width = own[0][0].shape[1:]
    return pl.pallas_call(
        functools.partial(norm_kernel, [at for _, at in own]),
        out_shape=jax.ShapeDtypeStruct((1, rows * len(own), width), BF16),
        compiler_params=pltpu.CompilerParams(vmem_limit_bytes=VMEM_LIMIT),
        cost_estimate=cost(2),
        name="norm_join",
    )(gain, *[p for p, _ in own])


def space_stage(own, normed, made, ids, pos, wk, wv, wo, tables, prev, frame, frames):
    pieces, halves = len(own), len(normed[0])
    piece_rows, width = own[0][0].shape[1:]
    tokens = pieces * piece_rows
    blocks = tokens // BLOCK
    wide = NEIGHBOUR_COUNT * BLOCK
    sum_rows = 2 * (width // HEADS) + 16
    args = [wk, wv, wo, *tables, made[3], *[p for p, _ in own], *normed[0], *normed[1], *made[:3]]
    in_specs = [pl.BlockSpec(memory_space=pltpu.SMEM)] * 2 + [pl.BlockSpec(memory_space=pltpu.VMEM)] * len(args)
    aliases = {}
    if prev is not None:
        aliases = {2 + len(args): 0}
        args.append(prev)
        in_specs.append(pl.BlockSpec(memory_space=pl.ANY))
    return pl.pallas_call(
        functools.partial(space_kernel, [at for _, at in own], halves, frame, prev is not None),
        in_specs=in_specs,
        out_specs=pl.BlockSpec(memory_space=pl.ANY),
        out_shape=jax.ShapeDtypeStruct((frames, tokens, width), BF16),
        scratch_shapes=[
            pltpu.VMEM((tokens, width), BF16),
            pltpu.VMEM((3 * tokens, width), BF16),
            pltpu.VMEM((3 * blocks, width, BLOCK), BF16),
            pltpu.VMEM((blocks, BLOCK, width), BF16),
        ]
        + [pltpu.VMEM((wide, width), BF16)] * 2
        + [pltpu.VMEM((HEADS // 2, sum_rows, wide), BF16)] * 2
        + [pltpu.VMEM((width, HEADS * BLOCK), BF16)] * 2
        + [pltpu.VMEM((wide, HEADS * BLOCK), BF16)] * 2
        + [pltpu.SemaphoreType.DMA((blocks,))],
        input_output_aliases=aliases,
        compiler_params=pltpu.CompilerParams(vmem_limit_bytes=VMEM_LIMIT),
        cost_estimate=cost(14),
        name="space_attention",
    )(ids, pos, *args)


def rotary_tables(tokens, width):
    half = width // HEADS // 2
    freqs = np.power(10000.0, -np.arange(half, dtype=np.float64) / half)
    angle = (np.arange(tokens) % ROT_PERIOD)[:, None] * freqs[None, :]
    by_rows = [np.tile(f(angle).astype(np.float32), (1, HEADS)) for f in (np.cos, np.sin)]
    return [jnp.asarray(t) for t in by_rows] + [jnp.asarray(np.ascontiguousarray(t.T)) for t in by_rows]


def after(value, *earlier):
    return lax.optimization_barrier((value, *earlier))[0]


def body(
    state_tokens,
    gain_time,
    query_time,
    key_time,
    value_time,
    output_time,
    gain_space,
    query_space,
    key_space,
    value_space,
    output_space,
    neighbours,
):
    frames_here, tokens_here, width = state_tokens.shape
    frame_count = lax.axis_size("frame")
    tile_count = lax.axis_size("tile")
    me = lax.axis_index("frame")
    tile = lax.axis_index("tile")
    rows = tokens_here // frame_count
    parts = 2 if rows % (2 * BLOCK) == 0 else 1
    part_rows = rows // parts

    def swap(value, k):
        return value if k == 0 else lax.ppermute(value, "frame", [(i, i ^ k) for i in range(frame_count)])

    last_cut = [1] * frames_here if frames_here < 3 else [1, 1, frames_here - 2]
    wq, wk, wv = weights_stage(query_space, key_space, value_space)

    def give_back(one, c, earlier):
        cut, outs, back = one
        for k in range(frame_count):
            out = outs[k * len(cut) + c]
            back[k][c] = swap(after(out, *earlier) if k and earlier else out, k)

    held = []
    pieces = []
    for part in range(parts):
        source = after(state_tokens, pieces[1]) if part else state_tokens
        pieces = []
        for k in range(frame_count):
            low = (me ^ k) * rows + part * part_rows
            pieces.append(swap(lax.dynamic_slice_in_dim(source, low, part_rows, axis=1), k))
        if part == 0:
            pieces[0] = after(pieces[0], wq, wk, wv)
        cut = last_cut if part == parts - 1 else [frames_here]
        outs = time_stage(
            pieces, cut, gain_time.reshape(1, width), query_time, key_time, value_time, output_time
        )
        held.append((cut, outs, [[None] * len(cut) for _ in range(frame_count)]))
        if part < parts - 1:
            give_back(held[-1], 0, ())

    def frame_pieces(frame):
        own = []
        for k in range(frame_count):
            for cut, _, back in held:
                low = 0
                for c, step in enumerate(cut):
                    if low <= frame < low + step:
                        own.append((back[k][c], frame - low))
                    low += step
        return own

    pairs = [(i, i ^ 1) for i in range(tile_count)]
    onward = [(i, (i + 2) % tile_count if i % 2 == 0 else (i - 2) % tile_count) for i in range(tile_count)]
    split = part_rows % BLOCK == 0
    places = me ^ jnp.arange(frame_count, dtype=jnp.int32)
    if split:
        pos = (places[:, None] * rows + jnp.arange(parts, dtype=jnp.int32) * part_rows).reshape(-1)
    else:
        pos = jnp.zeros((1,), jnp.int32)
    tables = rotary_tables(tokens_here, width)
    gain = gain_space.reshape(1, width)
    owns, nears, mades = [], [], []
    sent, normed = -1, ()
    for frame in range(frames_here):
        low = 0
        for c, step in enumerate(last_cut):
            if low <= frame < low + step and c > sent:
                give_back(held[-1], c, normed)
                sent = c
            low += step
        own = frame_pieces(frame)
        if not split:
            stacked = jnp.stack([p[at] for p, at in own])[places]
            own = [(stacked.reshape(1, tokens_here, width), 0)]
        own_normed = [norm_stage(own, gain)]
        if frame == 0:
            normed = own_normed
        owns.append(own)
        earlier = nears[-1] if frame > 1 else ()
        nears.append([lax.ppermute(after(n, *earlier) if earlier else n, "tile", pairs) for n in own_normed])
        mades.append(own_stage(own_normed, pos, wq, wk, wv, tables))

    blocks = tokens_here // BLOCK
    total = blocks * tile_count
    even = tile % 2 == 0
    offset = (neighbours - (tile - 1) * blocks) % total
    side_of = offset // blocks
    side_at = jnp.where(side_of == 1, 0, jnp.where((side_of == 2) == even, 1, 2))
    inner = offset % blocks
    own_inner = jnp.arange(blocks, dtype=jnp.int32)
    if split:
        per = rows // BLOCK
        inner = ((inner // per) ^ me) * per + inner % per
        own_inner = ((own_inner // per) ^ me) * per + own_inner % per
    present = neighbours >= 0
    ids = jnp.where(present, side_at * blocks + inner, own_inner[:, None])
    ids = jnp.concatenate(
        [ids, present[:, -1:].astype(jnp.int32), own_inner[:, None]], axis=1
    ).reshape(-1)
    result = None
    far = [lax.ppermute(n, "tile", onward) for n in nears[0]]
    for frame in range(frames_here):
        later = None
        near = nears[frame]
        if frame + 1 < frames_here:
            if result is None:
                near, nears[frame + 1] = lax.optimization_barrier((near, nears[frame + 1]))
            else:
                near, nears[frame + 1], result = lax.optimization_barrier((near, nears[frame + 1], result))
            later = [lax.ppermute(n, "tile", onward) for n in nears[frame + 1]]
        result = space_stage(
            owns[frame], (near, far), mades[frame], ids, pos, wk, wv, output_space,
            tables[:2], result, frame, frames_here,
        )
        far = later
    return result


def solution(mesh):
    rows = P("frame", "tile", None)
    return jax.shard_map(
        body,
        mesh=mesh,
        in_specs=(rows,) + (P(),) * 10 + (P("tile", None),),
        out_specs=rows,
        check_vma=False,
    )
```
